256 devices in a mesh: grid: 64 (over x_hi, y, z), vis: 4 (over x_lo, core).
Axes of the slice: x: 4 (x_hi: 2, x_lo: 2; x = x_hi * 2 + x_lo), y: 4, z: 8, core: 2. Of those that a mesh axis runs over, the one named last changes fastest.
Arguments:
- vis_coords: float32 [64, 256, 2, 512], P('grid', 'vis'), may hold values from 0 to 64
- vis_values: float32 [64, 256, 2, 512], P('grid', 'vis'), may hold values from -6 to 6
- tile_index: int32 [64, 256], P('grid', 'vis'), may hold values from 0 to 63
Outputs:
- facets: float32 [64, 2, 1024, 1024], P('grid', None, 'vis')
The draws below stay inside these ranges and needn't reach their ends.
Inputs may be any that keep to these rules, and one draw needn't show every extreme that they name: `tile_index`: tile a * 8 + e covers subgrid rows from a * 64 and columns from e * 64.
All inputs are finite; a program needn't handle non-finite values.
Results may differ from the reference program's by a relative error of at most 0.014.
Values may be sent and summed in bfloat16 or wider, within the bound.
No kernel may reach another device: no remote copies, remote signals or barrier semaphores. Data moves between devices by JAX's collectives and lax.ppermute only.
A program may use at most 64 MiB of HBM per device.

```python
import math
import jax
import jax.numpy as jnp
from jax import lax

SUB = 512
FAC = 1024
CONTRIB = 64
TILE = 64
BLK = 512
BLK_DEV = 64
NBLK = 8
VBLOCKS = 256
SUBGRIDS = 64
N_GRID = 64
N_VIS = 4


def touch_ends(entries, stream_key, least, high):
    shape = entries.shape
    index_at = [jax.random.randint(jax.random.fold_in(stream_key, axis), (), 0, shape[axis]) for axis in range(len(shape))]
    entries = entries.at[tuple(index_at)].set(least)
    longest = shape.index(max(shape))
    index_at[longest] = (index_at[longest] + 1) % shape[longest]
    return entries.at[tuple(index_at)].set(high)


def block_scale(stream_key, shape, split, smallest, largest):
    loudness, own = 1.0, jax.random.fold_in(stream_key, 6)
    for position, shards_of in split:
        heights = jnp.exp(jax.random.uniform(jax.random.fold_in(own, position), (shards_of,), jnp.float32, smallest / len(split), largest / len(split)))
        loudness = loudness * jnp.repeat(heights, shape[position] // shards_of).reshape([-1 if axis == position else 1 for axis in range(len(shape))])
    return loudness


def noise(key, dims, width, reach, pieces=(), kind=jnp.bfloat16):
    result = jax.random.normal(key, dims, jnp.float32) * width
    if len(pieces) > 0:
        result = block_scale(key, dims, pieces, -0.22, 0.18) * result
    return jnp.clip(result, min=-reach, max=reach).astype(kind)


def setup_inputs(seed: int = 0) -> dict:
    seeds = jax.random.split(jax.random.key(seed), 4)
    vis_coords = jnp.clip(64.0 * jax.random.uniform(seeds[0], (SUBGRIDS, VBLOCKS, 2, BLK), jnp.float32) ** block_scale(seeds[0], (SUBGRIDS, VBLOCKS, 2, BLK), ((0, 64), (1, 4)), -0.2, 0.2), 0.0, 64.0)
    vis_values = noise(seeds[1], (SUBGRIDS, VBLOCKS, 2, BLK), 1.0, 6.0, ((0, 64), (1, 4)), jnp.float32)
    tile_index = touch_ends(jax.random.randint(seeds[2], (SUBGRIDS, VBLOCKS), 0, (SUB // TILE) * (SUB // TILE)), jax.random.fold_in(seeds[2], 1), 0, ((SUB // TILE) * (SUB // TILE)) - 1).astype(jnp.int32)
    return dict(vis_coords=vis_coords, vis_values=vis_values, tile_index=tile_index)


taper_scale = 16.0

def phase_pair(frequencies, points, length):
    phases = frequencies[:, None] * points[None, :] % length
    angles = phases.astype(jnp.float32) * (2.0 * math.pi / length)
    return (jnp.cos(angles), jnp.sin(angles))

def kernel_rows(places):
    pixels = jnp.arange(TILE, dtype=jnp.float32)
    distance = pixels - places[..., None]
    scaled = distance / taper_scale
    return jnp.sinc(distance) * jnp.exp(-scaled * scaled)

def exact_dot(first, second):
    return jnp.dot(first.astype(jnp.float32), second.astype(jnp.float32), precision=lax.Precision.HIGHEST, preferred_element_type=jnp.float32)

def grid_blocks(coords, values, tile_ids):
    across = SUB // TILE
    weights_u = kernel_rows(coords[:, 0])
    weights_v = kernel_rows(coords[:, 1])
    weighted = weights_u[:, None] * values[:, :, :, None]
    patches = jnp.einsum('bcnx,bny->bcxy', weighted, weights_v, precision=lax.Precision.HIGHEST, preferred_element_type=jnp.float32)
    onehot = (tile_ids[None, :] == jnp.arange(across * across, dtype=jnp.int32)[:, None]).astype(jnp.float32)
    placed = jnp.dot(onehot, patches.reshape(coords.shape[0], 2 * TILE * TILE), precision=lax.Precision.HIGHEST, preferred_element_type=jnp.float32)
    return placed.reshape(across, across, 2, TILE, TILE).transpose(0, 3, 2, 1, 4).reshape(SUB, 2, SUB)

def complex_block(part_real, part_imag):
    return jnp.concatenate([jnp.concatenate([part_real, part_imag], 1), jnp.concatenate([-part_imag, part_real], 1)], 0)

def reference(vis_coords, vis_values, tile_index):
    groups = N_GRID // NBLK
    column_count = groups * CONTRIB
    unitary = 1.0 / math.sqrt(SUB)
    spectrum = jnp.arange(SUB, dtype=jnp.int32)
    tab_real, tab_imag = phase_pair(spectrum, jnp.arange(column_count, dtype=jnp.int32), SUB)
    col_table = jnp.concatenate([jnp.concatenate([tab_real, -tab_imag], 1), jnp.concatenate([tab_imag, tab_real], 1)], 0).astype(jnp.bfloat16)
    rows_real, rows_imag = phase_pair(spectrum, spectrum, SUB)
    left_side = jnp.concatenate([rows_real, -rows_imag], 1).astype(jnp.bfloat16)

    def one_subgrid(inputs):
        coords, values, tile_ids = inputs
        running = jnp.zeros((SUB, 2, SUB), jnp.float32)
        for member in range(N_VIS):
            first = member * BLK_DEV
            placed = grid_blocks(coords[first:first + BLK_DEV], values[first:first + BLK_DEV], tile_ids[first:first + BLK_DEV])
            running = running + lax.optimization_barrier(placed.astype(jnp.bfloat16)).astype(jnp.float32)
        summed = running.astype(jnp.bfloat16)
        images = (exact_dot(summed.reshape(SUB, 2 * SUB), col_table) * unitary).astype(jnp.bfloat16).reshape(SUB, 2, column_count)
        stacked = complex_block(images[:, 0], images[:, 1])
        spectra = (exact_dot(left_side, stacked) * unitary).astype(jnp.bfloat16)
        return spectra.reshape(NBLK, CONTRIB, 2, groups, CONTRIB).transpose(3, 0, 2, 1, 4).reshape(N_GRID, 2, CONTRIB, CONTRIB)
    contribs = lax.map(one_subgrid, (vis_coords, vis_values, tile_index))
    embed_real, embed_imag = phase_pair(jnp.arange(FAC, dtype=jnp.int32), spectrum, FAC)
    embed_left = jnp.concatenate([embed_real, embed_imag], 1).astype(jnp.bfloat16)
    out_real, out_imag = phase_pair(jnp.arange(column_count, dtype=jnp.int32), jnp.arange(FAC, dtype=jnp.int32), FAC)
    real_right = jnp.concatenate([out_real, -out_imag], 0).astype(jnp.bfloat16)
    imag_right = jnp.concatenate([out_imag, out_real], 0).astype(jnp.bfloat16)
    sines = jnp.sin(math.pi * (jnp.arange(FAC, dtype=jnp.float32) + 0.5) / FAC)
    taper_rows = 0.25 + 0.75 * sines * sines
    weight = taper_rows[:, None] * taper_rows[None, :] * (1.0 / math.sqrt(CONTRIB * groups))

    def one_facet(facet_id):
        received = lax.dynamic_index_in_dim(contribs, facet_id, 1, keepdims=False)
        blocks = received.reshape(groups, NBLK, 2, CONTRIB, CONTRIB).transpose(1, 3, 2, 0, 4)
        part_real = blocks[:, :, 0].reshape(SUB, column_count)
        part_imag = blocks[:, :, 1].reshape(SUB, column_count)
        mixture = (exact_dot(embed_left, complex_block(part_real, part_imag)) * unitary).astype(jnp.bfloat16)
        return jnp.stack([exact_dot(mixture, real_right) * weight, exact_dot(mixture, imag_right) * weight])
    return lax.map(one_facet, jnp.arange(N_GRID, dtype=jnp.int32))
```

```python
import functools
import math

import jax
import jax.numpy as jnp
import ml_dtypes
import numpy as np
from jax import lax
from jax.experimental import pallas as pl
from jax.experimental.pallas import tpu as pltpu
from jax.sharding import PartitionSpec as P

SUB = 512
FAC = 1024
CONTRIB = 64
TILE = 64
BLK = 512
BLOCKS = 64
NBLK = 8
LANES = 128
QUARTER = 16
ROWS = NBLK * QUARTER
ROWS_OUT = FAC // 4
WIDTH = 2 * SUB
UNITARY = 1.0 / math.sqrt(SUB)
BF16 = jnp.bfloat16
F32 = jnp.float32


def angles(first, second, length):
    return (first[:, None] * second[None, :] % length) * (2.0 * math.pi / length)


def as_bf16(table):
    return np.ascontiguousarray(table.astype(np.float32)).astype(ml_dtypes.bfloat16)


@functools.lru_cache(maxsize=None)
def tables():
    spectrum = np.arange(SUB)
    turn = angles(spectrum, spectrum, SUB).reshape(NBLK, TILE, NBLK, CONTRIB)
    cos, sin = np.cos(turn), np.sin(turn)
    columns = np.empty((NBLK, 2, TILE, NBLK, 2, CONTRIB))
    columns[:, 0, :, :, 0] = cos
    columns[:, 1, :, :, 0] = sin
    columns[:, 0, :, :, 1] = -sin
    columns[:, 1, :, :, 1] = cos
    columns = as_bf16(columns.reshape(WIDTH, WIDTH))
    turn = angles(spectrum, spectrum, SUB)
    rows = np.concatenate([np.cos(turn), np.sin(turn)], 1)
    rows = rows.reshape(NBLK, 2, 2, QUARTER, WIDTH).transpose(2, 1, 0, 3, 4)
    rows = as_bf16(rows.reshape(SUB, WIDTH))
    turn = angles(np.arange(FAC), spectrum, FAC).reshape(4, ROWS_OUT, NBLK, 4, QUARTER)
    parts = np.stack([np.cos(turn), np.sin(turn)], 2)
    left = np.empty((4, ROWS_OUT, 4, 2, NBLK, QUARTER))
    for g in range(4):
        for j in range(4):
            left[g, :, j] = parts[g, :, :, :, g ^ j]
    left = as_bf16(left.reshape(4, ROWS_OUT, WIDTH))
    turn = angles(spectrum, np.arange(FAC), FAC).reshape(NBLK, CONTRIB, FAC)
    cos, sin = np.cos(turn), np.sin(turn)
    right = np.empty((NBLK, 2, CONTRIB, 2, FAC))
    right[:, 0, :, 0] = cos
    right[:, 1, :, 0] = -sin
    right[:, 0, :, 1] = sin
    right[:, 1, :, 1] = cos
    right = right.reshape(WIDTH, 4, FAC // 2).transpose(1, 0, 2)
    right = as_bf16(right)
    sines = np.sin(math.pi * (np.arange(FAC) + 0.5) / FAC)
    taper = 0.25 + 0.75 * sines * sines
    taper_rows = np.broadcast_to(taper.reshape(4, ROWS_OUT, 1), (4, ROWS_OUT, LANES)).astype(np.float32)
    taper_cols = (taper / math.sqrt(SUB)).reshape(2, 1, FAC // 2).astype(np.float32)
    pixel = np.arange(TILE)
    bell = (1.0 - 2.0 * (pixel % 2)) * np.exp(-(pixel * pixel) / 256.0)
    bell = (bell[:, None] * np.concatenate([bell, bell])[None, :]).astype(np.float32)
    return columns, rows, left, right, np.ascontiguousarray(taper_rows), taper_cols, bell


SINE = [math.pi ** (2 * k + 1) * (-1) ** k / math.factorial(2 * k + 1) for k in range(7)]


def gridding_kernel(
    tile_ref, place_ref, coords_hbm, values_hbm, columns_hbm, rows_hbm, bell_ref,
    send_ref, send_x_ref, keep_ref, keep_x_ref,
    coords, values, whole, offset, step8, slope, height, u_buf, v_buf, acc, grid16, stacked, columns, rows, sems,
):
    in_coords = pltpu.make_async_copy(coords_hbm, coords, sems.at[0])
    in_values = pltpu.make_async_copy(values_hbm, values, sems.at[1])
    in_columns = pltpu.make_async_copy(columns_hbm, columns, sems.at[2])
    in_rows = pltpu.make_async_copy(rows_hbm, rows, sems.at[3])
    in_coords.start()
    in_values.start()
    in_columns.start()
    in_rows.start()
    acc[...] = jnp.zeros_like(acc)
    u_buf[...] = jnp.zeros_like(u_buf)
    v_buf[...] = jnp.zeros_like(v_buf)
    in_coords.wait()
    in_values.wait()

    @pl.loop(0, BLOCKS * 8 // 64)
    def _(chunk):
        at = pl.ds(pl.multiple_of(chunk * 64, 64), 64)
        c = coords[at, :]
        r = jnp.round(c)
        f = c - r
        f = jnp.where(jnp.abs(f) < 1e-20, 1e-20, f)
        square = f * f
        sine = jnp.full_like(f, SINE[6])
        for k in range(5, -1, -1):
            sine = sine * square + SINE[k]
        half = r * 0.5
        odd = half - jnp.floor(half)
        sine = sine * f * ((1.0 - 4.0 * odd) * (1.0 / math.pi))
        whole[at, :] = r
        offset[at, :] = f
        step8[at, :] = jnp.exp(c * (1.0 / 16.0))
        slope[at, :] = c * (1.0 / 128.0)
        height[at, :] = sine * jnp.exp(c * c * (-1.0 / 256.0))

    row_of = lax.broadcasted_iota(jnp.int32, (8, LANES), 0).astype(F32)

    def spread(ref, row):
        return jnp.broadcast_to(ref[pl.ds(row, 1), :], (8, LANES))

    def generate(b, slot):
        for t in range(4):
            lanes = slice(t * LANES, (t + 1) * LANES)
            for axis in range(2):
                row = b * 8 + t * 2 + axis
                base = row_of - spread(whole, row)
                f = spread(offset, row)
                ratio = spread(step8, row)
                w = spread(height, row) * jnp.exp(row_of * spread(slope, row))
                if axis == 0:
                    found = []
                    for a in range(8):
                        inverse = pl.reciprocal((base + 8.0 * a) - f, approx=True)
                        found.append(w * inverse)
                        w = w * ratio
                    u_buf[slot, :, lanes] = jnp.concatenate(found, 0).astype(BF16)
                else:
                    w_real = w * spread(values, b * 8 + t * 2)
                    w_imag = w * spread(values, b * 8 + t * 2 + 1)
                    real, imag = [], []
                    for a in range(8):
                        inverse = pl.reciprocal((base + 8.0 * a) - f, approx=True)
                        real.append(w_real * inverse)
                        imag.append(w_imag * inverse)
                        w_real = w_real * ratio
                        w_imag = w_imag * ratio
                    v_buf[slot, :TILE, lanes] = jnp.concatenate(real, 0).astype(BF16)
                    v_buf[slot, TILE:, lanes] = jnp.concatenate(imag, 0).astype(BF16)

    def deposit(b, slot):
        patch = lax.dot_general(
            u_buf[slot], v_buf[slot], (((1,), (1,)), ((), ())), preferred_element_type=F32
        )
        tile = tile_ref[b]
        at = (
            pl.ds(pl.multiple_of((tile // NBLK) * TILE, TILE), TILE),
            pl.ds(pl.multiple_of((tile % NBLK) * LANES, LANES), LANES),
        )
        acc[at] = acc[at] + patch

    @pl.loop(0, BLOCKS // 2)
    def _(pair):
        deposit(jnp.maximum(pair * 2 - 1, 0), 1)
        generate(pair * 2, 0)
        deposit(pair * 2, 0)
        generate(pair * 2 + 1, 1)

    deposit(BLOCKS - 1, 1)

    bell = bell_ref[...]

    @pl.loop(0, NBLK)
    def _(a):
        at = pl.ds(pl.multiple_of(a * TILE, TILE), TILE)
        for e in range(NBLK):
            lanes = slice(e * LANES, (e + 1) * LANES)
            grid16[at, lanes] = (acc[at, lanes] * bell).astype(BF16)

    in_columns.wait()
    in_rows.wait()
    sign = jnp.where(lax.broadcasted_iota(jnp.int32, (1, LANES), 1) < CONTRIB, 1.0, -1.0)

    @pl.loop(0, WIDTH // 256)
    def _(n):
        at = pl.ds(pl.multiple_of(n * 256, 256), 256)
        images = jnp.dot(grid16[...], columns[:, at], preferred_element_type=F32) * UNITARY
        stacked[:SUB, at] = images.astype(BF16)
        turned = jnp.concatenate(
            [pltpu.roll(images[:, :LANES], CONTRIB, 1) * sign, pltpu.roll(images[:, LANES:], CONTRIB, 1) * sign], 1
        )
        stacked[SUB:, at] = turned.astype(BF16)

    core = place_ref[0] % 2
    side = place_ref[0] // 2
    for half, outs in ((1 - core, (send_ref, send_x_ref)), (core, (keep_ref, keep_x_ref))):
        left = rows[pl.ds(pl.multiple_of(half * 2 * ROWS, 2 * ROWS), 2 * ROWS), :]

        @pl.loop(0, WIDTH // 256)
        def _(n):
            at = pl.ds(pl.multiple_of(n * 256, 256), 256)
            spectra = jnp.dot(left, stacked[:, at], preferred_element_type=F32) * UNITARY
            spectra = spectra.astype(BF16)
            for i in range(2):
                lanes = slice(i * LANES, (i + 1) * LANES)

                @pl.when(side == 0)
                def _():
                    outs[0][n * 2 + i] = spectra[:ROWS, lanes]
                    outs[1][n * 2 + i] = spectra[ROWS:, lanes]

                @pl.when(side == 1)
                def _():
                    outs[1][n * 2 + i] = spectra[:ROWS, lanes]
                    outs[0][n * 2 + i] = spectra[ROWS:, lanes]


def gridding(tile_ids, place, coords, values, columns, rows, bell):
    any_space = pl.BlockSpec(memory_space=pl.ANY)
    scalar = pl.BlockSpec(memory_space=pltpu.SMEM)
    vector = pl.BlockSpec(memory_space=pltpu.VMEM)
    quarter = jax.ShapeDtypeStruct((NBLK, ROWS, LANES), BF16)
    plane = pltpu.VMEM((BLOCKS * 8, LANES), F32)
    return pl.pallas_call(
        gridding_kernel,
        out_shape=[quarter] * 4,
        in_specs=[scalar, scalar, any_space, any_space, any_space, any_space, vector],
        out_specs=[vector] * 4,
        scratch_shapes=[
            plane, plane, plane, plane, plane, plane, plane,
            pltpu.VMEM((2, TILE, BLK), BF16),
            pltpu.VMEM((2, 2 * TILE, BLK), BF16),
            pltpu.VMEM((SUB, WIDTH), F32),
            pltpu.VMEM((SUB, WIDTH), BF16),
            pltpu.VMEM((WIDTH, WIDTH), BF16),
            pltpu.VMEM((WIDTH, WIDTH), BF16),
            pltpu.VMEM((SUB, WIDTH), BF16),
            pltpu.SemaphoreType.DMA((4,)),
        ],
        compiler_params=pltpu.CompilerParams(vmem_limit_bytes=63 * 1024 * 1024),
        name="gridding",
    )(tile_ids, place, coords, values, columns, rows, bell)


def facet_kernel(place_ref, own, by_core, by_x, by_both, left, right, taper_rows, taper_cols, out_ref, stacked, mixture):
    @pl.when(pl.program_id(0) == 0)
    def _():
        sign = jnp.where(lax.broadcasted_iota(jnp.int32, (1, LANES), 1) < CONTRIB, -1.0, 1.0)
        for j, part in enumerate((own, by_core, by_x, by_both)):
            for sb in range(NBLK):
                lanes = slice(sb * LANES, (sb + 1) * LANES)
                block = part[sb]
                stacked[2 * j * ROWS : (2 * j + 1) * ROWS, lanes] = block
                turned = pltpu.roll(block.astype(F32), CONTRIB, 1) * sign
                stacked[(2 * j + 1) * ROWS : (2 * j + 2) * ROWS, lanes] = turned.astype(BF16)

        @pl.loop(0, WIDTH // 256)
        def _(n):
            at = pl.ds(pl.multiple_of(n * 256, 256), 256)
            mixed = jnp.dot(left[0], stacked[:, at], preferred_element_type=F32) * UNITARY
            mixture[:, at] = mixed.astype(BF16)

    image = jnp.dot(mixture[...], right[0], preferred_element_type=F32)
    weight = taper_rows[0]
    for i in range(FAC // 2 // LANES):
        lanes = slice(i * LANES, (i + 1) * LANES)
        out_ref[0, :, lanes] = image[:, lanes] * (weight * taper_cols[0, :, lanes])


def facet(place, quarters, left, right, taper_rows, taper_cols):
    quarter = pl.BlockSpec((NBLK, ROWS, LANES), lambda n, place: (0, 0, 0))
    return pl.pallas_call(
        facet_kernel,
        out_shape=jax.ShapeDtypeStruct((2, ROWS_OUT, FAC), F32),
        grid_spec=pltpu.PrefetchScalarGridSpec(
            num_scalar_prefetch=1,
            grid=(4,),
            in_specs=[
                quarter, quarter, quarter, quarter,
                pl.BlockSpec((1, ROWS_OUT, WIDTH), lambda n, place: (place[0], 0, 0)),
                pl.BlockSpec((1, WIDTH, FAC // 2), lambda n, place: (n, 0, 0)),
                pl.BlockSpec((1, ROWS_OUT, LANES), lambda n, place: (place[0], 0, 0)),
                pl.BlockSpec((1, 1, FAC // 2), lambda n, place: (n % 2, 0, 0)),
            ],
            out_specs=pl.BlockSpec((1, ROWS_OUT, FAC // 2), lambda n, place: (n // 2, 0, n % 2)),
            scratch_shapes=[
                pltpu.VMEM((WIDTH, WIDTH), BF16),
                pltpu.VMEM((ROWS_OUT, WIDTH), BF16),
            ],
        ),
        compiler_params=pltpu.CompilerParams(vmem_limit_bytes=63 * 1024 * 1024),
        name="facet",
    )(place, *quarters, left, right, taper_rows, taper_cols)


def by_visibility_row(array):
    return array.reshape(BLOCKS, 2, BLK // LANES, LANES).transpose(0, 2, 1, 3).reshape(BLOCKS * 8, LANES)


def shards(vis_coords, vis_values, tile_index):
    columns, rows, left, right, taper_rows, taper_cols, bell = (jnp.asarray(table) for table in tables())
    place = lax.axis_index("vis").astype(jnp.int32).reshape(1)

    def swap(array, bit):
        return lax.ppermute(array, "vis", [(i, i ^ bit) for i in range(4)])

    send, send_x, keep, keep_x = gridding(
        tile_index[0], place, by_visibility_row(vis_coords), by_visibility_row(vis_values), columns, rows, bell
    )
    got_x = swap(send_x, 1)
    got = swap(send, 1)
    give = (keep_x.astype(F32) + got_x.astype(F32)).astype(BF16)
    arrived = swap(give, 2)
    total = (keep.astype(F32) + got.astype(F32) + arrived.astype(F32)).astype(BF16)
    outgoing = total.reshape(NBLK * NBLK, QUARTER, LANES)
    own = lax.all_to_all(outgoing, "grid", split_axis=0, concat_axis=0, tiled=True)
    own = own.reshape(NBLK, ROWS, LANES)
    by_x = swap(own, 2)
    by_core = swap(own, 1)
    by_both = swap(by_x, 1)
    return facet(place, (own, by_core, by_x, by_both), left, right, taper_rows, taper_cols)[None]


def solution(mesh):
    placed = (P("grid", "vis", None, None), P("grid", "vis", None, None), P("grid", "vis"))
    return jax.shard_map(
        shards, mesh=mesh, in_specs=placed, out_specs=P("grid", None, "vis", None), check_vma=False
    )
```

```python
import functools
import math

import jax
import jax.numpy as jnp
import ml_dtypes
import numpy as np
from jax import lax
from jax.experimental import pallas as pl
from jax.experimental.pallas import tpu as pltpu
from jax.sharding import PartitionSpec as P

SUB = 512
FAC = 1024
CONTRIB = 64
TILE = 64
BLK = 512
BLOCKS = 64
GROUP = 8
NBLK = 8
LANES = 128
QUARTER = 16
ROWS = NBLK * QUARTER
ROWS_OUT = FAC // 4
WIDTH = 2 * SUB
UNITARY = 1.0 / math.sqrt(SUB)
BF16 = jnp.bfloat16
F32 = jnp.float32


def angles(first, second, length):
    return (first[:, None] * second[None, :] % length) * (2.0 * math.pi / length)


def as_bf16(table):
    return np.ascontiguousarray(table.astype(np.float32)).astype(ml_dtypes.bfloat16)


@functools.lru_cache(maxsize=None)
def tables():
    spectrum = np.arange(SUB)
    turn = angles(spectrum, spectrum, SUB).reshape(NBLK, TILE, NBLK, CONTRIB)
    cos, sin = np.cos(turn), np.sin(turn)
    columns = np.empty((NBLK, 2, TILE, NBLK, 2, CONTRIB))
    columns[:, 0, :, :, 0] = cos
    columns[:, 1, :, :, 0] = sin
    columns[:, 0, :, :, 1] = -sin
    columns[:, 1, :, :, 1] = cos
    columns = as_bf16(columns.reshape(WIDTH, WIDTH))
    turn = angles(spectrum, spectrum, SUB)
    rows = np.concatenate([np.cos(turn), np.sin(turn)], 1)
    rows = rows.reshape(NBLK, 4, QUARTER, WIDTH).transpose(1, 0, 2, 3)
    rows = as_bf16(rows.reshape(SUB, WIDTH))
    turn = angles(np.arange(FAC), spectrum, FAC).reshape(4, ROWS_OUT, NBLK, 4, QUARTER)
    left = np.empty((4, 2, ROWS_OUT, 4, NBLK, QUARTER))
    for g in range(4):
        for j in range(4):
            left[g, 0, :, j] = np.cos(turn[g, :, :, g ^ j])
            left[g, 1, :, j] = np.sin(turn[g, :, :, g ^ j])
    left = as_bf16(left.reshape(4, 2 * ROWS_OUT, SUB))
    turn = angles(spectrum, np.arange(FAC), FAC).reshape(NBLK, CONTRIB, FAC)
    cos, sin = np.cos(turn), np.sin(turn)
    right = np.empty((NBLK, 2, CONTRIB, 2, FAC))
    right[:, 0, :, 0] = cos
    right[:, 1, :, 0] = -sin
    right[:, 0, :, 1] = sin
    right[:, 1, :, 1] = cos
    right = right.reshape(WIDTH, CHUNKS, 2 * FAC // CHUNKS).transpose(1, 0, 2)
    right = as_bf16(right)
    sines = np.sin(math.pi * (np.arange(FAC) + 0.5) / FAC)
    taper = 0.25 + 0.75 * sines * sines
    taper_rows = np.broadcast_to(taper.reshape(4, ROWS_OUT, 1), (4, ROWS_OUT, LANES)).astype(np.float32)
    taper_cols = (taper / math.sqrt(SUB)).reshape(1, FAC).astype(np.float32)
    pixel = np.arange(TILE)
    bell = (1.0 - 2.0 * (pixel % 2)) * np.exp(-(pixel * pixel) / 256.0)
    bell = (bell[:, None] * np.concatenate([bell, bell])[None, :]).astype(np.float32)
    return columns, rows, left, right, np.ascontiguousarray(taper_rows), taper_cols, bell


SINE = [math.pi ** (2 * k + 1) * (-1) ** k / math.factorial(2 * k + 1) for k in range(7)]


def gridding_kernel(
    place_ref, tiles_hbm, coords_hbm, values_hbm, columns_hbm, rows_hbm, bell_hbm, left_hbm, taper_rows_hbm, taper_cols_hbm,
    keep_ref, send_ref, keep_x_ref, send_x_ref, left_ref, taper_rows_ref, taper_cols_ref,
    tile_ref, coords, values, whole, offset, step8, slope, height, u_buf, v_buf, acc, grid16, stacked, columns, rows, bell_ref,
    sems,
):
    place = place_ref[0]
    first = [(coords_hbm, coords), (values_hbm, values), (tiles_hbm, tile_ref)]
    later = [(columns_hbm, columns), (bell_hbm, bell_ref)]
    for i in range(4):
        quarter = pl.ds(pl.multiple_of((place ^ i) * ROWS, ROWS), ROWS)
        later.append((rows_hbm.at[quarter], rows.at[i * ROWS : (i + 1) * ROWS]))
    last = [(left_hbm.at[place], left_ref), (taper_rows_hbm.at[place], taper_rows_ref), (taper_cols_hbm, taper_cols_ref)]
    copies = [pltpu.make_async_copy(*ends, sems.at[i]) for i, ends in enumerate(first + later + last)]
    for copy in copies:
        copy.start()
    acc[...] = jnp.zeros_like(acc)
    for copy in copies[: len(first)]:
        copy.wait()

    @pl.loop(0, BLOCKS * 8 // 64)
    def _(chunk):
        at = pl.ds(pl.multiple_of(chunk * 64, 64), 64)
        c = coords[at, :]
        r = jnp.round(c)
        f = c - r
        f = jnp.where(jnp.abs(f) < 1e-20, 1e-20, f)
        square = f * f
        sine = jnp.full_like(f, SINE[6])
        for k in range(5, -1, -1):
            sine = sine * square + SINE[k]
        half = r * 0.5
        odd = half - jnp.floor(half)
        sine = sine * f * ((1.0 - 4.0 * odd) * (1.0 / math.pi))
        whole[at, :] = r
        offset[at, :] = f
        step8[at, :] = jnp.exp(c * (1.0 / 16.0))
        slope[at, :] = c * (1.0 / 128.0)
        height[at, :] = sine * jnp.exp(c * c * (-1.0 / 256.0))

    row_of = lax.broadcasted_iota(jnp.int32, (8, LANES), 0).astype(F32)

    def spread(ref, row):
        return jnp.broadcast_to(ref[pl.ds(row, 1), :], (8, LANES))

    def generate(b, slot):
        for t in range(4):
            lanes = slice(t * LANES, (t + 1) * LANES)
            for axis in range(2):
                row = b * 8 + t * 2 + axis
                base = row_of - spread(whole, row)
                f = spread(offset, row)
                ratio = spread(step8, row)
                w = spread(height, row) * jnp.exp(row_of * spread(slope, row))
                if axis == 0:
                    found = []
                    for a in range(8):
                        inverse = pl.reciprocal((base + 8.0 * a) - f, approx=True)
                        found.append(w * inverse)
                        w = w * ratio
                    u_buf[slot, :, lanes] = jnp.concatenate(found, 0).astype(BF16)
                else:
                    w_real = w * spread(values, b * 8 + t * 2)
                    w_imag = w * spread(values, b * 8 + t * 2 + 1)
                    real, imag = [], []
                    for a in range(8):
                        inverse = pl.reciprocal((base + 8.0 * a) - f, approx=True)
                        real.append(w_real * inverse)
                        imag.append(w_imag * inverse)
                        w_real = w_real * ratio
                        w_imag = w_imag * ratio
                    v_buf[slot, :TILE, lanes] = jnp.concatenate(real, 0).astype(BF16)
                    v_buf[slot, TILE:, lanes] = jnp.concatenate(imag, 0).astype(BF16)

    def patch_of(slot):
        return lax.dot_general(
            u_buf[slot], v_buf[slot], (((1,), (1,)), ((), ())), preferred_element_type=F32
        )

    def deposit(b, patch):
        tile = tile_ref[0, b]
        at = (
            pl.ds(pl.multiple_of((tile // NBLK) * TILE, TILE), TILE),
            pl.ds(pl.multiple_of((tile % NBLK) * LANES, LANES), LANES),
        )
        acc[at] = acc[at] + patch

    @pl.loop(0, BLOCKS // GROUP)
    def _(group):
        held = None
        for i in range(GROUP):
            generate(group * GROUP + i, i)
            patch = patch_of(i)
            if held is not None:
                deposit(group * GROUP + i - 1, held)
            held = patch
        deposit(group * GROUP + GROUP - 1, held)

    for copy in copies[len(first) :]:
        copy.wait()
    bell = bell_ref[...]

    @pl.loop(0, NBLK)
    def _(a):
        at = pl.ds(pl.multiple_of(a * TILE, TILE), TILE)
        for e in range(NBLK):
            lanes = slice(e * LANES, (e + 1) * LANES)
            grid16[at, lanes] = (acc[at, lanes] * bell).astype(BF16)

    sign = jnp.where(lax.broadcasted_iota(jnp.int32, (1, LANES), 1) < CONTRIB, 1.0, -1.0)

    @pl.loop(0, WIDTH // 256)
    def _(n):
        at = pl.ds(pl.multiple_of(n * 256, 256), 256)
        images = jnp.dot(grid16[...], columns[:, at], preferred_element_type=F32) * UNITARY
        stacked[:SUB, at] = images.astype(BF16)
        turned = jnp.concatenate(
            [pltpu.roll(images[:, :LANES], CONTRIB, 1) * sign, pltpu.roll(images[:, LANES:], CONTRIB, 1) * sign], 1
        )
        stacked[SUB:, at] = turned.astype(BF16)

    @pl.loop(0, WIDTH // 256)
    def _(n):
        at = pl.ds(pl.multiple_of(n * 256, 256), 256)
        spectra = jnp.dot(rows[...], stacked[:, at], preferred_element_type=F32) * UNITARY
        spectra = spectra.astype(BF16)
        for quarter, out in enumerate((keep_ref, send_ref, keep_x_ref, send_x_ref)):
            for i in range(2):
                out[n * 2 + i] = spectra[quarter * ROWS : (quarter + 1) * ROWS, i * LANES : (i + 1) * LANES]


def gridding(place, arrays):
    hbm = pl.BlockSpec(memory_space=pltpu.HBM)
    vector = pl.BlockSpec(memory_space=pltpu.VMEM)
    quarter = jax.ShapeDtypeStruct((NBLK, ROWS, LANES), BF16)
    plane = pltpu.VMEM((BLOCKS * 8, LANES), F32)
    return pl.pallas_call(
        gridding_kernel,
        out_shape=[quarter] * 4
        + [
            jax.ShapeDtypeStruct((2 * ROWS_OUT, SUB), BF16),
            jax.ShapeDtypeStruct((ROWS_OUT, LANES), F32),
            jax.ShapeDtypeStruct((1, FAC), F32),
        ],
        in_specs=[pl.BlockSpec(memory_space=pltpu.SMEM)] + [hbm] * len(arrays),
        out_specs=[vector] * 7,
        scratch_shapes=[
            pltpu.SMEM((1, BLOCKS), jnp.int32),
            plane, plane, plane, plane, plane, plane, plane,
            pltpu.VMEM((GROUP, TILE, BLK), BF16),
            pltpu.VMEM((GROUP, 2 * TILE, BLK), BF16),
            pltpu.VMEM((SUB, WIDTH), F32),
            pltpu.VMEM((SUB, WIDTH), BF16),
            pltpu.VMEM((WIDTH, WIDTH), BF16),
            pltpu.VMEM((WIDTH, WIDTH), BF16),
            pltpu.VMEM((SUB, WIDTH), BF16),
            pltpu.VMEM((TILE, LANES), F32),
            pltpu.SemaphoreType.DMA((12,)),
        ],
        compiler_params=pltpu.CompilerParams(vmem_limit_bytes=24 * 1024 * 1024),
        name="gridding",
    )(place, *(stay(array) for array in arrays))


def stay(array):
    return pltpu.with_memory_space_constraint(array, pltpu.HBM)


CHUNKS = 8


def facet_kernel(own, by_core, by_x, by_both, left, taper_rows, taper_cols, right_hbm, out_hbm, right, mixture, image, sems):
    for chunk in range(CHUNKS):
        pltpu.make_async_copy(right_hbm.at[chunk], right.at[chunk], sems.at[chunk]).start()
    sign = jnp.where(lax.broadcasted_iota(jnp.int32, (1, LANES), 1) < CONTRIB, -UNITARY, UNITARY)

    @pl.loop(0, NBLK // 2)
    def _(n):
        right_side = jnp.concatenate(
            [jnp.concatenate([part[2 * n], part[2 * n + 1]], 1) for part in (own, by_core, by_x, by_both)], 0
        )
        both = jnp.dot(left[...], right_side, preferred_element_type=F32)
        mixed = [
            both[:ROWS_OUT, lanes] * UNITARY + pltpu.roll(both[ROWS_OUT:, lanes], CONTRIB, 1) * sign
            for lanes in (slice(0, LANES), slice(LANES, 2 * LANES))
        ]
        at = pl.ds(pl.multiple_of(n * 2 * LANES, 2 * LANES), 2 * LANES)
        mixture[:, at] = jnp.concatenate(mixed, 1).astype(BF16)

    width = 2 * FAC // CHUNKS

    def departure(chunk):
        first = pl.multiple_of(chunk % (CHUNKS // 2) * width, width)
        into = out_hbm.at[chunk // (CHUNKS // 2), :, pl.ds(first, width)]
        return pltpu.make_async_copy(image.at[chunk], into, sems.at[CHUNKS + chunk])

    @pl.loop(0, CHUNKS)
    def _(chunk):
        pltpu.make_async_copy(right_hbm.at[chunk], right.at[chunk], sems.at[chunk]).wait()
        pixels = jnp.dot(mixture[...], right[chunk], preferred_element_type=F32)
        for i in range(width // LANES):
            first = pl.multiple_of(chunk % (CHUNKS // 2) * width + i * LANES, LANES)
            weight = taper_rows[...] * taper_cols[:, pl.ds(first, LANES)]
            image[chunk, :, i * LANES : (i + 1) * LANES] = pixels[:, i * LANES : (i + 1) * LANES] * weight
        departure(chunk).start()

    for chunk in range(CHUNKS):
        departure(chunk).wait()


def facet(quarters, left, taper_rows, taper_cols, right):
    vector = pl.BlockSpec(memory_space=pltpu.VMEM)
    hbm = pl.BlockSpec(memory_space=pltpu.HBM)
    return pl.pallas_call(
        facet_kernel,
        out_shape=jax.ShapeDtypeStruct((2, ROWS_OUT, FAC), F32),
        in_specs=[vector] * 7 + [hbm],
        out_specs=hbm,
        scratch_shapes=[
            pltpu.VMEM((CHUNKS, WIDTH, 2 * FAC // CHUNKS), BF16),
            pltpu.VMEM((ROWS_OUT, WIDTH), BF16),
            pltpu.VMEM((CHUNKS, ROWS_OUT, 2 * FAC // CHUNKS), F32),
            pltpu.SemaphoreType.DMA((2 * CHUNKS,)),
        ],
        compiler_params=pltpu.CompilerParams(vmem_limit_bytes=24 * 1024 * 1024),
        name="facet",
    )(*quarters, left, taper_rows, taper_cols, stay(right))


def by_visibility_row(array):
    return array.reshape(BLOCKS, 2, BLK // LANES, LANES).transpose(0, 2, 1, 3).reshape(BLOCKS * 8, LANES)


def shards(vis_coords, vis_values, tile_index):
    columns, rows, left, right, taper_rows, taper_cols, bell = (jnp.asarray(table) for table in tables())
    place = lax.axis_index("vis").astype(jnp.int32).reshape(1)

    def swap(array, bit):
        return lax.ppermute(array, "vis", [(i, i ^ bit) for i in range(4)])

    keep, send, keep_x, send_x, left, taper_rows, taper_cols = gridding(
        place,
        [
            tile_index, by_visibility_row(vis_coords), by_visibility_row(vis_values),
            columns, rows, bell, left, taper_rows, taper_cols,
        ],
    )
    got_x = swap(send_x, 1)
    got = swap(send, 1)
    give = (keep_x.astype(F32) + got_x.astype(F32)).astype(BF16)
    arrived = swap(give, 2)
    total = (keep.astype(F32) + got.astype(F32) + arrived.astype(F32)).astype(BF16)
    outgoing = total.reshape(NBLK * NBLK, QUARTER, LANES)
    own = lax.all_to_all(outgoing, "grid", split_axis=0, concat_axis=0, tiled=True)
    own = own.reshape(NBLK, ROWS, LANES)
    by_x = swap(own, 2)
    by_core = swap(own, 1)
    by_both = swap(by_x, 1)
    return facet((own, by_core, by_x, by_both), left, taper_rows, taper_cols, right)[None]


def solution(mesh):
    placed = (P("grid", "vis", None, None), P("grid", "vis", None, None), P("grid", "vis"))
    return jax.shard_map(
        shards, mesh=mesh, in_specs=placed, out_specs=P("grid", None, "vis", None), check_vma=False
    )
```

```python
import functools
import math

import jax
import jax.numpy as jnp
import ml_dtypes
import numpy as np
from jax import lax
from jax.experimental import pallas as pl
from jax.experimental.pallas import tpu as pltpu
from jax.sharding import PartitionSpec as P

SUB = 512
FAC = 1024
CONTRIB = 64
TILE = 64
BLK = 512
BLOCKS = 64
GROUP = 8
NBLK = 8
LANES = 128
QUARTER = 16
ROWS = NBLK * QUARTER
HALF = 2 * ROWS
ROWS_OUT = FAC // 4
WIDTH = 2 * SUB
UNITARY = 1.0 / math.sqrt(SUB)
BF16 = jnp.bfloat16
F32 = jnp.float32


def angles(first, second, length):
    return (first[:, None] * second[None, :] % length) * (2.0 * math.pi / length)


def as_bf16(table):
    return np.ascontiguousarray(table.astype(np.float32)).astype(ml_dtypes.bfloat16)


@functools.lru_cache(maxsize=None)
def tables():
    spectrum = np.arange(SUB)
    turn = angles(spectrum, spectrum, SUB).reshape(NBLK, TILE, NBLK, CONTRIB)
    cos, sin = np.cos(turn), np.sin(turn)
    columns = np.empty((NBLK, 2, TILE, NBLK, 2, CONTRIB))
    columns[:, 0, :, :, 0] = cos
    columns[:, 1, :, :, 0] = sin
    columns[:, 0, :, :, 1] = -sin
    columns[:, 1, :, :, 1] = cos
    columns = as_bf16(columns.reshape(WIDTH, WIDTH))
    turn = angles(spectrum, spectrum, SUB)
    rows = np.concatenate([np.cos(turn), np.sin(turn)], 1)
    rows = rows.reshape(NBLK, 2, 2, QUARTER, WIDTH).transpose(2, 0, 1, 3, 4)
    rows = as_bf16(rows.reshape(SUB, WIDTH))
    turn = angles(np.arange(FAC), spectrum, FAC).reshape(4, ROWS_OUT, NBLK, 4, QUARTER)
    left = np.empty((4, 2, ROWS_OUT, 4, NBLK, QUARTER))
    for g in range(4):
        for j in range(4):
            left[g, 0, :, j] = np.cos(turn[g, :, :, g ^ j])
            left[g, 1, :, j] = np.sin(turn[g, :, :, g ^ j])
    left = as_bf16(left.reshape(4, 2 * ROWS_OUT, SUB))
    turn = angles(spectrum, np.arange(FAC), FAC).reshape(NBLK, CONTRIB, FAC)
    cos, sin = np.cos(turn), np.sin(turn)
    right = np.empty((NBLK, 2, CONTRIB, 2, FAC))
    right[:, 0, :, 0] = cos
    right[:, 1, :, 0] = -sin
    right[:, 0, :, 1] = sin
    right[:, 1, :, 1] = cos
    right = right.reshape(WIDTH, CHUNKS, 2 * FAC // CHUNKS).transpose(1, 0, 2)
    right = as_bf16(right)
    sines = np.sin(math.pi * (np.arange(FAC) + 0.5) / FAC)
    taper = 0.25 + 0.75 * sines * sines
    taper_rows = np.broadcast_to(taper.reshape(4, ROWS_OUT, 1), (4, ROWS_OUT, LANES)).astype(np.float32)
    taper_cols = (taper / math.sqrt(SUB)).reshape(1, FAC).astype(np.float32)
    pixel = np.arange(TILE)
    bell = (1.0 - 2.0 * (pixel % 2)) * np.exp(-(pixel * pixel) / 256.0)
    bell = (bell[:, None] * np.concatenate([bell, bell])[None, :]).astype(np.float32)
    return columns, rows, left, right, np.ascontiguousarray(taper_rows), taper_cols, bell


SINE = [math.pi ** (2 * k + 1) * (-1) ** k / math.factorial(2 * k + 1) for k in range(7)]


def gridding_kernel(
    place_ref, tiles_hbm, coords_hbm, values_hbm, columns_hbm, rows_hbm, bell_hbm, left_hbm, taper_rows_hbm, taper_cols_hbm,
    keep_ref, send_ref, left_ref, taper_rows_ref, taper_cols_ref,
    tile_ref, coords, values, whole, offset, step8, slope, height, u_buf, v_buf, acc, grid16, stacked, columns, rows, bell_ref,
    sems,
):
    place = place_ref[0]
    first = [(coords_hbm, coords), (values_hbm, values), (tiles_hbm, tile_ref)]
    later = [(columns_hbm, columns), (bell_hbm, bell_ref)]
    for i in range(2):
        half = pl.ds(pl.multiple_of((place % 2 ^ i) * HALF, HALF), HALF)
        later.append((rows_hbm.at[half], rows.at[i * HALF : (i + 1) * HALF]))
    last = [(left_hbm.at[place], left_ref), (taper_rows_hbm.at[place], taper_rows_ref), (taper_cols_hbm, taper_cols_ref)]
    copies = [pltpu.make_async_copy(*ends, sems.at[i]) for i, ends in enumerate(first + later + last)]
    for copy in copies:
        copy.start()
    acc[...] = jnp.zeros_like(acc)
    for copy in copies[: len(first)]:
        copy.wait()

    @pl.loop(0, BLOCKS * 8 // 64)
    def _(chunk):
        at = pl.ds(pl.multiple_of(chunk * 64, 64), 64)
        c = coords[at, :]
        r = jnp.round(c)
        f = c - r
        f = jnp.where(jnp.abs(f) < 1e-20, 1e-20, f)
        square = f * f
        sine = jnp.full_like(f, SINE[6])
        for k in range(5, -1, -1):
            sine = sine * square + SINE[k]
        half = r * 0.5
        odd = half - jnp.floor(half)
        sine = sine * f * ((1.0 - 4.0 * odd) * (1.0 / math.pi))
        whole[at, :] = r
        offset[at, :] = f
        step8[at, :] = jnp.exp(c * (1.0 / 16.0))
        slope[at, :] = c * (1.0 / 128.0)
        height[at, :] = sine * jnp.exp(c * c * (-1.0 / 256.0))

    row_of = lax.broadcasted_iota(jnp.int32, (8, LANES), 0).astype(F32)

    def spread(ref, row):
        return jnp.broadcast_to(ref[pl.ds(row, 1), :], (8, LANES))

    def generate(b, slot):
        for t in range(4):
            lanes = slice(t * LANES, (t + 1) * LANES)
            for axis in range(2):
                row = b * 8 + t * 2 + axis
                base = row_of - spread(whole, row)
                f = spread(offset, row)
                ratio = spread(step8, row)
                w = spread(height, row) * jnp.exp(row_of * spread(slope, row))
                if axis == 0:
                    found = []
                    for a in range(8):
                        inverse = pl.reciprocal((base + 8.0 * a) - f, approx=True)
                        found.append(w * inverse)
                        w = w * ratio
                    u_buf[slot, :, lanes] = jnp.concatenate(found, 0).astype(BF16)
                else:
                    w_real = w * spread(values, b * 8 + t * 2)
                    w_imag = w * spread(values, b * 8 + t * 2 + 1)
                    real, imag = [], []
                    for a in range(8):
                        inverse = pl.reciprocal((base + 8.0 * a) - f, approx=True)
                        real.append(w_real * inverse)
                        imag.append(w_imag * inverse)
                        w_real = w_real * ratio
                        w_imag = w_imag * ratio
                    v_buf[slot, :TILE, lanes] = jnp.concatenate(real, 0).astype(BF16)
                    v_buf[slot, TILE:, lanes] = jnp.concatenate(imag, 0).astype(BF16)

    def patch_of(slot):
        return lax.dot_general(
            u_buf[slot], v_buf[slot], (((1,), (1,)), ((), ())), preferred_element_type=F32
        )

    def deposit(b, patch):
        tile = tile_ref[0, b]
        at = (
            pl.ds(pl.multiple_of((tile // NBLK) * TILE, TILE), TILE),
            pl.ds(pl.multiple_of((tile % NBLK) * LANES, LANES), LANES),
        )
        acc[at] = acc[at] + patch

    @pl.loop(0, BLOCKS // GROUP)
    def _(group):
        held = None
        for i in range(GROUP):
            generate(group * GROUP + i, i)
            patch = patch_of(i)
            if held is not None:
                deposit(group * GROUP + i - 1, held)
            held = patch
        deposit(group * GROUP + GROUP - 1, held)

    for copy in copies[len(first) :]:
        copy.wait()
    bell = bell_ref[...]

    @pl.loop(0, NBLK)
    def _(a):
        at = pl.ds(pl.multiple_of(a * TILE, TILE), TILE)
        for e in range(NBLK):
            lanes = slice(e * LANES, (e + 1) * LANES)
            grid16[at, lanes] = (acc[at, lanes] * bell).astype(BF16)

    sign = jnp.where(lax.broadcasted_iota(jnp.int32, (1, LANES), 1) < CONTRIB, 1.0, -1.0)

    @pl.loop(0, WIDTH // 256)
    def _(n):
        at = pl.ds(pl.multiple_of(n * 256, 256), 256)
        images = jnp.dot(grid16[...], columns[:, at], preferred_element_type=F32) * UNITARY
        stacked[:SUB, at] = images.astype(BF16)
        turned = jnp.concatenate(
            [pltpu.roll(images[:, :LANES], CONTRIB, 1) * sign, pltpu.roll(images[:, LANES:], CONTRIB, 1) * sign], 1
        )
        stacked[SUB:, at] = turned.astype(BF16)

    @pl.loop(0, WIDTH // 256)
    def _(n):
        at = pl.ds(pl.multiple_of(n * 256, 256), 256)
        spectra = jnp.dot(rows[...], stacked[:, at], preferred_element_type=F32) * UNITARY
        spectra = spectra.astype(BF16)
        for half, out in enumerate((keep_ref, send_ref)):
            for i in range(2):
                out[n * 2 + i] = spectra[half * HALF : (half + 1) * HALF, i * LANES : (i + 1) * LANES]


def gridding(place, arrays):
    hbm = pl.BlockSpec(memory_space=pltpu.HBM)
    vector = pl.BlockSpec(memory_space=pltpu.VMEM)
    half = jax.ShapeDtypeStruct((NBLK, HALF, LANES), BF16)
    plane = pltpu.VMEM((BLOCKS * 8, LANES), F32)
    return pl.pallas_call(
        gridding_kernel,
        out_shape=[half] * 2
        + [
            jax.ShapeDtypeStruct((2 * ROWS_OUT, SUB), BF16),
            jax.ShapeDtypeStruct((ROWS_OUT, LANES), F32),
            jax.ShapeDtypeStruct((1, FAC), F32),
        ],
        in_specs=[pl.BlockSpec(memory_space=pltpu.SMEM)] + [hbm] * len(arrays),
        out_specs=[vector] * 5,
        scratch_shapes=[
            pltpu.SMEM((1, BLOCKS), jnp.int32),
            plane, plane, plane, plane, plane, plane, plane,
            pltpu.VMEM((GROUP, TILE, BLK), BF16),
            pltpu.VMEM((GROUP, 2 * TILE, BLK), BF16),
            pltpu.VMEM((SUB, WIDTH), F32),
            pltpu.VMEM((SUB, WIDTH), BF16),
            pltpu.VMEM((WIDTH, WIDTH), BF16),
            pltpu.VMEM((WIDTH, WIDTH), BF16),
            pltpu.VMEM((SUB, WIDTH), BF16),
            pltpu.VMEM((TILE, LANES), F32),
            pltpu.SemaphoreType.DMA((10,)),
        ],
        compiler_params=pltpu.CompilerParams(vmem_limit_bytes=24 * 1024 * 1024),
        name="gridding",
    )(place, *(stay(array) for array in arrays))


def stay(array):
    return pltpu.with_memory_space_constraint(array, pltpu.HBM)


def pair_sum_kernel(arrived, *halves):
    count = NBLK * NBLK // 2
    for i, half in enumerate(halves):

        @pl.loop(0, count // 8)
        def _(n):
            pairs = arrived[pl.ds(i * count + n * 8, 8)].astype(F32)
            half[pl.ds(n * 8, 8)] = (pairs[:, 0] + pairs[:, 1]).astype(BF16)


def pair_sum(arrived):
    vector = pl.BlockSpec(memory_space=pltpu.VMEM)
    half = jax.ShapeDtypeStruct((NBLK * NBLK // 2, QUARTER, LANES), BF16)
    return pl.pallas_call(
        pair_sum_kernel,
        out_shape=[half] * 2,
        in_specs=[vector],
        out_specs=[vector] * 2,
        compiler_params=pltpu.CompilerParams(vmem_limit_bytes=24 * 1024 * 1024),
        name="pair_sum",
    )(arrived)


CHUNKS = 8


def facet_kernel(*refs):
    parts = refs[:8]
    left, taper_rows, taper_cols, right_hbm, out_hbm, right, mixture, image, sems = refs[8:]
    for chunk in range(CHUNKS):
        pltpu.make_async_copy(right_hbm.at[chunk], right.at[chunk], sems.at[chunk]).start()
    sign = jnp.where(lax.broadcasted_iota(jnp.int32, (1, LANES), 1) < CONTRIB, -UNITARY, UNITARY)

    for half in range(2):

        @pl.loop(0, NBLK // 4)
        def _(n):
            right_side = jnp.concatenate(
                [jnp.concatenate([part[2 * n], part[2 * n + 1]], 1) for part in parts[half::2]], 0
            )
            both = jnp.dot(left[...], right_side, preferred_element_type=F32)
            mixed = [
                both[:ROWS_OUT, lanes] * UNITARY + pltpu.roll(both[ROWS_OUT:, lanes], CONTRIB, 1) * sign
                for lanes in (slice(0, LANES), slice(LANES, 2 * LANES))
            ]
            first = pl.multiple_of((half * 2 + n) * 2 * LANES, 2 * LANES)
            mixture[:, pl.ds(first, 2 * LANES)] = jnp.concatenate(mixed, 1).astype(BF16)

    width = 2 * FAC // CHUNKS

    def departure(chunk):
        first = pl.multiple_of(chunk % (CHUNKS // 2) * width, width)
        into = out_hbm.at[chunk // (CHUNKS // 2), :, pl.ds(first, width)]
        return pltpu.make_async_copy(image.at[chunk], into, sems.at[CHUNKS + chunk])

    @pl.loop(0, CHUNKS)
    def _(chunk):
        pltpu.make_async_copy(right_hbm.at[chunk], right.at[chunk], sems.at[chunk]).wait()
        pixels = jnp.dot(mixture[...], right[chunk], preferred_element_type=F32)
        for i in range(width // LANES):
            first = pl.multiple_of(chunk % (CHUNKS // 2) * width + i * LANES, LANES)
            weight = taper_rows[...] * taper_cols[:, pl.ds(first, LANES)]
            image[chunk, :, i * LANES : (i + 1) * LANES] = pixels[:, i * LANES : (i + 1) * LANES] * weight
        departure(chunk).start()

    for chunk in range(CHUNKS):
        departure(chunk).wait()


def facet(quarters, left, taper_rows, taper_cols, right):
    vector = pl.BlockSpec(memory_space=pltpu.VMEM)
    hbm = pl.BlockSpec(memory_space=pltpu.HBM)
    return pl.pallas_call(
        facet_kernel,
        out_shape=jax.ShapeDtypeStruct((2, ROWS_OUT, FAC), F32),
        in_specs=[vector] * 11 + [hbm],
        out_specs=hbm,
        scratch_shapes=[
            pltpu.VMEM((CHUNKS, WIDTH, 2 * FAC // CHUNKS), BF16),
            pltpu.VMEM((ROWS_OUT, WIDTH), BF16),
            pltpu.VMEM((CHUNKS, ROWS_OUT, 2 * FAC // CHUNKS), F32),
            pltpu.SemaphoreType.DMA((2 * CHUNKS,)),
        ],
        compiler_params=pltpu.CompilerParams(vmem_limit_bytes=24 * 1024 * 1024),
        name="facet",
    )(*quarters, left, taper_rows, taper_cols, stay(right))


def by_visibility_row(array):
    return array.reshape(BLOCKS, 2, BLK // LANES, LANES).transpose(0, 2, 1, 3).reshape(BLOCKS * 8, LANES)


def shards(vis_coords, vis_values, tile_index):
    columns, rows, left, right, taper_rows, taper_cols, bell = (jnp.asarray(table) for table in tables())
    place = (lax.axis_index("x_lo") * 2 + lax.axis_index("core")).astype(jnp.int32).reshape(1)

    def swap(array, axis):
        return lax.ppermute(array, axis, [(0, 1), (1, 0)])

    keep, send, left, taper_rows, taper_cols = gridding(
        place,
        [
            tile_index, by_visibility_row(vis_coords), by_visibility_row(vis_values),
            columns, rows, bell, left, taper_rows, taper_cols,
        ],
    )
    total = (keep.astype(F32) + swap(send, "core").astype(F32)).astype(BF16)
    outgoing = total.reshape(NBLK * NBLK * 2, QUARTER, LANES)
    arrived = lax.all_to_all(outgoing, ("grid", "x_lo"), split_axis=0, concat_axis=0, tiled=True)
    halves = [half.reshape(NBLK // 2, ROWS, LANES) for half in pair_sum(arrived.reshape(NBLK * NBLK, 2, QUARTER, LANES))]
    by_core = [swap(half, "core") for half in halves]
    by_x = [swap(half, "x_lo") for half in halves]
    by_both = [swap(half, "core") for half in by_x]
    quarters = [*halves, *by_core, *by_x, *by_both]
    return facet(quarters, left, taper_rows, taper_cols, right)[None]


def solution(mesh):
    shape = (mesh.shape["grid"], 2, 2)
    split = jax.sharding.Mesh(mesh.devices.reshape(shape), ("grid", "x_lo", "core"))
    vis = ("x_lo", "core")
    placed = (P("grid", vis, None, None), P("grid", vis, None, None), P("grid", vis))
    return jax.shard_map(
        shards, mesh=split, in_specs=placed, out_specs=P("grid", None, vis, None), check_vma=False
    )
```

```python
import functools
import math

import jax
import jax.numpy as jnp
import ml_dtypes
import numpy as np
from jax import lax
from jax.experimental import pallas as pl
from jax.experimental.pallas import tpu as pltpu
from jax.sharding import PartitionSpec as P

SUB = 512
FAC = 1024
CONTRIB = 64
TILE = 64
BLK = 512
BLOCKS = 64
GROUP = 16
CHUNKS = FAC // 2 // 128
NBLK = 8
LANES = 128
QUARTER = 16
ROWS = NBLK * QUARTER
HALF = 2 * ROWS
ROWS_OUT = FAC // 4
WIDTH = 2 * SUB
BF16 = jnp.bfloat16
F32 = jnp.float32


def angles(first, second, length):
    return (first[:, None] * second[None, :] % length) * (2.0 * math.pi / length)


def as_bf16(table):
    return np.ascontiguousarray(table.astype(np.float32)).astype(ml_dtypes.bfloat16)


@functools.lru_cache(maxsize=None)
def tables():
    spectrum = np.arange(SUB)
    turn = angles(spectrum, np.arange(SUB // 2), SUB)
    turn = turn.reshape(NBLK // 2, 2, TILE // 2, 2, NBLK // 2, CONTRIB // 2, 2).transpose(3, 0, 1, 2, 4, 6, 5)
    turn = np.stack([turn[0], turn[1][:, ::-1]])
    cos, sin = np.cos(turn), np.sin(turn)
    columns = np.empty((2, NBLK // 2, 2, 2, TILE // 2, NBLK // 2, 2, 2, CONTRIB // 2))
    columns[:, :, :, 0, :, :, 0] = cos
    columns[:, :, :, 1, :, :, 0] = sin
    columns[:, :, :, 0, :, :, 1] = -sin
    columns[:, :, :, 1, :, :, 1] = cos
    columns = as_bf16(columns.reshape(2, SUB, SUB))
    turn = angles(spectrum, np.arange(SUB // 4), SUB).reshape(ROWS, 4, SUB // 4).transpose(1, 0, 2)
    rows = as_bf16(np.concatenate([np.cos(turn), np.sin(turn)], 2))
    turn = angles(np.arange(FAC), spectrum, FAC).reshape(4, ROWS_OUT, NBLK, QUARTER, 4)
    left = np.empty((4, 2, ROWS_OUT, 4, NBLK, QUARTER))
    for g in range(4):
        for j in range(4):
            left[g, 0, :, j] = np.cos(turn[g, ..., g ^ j])
            left[g, 1, :, j] = np.sin(turn[g, ..., g ^ j])
    left = as_bf16(left.reshape(4, 2 * ROWS_OUT, SUB))
    turn = angles(spectrum, np.arange(FAC // 2), FAC).reshape(NBLK // 2, 2, CONTRIB // 2, 2, CHUNKS, LANES)
    turn = turn.transpose(3, 4, 0, 1, 2, 5)
    cos, sin = np.cos(turn), np.sin(turn)
    right = np.empty((2, CHUNKS, NBLK // 2, 2, 2, CONTRIB // 2, 2, LANES))
    right[:, :, :, 0, :, :, 0] = cos
    right[:, :, :, 1, :, :, 0] = -sin
    right[:, :, :, 0, :, :, 1] = sin
    right[:, :, :, 1, :, :, 1] = cos
    right = as_bf16(right.reshape(2, CHUNKS, SUB, 2 * LANES))
    sines = np.sin(math.pi * (np.arange(FAC) + 0.5) / FAC)
    taper = 0.25 + 0.75 * sines * sines
    taper_rows = np.broadcast_to(taper.reshape(4, ROWS_OUT, 1), (4, ROWS_OUT, LANES)).astype(np.float32)
    taper_cols = (taper / SUB).reshape(1, FAC).astype(np.float32)
    pixel = np.arange(TILE)
    bell = (1.0 - 2.0 * (pixel % 2)) * np.exp(-(pixel * pixel) / 256.0)
    across = bell.reshape(TILE // 2, 2).T
    across = np.stack([across, across[::-1]])[:, :, None, :].repeat(2, 2).reshape(2, 1, LANES)
    bell = (bell[:, None] * across / SUB).astype(np.float32)
    return columns, rows, left, right, np.ascontiguousarray(taper_rows), taper_cols, bell


SINE = [math.pi ** (2 * k + 1) * (-1) ** k / math.factorial(2 * k + 1) for k in range(7)]


def gridding_kernel(
    place_ref, tiles_hbm, coords_hbm, values_hbm, columns_hbm, rows_hbm, bell_hbm, left_hbm, taper_rows_hbm, taper_cols_hbm,
    keep_ref, send_ref, left_ref, taper_rows_ref, taper_cols_ref,
    tile_ref, coords, values, step8, slope, height, acc, grid16, halves, stacked, columns, rows, bell_ref,
    sems,
):
    place = place_ref[0]
    first = [(coords_hbm, coords), (values_hbm, values), (tiles_hbm, tile_ref)]
    later = [(columns_hbm, columns), (rows_hbm, rows), (bell_hbm, bell_ref)]
    last = [(left_hbm.at[place], left_ref), (taper_rows_hbm.at[place], taper_rows_ref), (taper_cols_hbm, taper_cols_ref)]
    copies = [pltpu.make_async_copy(*ends, sems.at[i]) for i, ends in enumerate(first + later + last)]
    for copy in copies:
        copy.start()
    acc[...] = jnp.zeros_like(acc)
    for copy in copies[: len(first)]:
        copy.wait()

    @pl.loop(0, BLOCKS * 8 // 64)
    def _(chunk):
        at = pl.ds(pl.multiple_of(chunk * 64, 64), 64)
        c = coords[at, :]
        r = jnp.round(c)
        c = jnp.where(c == r, c + (c * 2.0**-23 + 1e-20), c)
        f = c - r
        square = f * f
        sine = jnp.full_like(f, SINE[6])
        for k in range(5, -1, -1):
            sine = sine * square + SINE[k]
        half = r * 0.5
        odd = half - jnp.floor(half)
        sine = sine * f * ((1.0 - 4.0 * odd) * (1.0 / math.pi))
        coords[at, :] = c
        step8[at, :] = jnp.exp(c * (1.0 / 16.0))
        slope[at, :] = c * (1.0 / 128.0)
        height[at, :] = sine * jnp.exp(c * c * (-1.0 / 256.0))

    row_of = lax.broadcasted_iota(jnp.int32, (8, LANES), 0).astype(F32)

    def spread(ref, row, count=8):
        return jnp.broadcast_to(ref[pl.ds(row, 1), :], (count, LANES))

    rises = [row_of + 8.0 * a for a in range(8)]

    def taps(row, rises, ratio):
        c = spread(coords, row)
        w = spread(height, row) * jnp.exp(rises[0] * spread(slope, row))
        found = []
        for rise in rises:
            found.append(w * pl.reciprocal(rise - c, approx=True))
            w = w * ratio
        return jnp.concatenate(found, 0).astype(BF16)

    def patch_of(b):
        odd = (tile_ref[0, b] % 2).astype(F32)
        halves_v = [row_of * 2.0 + odd, row_of * 2.0 + (1.0 - odd)]
        rises_v = [[first + 16.0 * a for a in range(4)] for first in halves_v]
        u, v = [], [[] for _ in range(4)]
        for t in range(4):
            row = b * 8 + t * 2
            u.append(taps(row, rises, spread(step8, row)))
            ratio = spread(step8, row + 1)
            ratio = ratio * ratio
            found = [taps(row + 1, some, ratio) for some in rises_v]
            for part in range(2):
                value = spread(values, row + part, TILE // 2).astype(BF16)
                for half in range(2):
                    v[half * 2 + part].append(found[half] * value)
        u = jnp.concatenate(u, 1)
        v = jnp.concatenate([jnp.concatenate(piece, 1) for piece in v], 0)
        return lax.dot_general(u, v, (((1,), (1,)), ((), ())), preferred_element_type=F32)

    def deposit(b, patch):
        tile = tile_ref[0, b]
        at = (
            pl.ds(pl.multiple_of((tile // NBLK) * TILE, TILE), TILE),
            pl.ds(pl.multiple_of((tile % NBLK) * LANES, LANES), LANES),
        )
        acc[at] = acc[at] + patch

    @pl.loop(0, BLOCKS // GROUP)
    def _(group):
        held = None
        for i in range(GROUP):
            patch = patch_of(group * GROUP + i)
            if held is not None:
                deposit(group * GROUP + i - 1, held)
            held = patch
        deposit(group * GROUP + GROUP - 1, held)

    for copy in copies[len(first) :]:
        copy.wait()

    lane = lax.broadcasted_iota(jnp.int32, (1, LANES), 1)
    left_lane = lane < CONTRIB
    sign = jnp.where(left_lane, 1.0, -1.0)
    sign16 = jnp.broadcast_to(sign, (QUARTER, LANES)).astype(BF16)
    step = SUB // 4

    @pl.loop(0, NBLK)
    def _(a):
        at = pl.ds(pl.multiple_of(a * TILE, TILE), TILE)
        for e in range(NBLK // 2):
            even = acc[at, 2 * e * LANES : (2 * e + 1) * LANES] * bell_ref[0]
            odd = acc[at, (2 * e + 1) * LANES : (2 * e + 2) * LANES] * bell_ref[1]
            lanes = slice(e * LANES, (e + 1) * LANES)
            grid16[0, at, lanes] = jnp.where(left_lane, even, odd).astype(BF16)
            grid16[1, at, lanes] = jnp.where(left_lane, odd, even).astype(BF16)

    @pl.loop(0, SUB // 256)
    def _(n):
        at = pl.ds(pl.multiple_of(n * 256, 256), 256)
        for h in range(2):
            halves[h, :, at] = jnp.dot(grid16[h], columns[h, :, at], preferred_element_type=F32)

    @pl.loop(0, step // QUARTER)
    def _(m):
        first = pl.multiple_of(m * QUARTER, QUARTER)
        for i in range(NBLK // 2):
            lanes = slice(i * LANES, (i + 1) * LANES)
            low, high = [], []
            for q in range(4):
                some = halves[0, pl.ds(first + q * step, QUARTER), lanes]
                other = halves[1, pl.ds(first + q * step, QUARTER), lanes]
                low.append(some + other)
                high.append(some - other)
            for image, block in ((low, i), (high, i + NBLK // 2)):
                into = slice(block * LANES, (block + 1) * LANES)
                sum02, diff02 = image[0] + image[2], image[0] - image[2]
                sum13, diff13 = image[1] + image[3], image[1] - image[3]
                turned13 = pltpu.roll(diff13, CONTRIB, 1) * sign
                for v, x in enumerate((sum02 + sum13, diff02 + turned13, sum02 - sum13, diff02 - turned13)):
                    x = x.astype(BF16)
                    stacked[v, pl.ds(first, QUARTER), into] = x
                    stacked[v, pl.ds(first + step, QUARTER), into] = pltpu.roll(x, CONTRIB, 1) * sign16

    core = place % 2

    @pl.loop(0, WIDTH // 256)
    def _(n):
        at = pl.ds(pl.multiple_of(n * 256, 256), 256)
        for which, out in ((core, keep_ref), (1 - core, send_ref)):
            for x_lo in range(2):
                v = which + 2 * x_lo
                spectra = jnp.dot(rows[v], stacked[v, :, at], preferred_element_type=F32).astype(BF16)
                for i in range(2):
                    for ra in range(NBLK):
                        first = (ra * 2 + x_lo) * QUARTER
                        block = spectra[ra * QUARTER : (ra + 1) * QUARTER, i * LANES : (i + 1) * LANES]
                        out[n * 2 + i, first : first + QUARTER] = block


def gridding(place, arrays):
    hbm = pl.BlockSpec(memory_space=pltpu.HBM)
    vector = pl.BlockSpec(memory_space=pltpu.VMEM)
    half = jax.ShapeDtypeStruct((NBLK, HALF, LANES), BF16)
    plane = pltpu.VMEM((BLOCKS * 8, LANES), F32)
    return pl.pallas_call(
        gridding_kernel,
        out_shape=[half] * 2
        + [
            jax.ShapeDtypeStruct((2 * ROWS_OUT, SUB), BF16),
            jax.ShapeDtypeStruct((ROWS_OUT, LANES), F32),
            jax.ShapeDtypeStruct((1, FAC), F32),
        ],
        in_specs=[pl.BlockSpec(memory_space=pltpu.SMEM)] + [hbm] * len(arrays),
        out_specs=[vector] * 5,
        scratch_shapes=[
            pltpu.SMEM((1, BLOCKS), jnp.int32),
            plane, plane, plane, plane, plane,
            pltpu.VMEM((SUB, WIDTH), F32),
            pltpu.VMEM((2, SUB, SUB), BF16),
            pltpu.VMEM((2, SUB, SUB), F32),
            pltpu.VMEM((4, SUB // 2, WIDTH), BF16),
            pltpu.VMEM((2, SUB, SUB), BF16),
            pltpu.VMEM((4, ROWS, SUB // 2), BF16),
            pltpu.VMEM((2, TILE, LANES), F32),
            pltpu.SemaphoreType.DMA((9,)),
        ],
        compiler_params=pltpu.CompilerParams(vmem_limit_bytes=24 * 1024 * 1024),
        name="gridding",
    )(place, *(stay(array) for array in arrays))


def stay(array):
    return pltpu.with_memory_space_constraint(array, pltpu.HBM)


def pair_sum_kernel(arrived, *halves):
    count = NBLK * NBLK // 2
    for i, half in enumerate(halves):

        @pl.loop(0, count // 8)
        def _(n):
            pairs = arrived[pl.ds(i * count + n * 8, 8)].astype(F32)
            half[pl.ds(n * 8, 8)] = (pairs[:, 0] + pairs[:, 1]).astype(BF16)


def pair_sum(arrived):
    vector = pl.BlockSpec(memory_space=pltpu.VMEM)
    half = jax.ShapeDtypeStruct((NBLK * NBLK // 2, QUARTER, LANES), BF16)
    return pl.pallas_call(
        pair_sum_kernel,
        out_shape=[half] * 2,
        in_specs=[vector],
        out_specs=[vector] * 2,
        compiler_params=pltpu.CompilerParams(vmem_limit_bytes=24 * 1024 * 1024),
        name="pair_sum",
    )(arrived)


def facet_kernel(*refs):
    parts = refs[:8]
    left, taper_rows, taper_cols, right_hbm, out_hbm, right, mixture, image, sems = refs[8:]
    for chunk in range(CHUNKS):
        pltpu.make_async_copy(right_hbm.at[:, chunk], right.at[:, chunk], sems.at[chunk]).start()
    lane = lax.broadcasted_iota(jnp.int32, (1, LANES), 1)
    sign = jnp.where(lane < CONTRIB, -1.0, 1.0)
    even = lane % CONTRIB < CONTRIB // 2
    for half in range(2):

        @pl.loop(0, NBLK // 4)
        def _(n):
            right_side = jnp.concatenate(
                [jnp.concatenate([part[2 * n], part[2 * n + 1]], 1) for part in parts[half::2]], 0
            )
            both = jnp.dot(left[...], right_side, preferred_element_type=F32)
            first, second = (
                both[:ROWS_OUT, lanes] + pltpu.roll(both[ROWS_OUT:, lanes], CONTRIB, 1) * sign
                for lanes in (slice(0, LANES), slice(LANES, 2 * LANES))
            )
            into = pl.ds(pl.multiple_of((half * 2 + n) * LANES, LANES), LANES)
            mixture[0, :, into] = jnp.where(even, first, pltpu.roll(second, CONTRIB // 2, 1)).astype(BF16)
            mixture[1, :, into] = jnp.where(even, pltpu.roll(first, LANES - CONTRIB // 2, 1), second).astype(BF16)

    def departures(chunk):
        copies = []
        for part in range(2):
            for half in range(2):
                first = pl.multiple_of(half * (FAC // 2) + chunk * LANES, LANES)
                into = out_hbm.at[part, :, pl.ds(first, LANES)]
                sem = sems.at[CHUNKS + chunk * 4 + part * 2 + half]
                copies.append(pltpu.make_async_copy(image.at[chunk, part, half], into, sem))
        return copies

    @pl.loop(0, CHUNKS)
    def _(chunk):
        pltpu.make_async_copy(right_hbm.at[:, chunk], right.at[:, chunk], sems.at[chunk]).wait()
        evens = jnp.dot(mixture[0], right[0, chunk], preferred_element_type=F32)
        odds = jnp.dot(mixture[1], right[1, chunk], preferred_element_type=F32)
        weights = [
            taper_rows[...] * taper_cols[:, pl.ds(pl.multiple_of(half * (FAC // 2) + chunk * LANES, LANES), LANES)]
            for half in range(2)
        ]
        for part in range(2):
            lanes = slice(part * LANES, (part + 1) * LANES)
            image[chunk, part, 0] = (evens[:, lanes] + odds[:, lanes]) * weights[0]
            image[chunk, part, 1] = (evens[:, lanes] - odds[:, lanes]) * weights[1]
        for copy in departures(chunk):
            copy.start()

    for chunk in range(CHUNKS):
        for copy in departures(chunk):
            copy.wait()


def facet(quarters, left, taper_rows, taper_cols, right):
    vector = pl.BlockSpec(memory_space=pltpu.VMEM)
    hbm = pl.BlockSpec(memory_space=pltpu.HBM)
    return pl.pallas_call(
        facet_kernel,
        out_shape=jax.ShapeDtypeStruct((2, ROWS_OUT, FAC), F32),
        in_specs=[vector] * 11 + [hbm],
        out_specs=hbm,
        scratch_shapes=[
            pltpu.VMEM((2, CHUNKS, SUB, 2 * LANES), BF16),
            pltpu.VMEM((2, ROWS_OUT, SUB), BF16),
            pltpu.VMEM((CHUNKS, 2, 2, ROWS_OUT, LANES), F32),
            pltpu.SemaphoreType.DMA((5 * CHUNKS,)),
        ],
        compiler_params=pltpu.CompilerParams(vmem_limit_bytes=24 * 1024 * 1024),
        name="facet",
    )(*quarters, left, taper_rows, taper_cols, stay(right))


def by_visibility_row(array):
    return array.reshape(BLOCKS, 2, BLK // LANES, LANES).transpose(0, 2, 1, 3).reshape(BLOCKS * 8, LANES)


def shards(vis_coords, vis_values, tile_index):
    columns, rows, left, right, taper_rows, taper_cols, bell = (jnp.asarray(table) for table in tables())
    place = (lax.axis_index("x_lo") * 2 + lax.axis_index("core")).astype(jnp.int32).reshape(1)

    def swap(array, axis):
        return lax.ppermute(array, axis, [(0, 1), (1, 0)])

    keep, send, left, taper_rows, taper_cols = gridding(
        place,
        [
            tile_index, by_visibility_row(vis_coords), by_visibility_row(vis_values),
            columns, rows, bell, left, taper_rows, taper_cols,
        ],
    )
    total = (keep.astype(F32) + swap(send, "core").astype(F32)).astype(BF16)
    outgoing = total.reshape(NBLK * NBLK * 2, QUARTER, LANES)
    arrived = lax.all_to_all(outgoing, ("grid", "x_lo"), split_axis=0, concat_axis=0, tiled=True)
    halves = [half.reshape(NBLK // 2, ROWS, LANES) for half in pair_sum(arrived.reshape(NBLK * NBLK, 2, QUARTER, LANES))]
    by_core = [swap(half, "core") for half in halves]
    by_x = [swap(half, "x_lo") for half in halves]
    by_both = [swap(half, "core") for half in by_x]
    quarters = [*halves, *by_core, *by_x, *by_both]
    return facet(quarters, left, taper_rows, taper_cols, right)[None]


def solution(mesh):
    shape = (mesh.shape["grid"], 2, 2)
    split = jax.sharding.Mesh(mesh.devices.reshape(shape), ("grid", "x_lo", "core"))
    vis = ("x_lo", "core")
    placed = (P("grid", vis, None, None), P("grid", vis, None, None), P("grid", vis))
    return jax.shard_map(
        shards, mesh=split, in_specs=placed, out_specs=P("grid", None, vis, None), check_vma=False
    )
```

```python
import functools
import math

import jax
import jax.numpy as jnp
import ml_dtypes
import numpy as np
from jax import lax
from jax.experimental import pallas as pl
from jax.experimental.pallas import tpu as pltpu
from jax.sharding import PartitionSpec as P

SUB = 512
FAC = 1024
CONTRIB = 64
TILE = 64
BLK = 512
BLOCKS = 64
GROUP = 16
CHUNKS = FAC // 2 // 128
NBLK = 8
LANES = 128
QUARTER = 16
ROWS = NBLK * QUARTER
HALF = 2 * ROWS
ROWS_OUT = FAC // 4
WIDTH = 2 * SUB
BF16 = jnp.bfloat16
F32 = jnp.float32


def angles(first, second, length):
    return (first[:, None] * second[None, :] % length) * (2.0 * math.pi / length)


def as_bf16(table):
    return np.ascontiguousarray(table.astype(np.float32)).astype(ml_dtypes.bfloat16)


@functools.lru_cache(maxsize=None)
def tables():
    spectrum = np.arange(SUB)
    turn = angles(spectrum, np.arange(SUB // 2), SUB)
    turn = turn.reshape(NBLK // 2, 2, TILE // 2, 2, NBLK // 2, CONTRIB // 2, 2).transpose(3, 0, 1, 2, 4, 6, 5)
    turn = np.stack([turn[0], turn[1][:, ::-1]])
    cos, sin = np.cos(turn), np.sin(turn)
    columns = np.empty((2, NBLK // 2, 2, 2, TILE // 2, NBLK // 2, 2, 2, CONTRIB // 2))
    columns[:, :, :, 0, :, :, 0] = cos
    columns[:, :, :, 1, :, :, 0] = sin
    columns[:, :, :, 0, :, :, 1] = -sin
    columns[:, :, :, 1, :, :, 1] = cos
    columns = as_bf16(columns.reshape(2, SUB, SUB))
    turn = angles(spectrum, np.arange(SUB // 4), SUB).reshape(ROWS, 4, SUB // 4).transpose(1, 0, 2)
    rows = as_bf16(np.concatenate([np.cos(turn), np.sin(turn)], 2))
    turn = angles(np.arange(FAC), spectrum, FAC).reshape(4, ROWS_OUT, NBLK, QUARTER, 4)
    left = np.empty((4, 2, ROWS_OUT, 4, NBLK, QUARTER))
    for g in range(4):
        for j in range(4):
            left[g, 0, :, j] = np.cos(turn[g, ..., g ^ j])
            left[g, 1, :, j] = np.sin(turn[g, ..., g ^ j])
    left = as_bf16(left.reshape(4, 2 * ROWS_OUT, SUB))
    turn = angles(spectrum, np.arange(FAC // 2), FAC).reshape(NBLK // 2, 2, CONTRIB // 2, 2, CHUNKS, LANES)
    turn = turn.transpose(3, 4, 0, 1, 2, 5)
    cos, sin = np.cos(turn), np.sin(turn)
    right = np.empty((2, CHUNKS, NBLK // 2, 2, 2, CONTRIB // 2, 2, LANES))
    right[:, :, :, 0, :, :, 0] = cos
    right[:, :, :, 1, :, :, 0] = -sin
    right[:, :, :, 0, :, :, 1] = sin
    right[:, :, :, 1, :, :, 1] = cos
    right = as_bf16(right.reshape(2, CHUNKS, SUB, 2 * LANES))
    sines = np.sin(math.pi * (np.arange(FAC) + 0.5) / FAC)
    taper = 0.25 + 0.75 * sines * sines
    taper_rows = np.broadcast_to(taper.reshape(4, ROWS_OUT, 1), (4, ROWS_OUT, LANES)).astype(np.float32)
    taper_cols = (taper / SUB).reshape(1, FAC).astype(np.float32)
    pixel = np.arange(TILE)
    bell = (1.0 - 2.0 * (pixel % 2)) * np.exp(-(pixel * pixel) / 256.0)
    across = bell.reshape(TILE // 2, 2).T
    across = np.stack([across, across[::-1]])[:, :, None, :].repeat(2, 2).reshape(2, 1, LANES)
    bell = (bell[:, None] * across / SUB).astype(np.float32)
    return columns, rows, left, right, np.ascontiguousarray(taper_rows), taper_cols, bell


SINE = [math.pi ** (2 * k + 1) * (-1) ** k / math.factorial(2 * k + 1) for k in range(7)]


def gridding_kernel(
    place_ref, tiles_hbm, coords_hbm, values_hbm, columns_hbm, rows_hbm, bell_hbm, left_hbm, taper_rows_hbm, taper_cols_hbm,
    keep_ref, send_ref, left_ref, taper_rows_ref, taper_cols_ref,
    tile_ref, coords, values, step8, slope, height, acc, grid16, halves, stacked, columns, rows, bell_ref,
    sems,
):
    place = place_ref[0]
    first = [(coords_hbm, coords), (values_hbm, values), (tiles_hbm, tile_ref)]
    later = [(columns_hbm, columns), (rows_hbm, rows), (bell_hbm, bell_ref)]
    last = [(left_hbm.at[place], left_ref), (taper_rows_hbm.at[place], taper_rows_ref), (taper_cols_hbm, taper_cols_ref)]
    copies = [pltpu.make_async_copy(*ends, sems.at[i]) for i, ends in enumerate(first + later + last)]
    for copy in copies:
        copy.start()
    acc[...] = jnp.zeros_like(acc)
    for copy in copies[: len(first)]:
        copy.wait()

    @pl.loop(0, BLOCKS * 8 // 64)
    def _(chunk):
        at = pl.ds(pl.multiple_of(chunk * 64, 64), 64)
        c = coords[at, :]
        r = jnp.round(c)
        c = jnp.where(c == r, c + (c * 2.0**-23 + 1e-20), c)
        f = c - r
        square = f * f
        sine = jnp.full_like(f, SINE[6])
        for k in range(5, -1, -1):
            sine = sine * square + SINE[k]
        half = r * 0.5
        odd = half - jnp.floor(half)
        sine = sine * f * ((1.0 - 4.0 * odd) * (1.0 / math.pi))
        coords[at, :] = c
        step8[at, :] = jnp.exp(c * (1.0 / 16.0))
        slope[at, :] = c * (1.0 / 128.0)
        height[at, :] = sine * jnp.exp(c * c * (-1.0 / 256.0))

    row_of = lax.broadcasted_iota(jnp.int32, (8, LANES), 0).astype(F32)

    def spread(ref, row, count=8):
        return jnp.broadcast_to(ref[pl.ds(row, 1), :], (count, LANES))

    rises = [row_of + 8.0 * a for a in range(8)]

    def taps(row, rises, ratio):
        c = spread(coords, row)
        w = spread(height, row) * jnp.exp(rises[0] * spread(slope, row))
        found = []
        for rise in rises:
            found.append(w * pl.reciprocal(rise - c, approx=True))
            w = w * ratio
        return jnp.concatenate(found, 0).astype(BF16)

    def patch_of(b):
        odd = (tile_ref[0, b] % 2).astype(F32)
        halves_v = [row_of * 2.0 + odd, row_of * 2.0 + (1.0 - odd)]
        rises_v = [[first + 16.0 * a for a in range(4)] for first in halves_v]
        u, v = [], [[] for _ in range(4)]
        for t in range(4):
            row = b * 8 + t * 2
            u.append(taps(row, rises, spread(step8, row)))
            ratio = spread(step8, row + 1)
            ratio = ratio * ratio
            found = [taps(row + 1, some, ratio) for some in rises_v]
            for part in range(2):
                value = spread(values, row + part, TILE // 2).astype(BF16)
                for half in range(2):
                    v[half * 2 + part].append(found[half] * value)
        u = jnp.concatenate(u, 1)
        v = jnp.concatenate([jnp.concatenate(piece, 1) for piece in v], 0)
        return lax.dot_general(u, v, (((1,), (1,)), ((), ())), preferred_element_type=F32)

    def deposit(b, patch):
        tile = tile_ref[0, b]
        at = (
            pl.ds(pl.multiple_of((tile // NBLK) * TILE, TILE), TILE),
            pl.ds(pl.multiple_of((tile % NBLK) * LANES, LANES), LANES),
        )
        acc[at] = acc[at] + patch

    @pl.loop(0, BLOCKS // GROUP)
    def _(group):
        held = None
        for i in range(GROUP):
            patch = patch_of(group * GROUP + i)
            if held is not None:
                deposit(group * GROUP + i - 1, held)
            held = patch
        deposit(group * GROUP + GROUP - 1, held)

    for copy in copies[len(first) :]:
        copy.wait()

    lane = lax.broadcasted_iota(jnp.int32, (1, LANES), 1)
    left_lane = lane < CONTRIB
    sign = jnp.where(left_lane, 1.0, -1.0)
    sign16 = jnp.broadcast_to(sign, (QUARTER, LANES)).astype(BF16)
    step = SUB // 4

    @pl.loop(0, NBLK)
    def _(a):
        at = pl.ds(pl.multiple_of(a * TILE, TILE), TILE)
        for e in range(NBLK // 2):
            even = acc[at, 2 * e * LANES : (2 * e + 1) * LANES] * bell_ref[0]
            odd = acc[at, (2 * e + 1) * LANES : (2 * e + 2) * LANES] * bell_ref[1]
            lanes = slice(e * LANES, (e + 1) * LANES)
            grid16[0, at, lanes] = jnp.where(left_lane, even, odd).astype(BF16)
            grid16[1, at, lanes] = jnp.where(left_lane, odd, even).astype(BF16)

    @pl.loop(0, SUB // 256)
    def _(n):
        at = pl.ds(pl.multiple_of(n * 256, 256), 256)
        for h in range(2):
            halves[h, :, at] = jnp.dot(grid16[h], columns[h, :, at], preferred_element_type=F32)

    @pl.loop(0, step // QUARTER)
    def _(m):
        first = pl.multiple_of(m * QUARTER, QUARTER)
        for i in range(NBLK // 2):
            lanes = slice(i * LANES, (i + 1) * LANES)
            low, high = [], []
            for q in range(4):
                some = halves[0, pl.ds(first + q * step, QUARTER), lanes]
                other = halves[1, pl.ds(first + q * step, QUARTER), lanes]
                low.append(some + other)
                high.append(some - other)
            for image, block in ((low, i), (high, i + NBLK // 2)):
                into = slice(block * LANES, (block + 1) * LANES)
                sum02, diff02 = image[0] + image[2], image[0] - image[2]
                sum13, diff13 = image[1] + image[3], image[1] - image[3]
                turned13 = pltpu.roll(diff13, CONTRIB, 1) * sign
                for v, x in enumerate((sum02 + sum13, diff02 + turned13, sum02 - sum13, diff02 - turned13)):
                    x = x.astype(BF16)
                    stacked[v, pl.ds(first, QUARTER), into] = x
                    stacked[v, pl.ds(first + step, QUARTER), into] = pltpu.roll(x, CONTRIB, 1) * sign16

    core = place % 2

    @pl.loop(0, WIDTH // 256)
    def _(n):
        at = pl.ds(pl.multiple_of(n * 256, 256), 256)
        for which, out in ((core, keep_ref), (1 - core, send_ref)):
            for x_lo in range(2):
                v = which + 2 * x_lo
                spectra = jnp.dot(rows[v], stacked[v, :, at], preferred_element_type=F32).astype(BF16)
                for i in range(2):
                    for ra in range(NBLK):
                        first = (ra * 2 + x_lo) * QUARTER
                        block = spectra[ra * QUARTER : (ra + 1) * QUARTER, i * LANES : (i + 1) * LANES]
                        out[n * 2 + i, first : first + QUARTER] = block


def gridding(place, arrays):
    hbm = pl.BlockSpec(memory_space=pltpu.HBM)
    vector = pl.BlockSpec(memory_space=pltpu.VMEM)
    half = jax.ShapeDtypeStruct((NBLK, HALF, LANES), BF16)
    plane = pltpu.VMEM((BLOCKS * 8, LANES), F32)
    return pl.pallas_call(
        gridding_kernel,
        out_shape=[half] * 2
        + [
            jax.ShapeDtypeStruct((2 * ROWS_OUT, SUB), BF16),
            jax.ShapeDtypeStruct((ROWS_OUT, LANES), F32),
            jax.ShapeDtypeStruct((1, FAC), F32),
        ],
        in_specs=[pl.BlockSpec(memory_space=pltpu.SMEM)] + [hbm] * len(arrays),
        out_specs=[vector] * 5,
        scratch_shapes=[
            pltpu.SMEM((1, BLOCKS), jnp.int32),
            plane, plane, plane, plane, plane,
            pltpu.VMEM((SUB, WIDTH), F32),
            pltpu.VMEM((2, SUB, SUB), BF16),
            pltpu.VMEM((2, SUB, SUB), F32),
            pltpu.VMEM((4, SUB // 2, WIDTH), BF16),
            pltpu.VMEM((2, SUB, SUB), BF16),
            pltpu.VMEM((4, ROWS, SUB // 2), BF16),
            pltpu.VMEM((2, TILE, LANES), F32),
            pltpu.SemaphoreType.DMA((9,)),
        ],
        compiler_params=pltpu.CompilerParams(vmem_limit_bytes=24 * 1024 * 1024),
        name="gridding",
    )(place, *(stay(array) for array in arrays))


def stay(array):
    return pltpu.with_memory_space_constraint(array, pltpu.HBM)


def pair_sum_kernel(arrived, *halves):
    count = NBLK * NBLK // 2
    for i, half in enumerate(halves):

        @pl.loop(0, count // 8)
        def _(n):
            pairs = arrived[pl.ds(i * count + n * 8, 8)].astype(F32)
            half[pl.ds(n * 8, 8)] = (pairs[:, 0] + pairs[:, 1]).astype(BF16)


def pair_sum(arrived):
    vector = pl.BlockSpec(memory_space=pltpu.VMEM)
    half = jax.ShapeDtypeStruct((NBLK * NBLK // 2, QUARTER, LANES), BF16)
    return pl.pallas_call(
        pair_sum_kernel,
        out_shape=[half] * 2,
        in_specs=[vector],
        out_specs=[vector] * 2,
        compiler_params=pltpu.CompilerParams(vmem_limit_bytes=24 * 1024 * 1024),
        name="pair_sum",
    )(arrived)


def mix(parts, left, products, mixture):
    lane = lax.broadcasted_iota(jnp.int32, (1, LANES), 1)
    sign = jnp.where(lane < CONTRIB, -1.0, 1.0)
    even = lane % CONTRIB < CONTRIB // 2
    for n in range(NBLK // 4):
        right_side = jnp.concatenate(
            [jnp.concatenate([part[2 * n], part[2 * n + 1]], 1) for part in parts], 0
        )
        products[n] = jnp.dot(left[...], right_side, preferred_element_type=F32)

    for n in range(NBLK // 4):
        into = slice(n * LANES, (n + 1) * LANES)

        @pl.loop(0, ROWS_OUT // 64)
        def _(m):
            at = pl.ds(pl.multiple_of(m * 64, 64), 64)
            below = pl.ds(pl.multiple_of(ROWS_OUT + m * 64, 64), 64)
            first, second = (
                products[n, at, lanes] + pltpu.roll(products[n, below, lanes], CONTRIB, 1) * sign
                for lanes in (slice(0, LANES), slice(LANES, 2 * LANES))
            )
            mixture[0, at, into] = jnp.where(even, first, pltpu.roll(second, CONTRIB // 2, 1)).astype(BF16)
            mixture[1, at, into] = jnp.where(even, pltpu.roll(first, LANES - CONTRIB // 2, 1), second).astype(BF16)


def mixture_kernel(own, by_core, by_x, by_both, left, mixture, products):
    mix((own, by_core, by_x, by_both), left, products, mixture)


def mixture_half(quarters, left):
    vector = pl.BlockSpec(memory_space=pltpu.VMEM)
    return pl.pallas_call(
        mixture_kernel,
        out_shape=jax.ShapeDtypeStruct((2, ROWS_OUT, SUB // 2), BF16),
        in_specs=[vector] * 5,
        out_specs=vector,
        scratch_shapes=[pltpu.VMEM((NBLK // 4, 2 * ROWS_OUT, 2 * LANES), F32)],
        compiler_params=pltpu.CompilerParams(vmem_limit_bytes=24 * 1024 * 1024),
        cost_estimate=pl.CostEstimate(flops=2**28, bytes_accessed=2**20, transcendentals=0),
        name="mixture_half",
    )(*quarters, left)


def facet_kernel(
    own, by_core, by_x, by_both, half_mixture, left, taper_rows, taper_cols, right_hbm, out_hbm,
    right, mixture, products, image, sems,
):
    for chunk in range(CHUNKS):
        pltpu.make_async_copy(right_hbm.at[:, chunk], right.at[:, chunk], sems.at[chunk]).start()
    mix((own, by_core, by_x, by_both), left, products, mixture)

    def departures(chunk):
        copies = []
        for part in range(2):
            for half in range(2):
                first = pl.multiple_of(half * (FAC // 2) + chunk * LANES, LANES)
                into = out_hbm.at[part, :, pl.ds(first, LANES)]
                sem = sems.at[CHUNKS + chunk * 4 + part * 2 + half]
                copies.append(pltpu.make_async_copy(image.at[chunk, part, half], into, sem))
        return copies

    @pl.loop(0, CHUNKS)
    def _(chunk):
        pltpu.make_async_copy(right_hbm.at[:, chunk], right.at[:, chunk], sems.at[chunk]).wait()
        evens, odds = (
            jnp.dot(
                jnp.concatenate([half_mixture[r], mixture[r]], 1), right[r, chunk], preferred_element_type=F32
            )
            for r in range(2)
        )
        weights = [
            taper_rows[...] * taper_cols[:, pl.ds(pl.multiple_of(half * (FAC // 2) + chunk * LANES, LANES), LANES)]
            for half in range(2)
        ]
        for part in range(2):
            lanes = slice(part * LANES, (part + 1) * LANES)
            image[chunk, part, 0] = (evens[:, lanes] + odds[:, lanes]) * weights[0]
            image[chunk, part, 1] = (evens[:, lanes] - odds[:, lanes]) * weights[1]
        for copy in departures(chunk):
            copy.start()

    for chunk in range(CHUNKS):
        for copy in departures(chunk):
            copy.wait()


def facet(quarters, half_mixture, left, taper_rows, taper_cols, right):
    vector = pl.BlockSpec(memory_space=pltpu.VMEM)
    hbm = pl.BlockSpec(memory_space=pltpu.HBM)
    return pl.pallas_call(
        facet_kernel,
        out_shape=jax.ShapeDtypeStruct((2, ROWS_OUT, FAC), F32),
        in_specs=[vector] * 8 + [hbm],
        out_specs=hbm,
        scratch_shapes=[
            pltpu.VMEM((2, CHUNKS, SUB, 2 * LANES), BF16),
            pltpu.VMEM((2, ROWS_OUT, SUB // 2), BF16),
            pltpu.VMEM((NBLK // 4, 2 * ROWS_OUT, 2 * LANES), F32),
            pltpu.VMEM((CHUNKS, 2, 2, ROWS_OUT, LANES), F32),
            pltpu.SemaphoreType.DMA((5 * CHUNKS,)),
        ],
        compiler_params=pltpu.CompilerParams(vmem_limit_bytes=24 * 1024 * 1024),
        name="facet",
    )(*quarters, half_mixture, left, taper_rows, taper_cols, stay(right))


def by_visibility_row(array):
    return array.reshape(BLOCKS, 2, BLK // LANES, LANES).transpose(0, 2, 1, 3).reshape(BLOCKS * 8, LANES)


def shards(vis_coords, vis_values, tile_index):
    columns, rows, left, right, taper_rows, taper_cols, bell = (jnp.asarray(table) for table in tables())
    place = (lax.axis_index("x_lo") * 2 + lax.axis_index("core")).astype(jnp.int32).reshape(1)

    def swap(array, axis):
        return lax.ppermute(array, axis, [(0, 1), (1, 0)])

    keep, send, left, taper_rows, taper_cols = gridding(
        place,
        [
            tile_index, by_visibility_row(vis_coords), by_visibility_row(vis_values),
            columns, rows, bell, left, taper_rows, taper_cols,
        ],
    )
    total = (keep.astype(F32) + swap(send, "core").astype(F32)).astype(BF16)
    outgoing = total.reshape(NBLK * NBLK * 2, QUARTER, LANES)
    arrived = lax.all_to_all(outgoing, ("grid", "x_lo"), split_axis=0, concat_axis=0, tiled=True)
    halves = [half.reshape(NBLK // 2, ROWS, LANES) for half in pair_sum(arrived.reshape(NBLK * NBLK, 2, QUARTER, LANES))]
    by_core = [swap(half, "core") for half in halves]
    by_x = [swap(half, "x_lo") for half in halves]
    by_both = [swap(half, "core") for half in by_x]
    first, second = zip(halves, by_core, by_x, by_both)
    half_mixture = mixture_half(first, left)
    return facet(second, half_mixture, left, taper_rows, taper_cols, right)[None]


def solution(mesh):
    shape = (mesh.shape["grid"], 2, 2)
    split = jax.sharding.Mesh(mesh.devices.reshape(shape), ("grid", "x_lo", "core"))
    vis = ("x_lo", "core")
    placed = (P("grid", vis, None, None), P("grid", vis, None, None), P("grid", vis))
    return jax.shard_map(
        shards, mesh=split, in_specs=placed, out_specs=P("grid", None, vis, None), check_vma=False
    )
```

```python
import functools
import math

import jax
import jax.numpy as jnp
import ml_dtypes
import numpy as np
from jax import lax
from jax.experimental import pallas as pl
from jax.experimental.pallas import tpu as pltpu
from jax.sharding import PartitionSpec as P

SUB = 512
FAC = 1024
CONTRIB = 64
TILE = 64
BLK = 512
BLOCKS = 64
GROUP = 16
CHUNKS = FAC // 2 // 128
NBLK = 8
LANES = 128
QUARTER = 16
ROWS = NBLK * QUARTER
HALF = 2 * ROWS
ROWS_OUT = FAC // 4
WIDTH = 2 * SUB
BF16 = jnp.bfloat16
F32 = jnp.float32


def angles(first, second, length):
    return (first[:, None] * second[None, :] % length) * (2.0 * math.pi / length)


def as_bf16(table):
    return np.ascontiguousarray(table.astype(np.float32)).astype(ml_dtypes.bfloat16)


@functools.lru_cache(maxsize=None)
def tables():
    spectrum = np.arange(SUB)
    turn = angles(spectrum, np.arange(SUB // 2), SUB)
    turn = turn.reshape(NBLK // 2, 2, TILE // 2, 2, NBLK // 2, CONTRIB // 2, 2).transpose(3, 0, 1, 2, 4, 6, 5)
    turn = np.stack([turn[0], turn[1][:, ::-1]])
    cos, sin = np.cos(turn), np.sin(turn)
    columns = np.empty((2, NBLK // 2, 2, 2, TILE // 2, NBLK // 2, 2, 2, CONTRIB // 2))
    columns[:, :, :, 0, :, :, 0] = cos
    columns[:, :, :, 1, :, :, 0] = sin
    columns[:, :, :, 0, :, :, 1] = -sin
    columns[:, :, :, 1, :, :, 1] = cos
    columns = as_bf16(columns.reshape(2, SUB, SUB))
    turn = angles(spectrum, np.arange(SUB // 4), SUB).reshape(ROWS, 4, SUB // 4).transpose(1, 0, 2)
    rows = as_bf16(np.concatenate([np.cos(turn), np.sin(turn)], 2))
    turn = angles(np.arange(FAC), spectrum, FAC).reshape(4, ROWS_OUT, NBLK, QUARTER, 4)
    left = np.empty((4, 2, ROWS_OUT, 4, NBLK, QUARTER))
    for g in range(4):
        for j in range(4):
            left[g, 0, :, j] = np.cos(turn[g, ..., g ^ j])
            left[g, 1, :, j] = np.sin(turn[g, ..., g ^ j])
    left = as_bf16(left.reshape(4, 2 * ROWS_OUT, SUB))
    turn = angles(spectrum, np.arange(FAC // 2), FAC).reshape(NBLK // 2, 2, CONTRIB // 2, 2, CHUNKS, LANES)
    turn = turn.transpose(3, 4, 0, 1, 2, 5)
    cos, sin = np.cos(turn), np.sin(turn)
    right = np.empty((2, CHUNKS, NBLK // 2, 2, 2, CONTRIB // 2, 2, LANES))
    right[:, :, :, 0, :, :, 0] = cos
    right[:, :, :, 1, :, :, 0] = -sin
    right[:, :, :, 0, :, :, 1] = sin
    right[:, :, :, 1, :, :, 1] = cos
    right = as_bf16(right.reshape(2, CHUNKS, SUB, 2 * LANES))
    fold = np.zeros((2, 2, 2, 2, CONTRIB // 2, 2, 2, 2, CONTRIB // 2))
    j = np.arange(CONTRIB // 2)
    for sb in range(2):
        for r in range(2):
            for part in range(2):
                fold[0, sb, part, r, j, r, part, sb, j] = 1.0
                fold[1, sb, part, r, j, r, 1 - part, sb, j] = 1.0 - 2.0 * part
    fold = as_bf16(fold.reshape(SUB, 2 * LANES))
    sines = np.sin(math.pi * (np.arange(FAC) + 0.5) / FAC)
    taper = 0.25 + 0.75 * sines * sines
    taper_rows = np.broadcast_to(taper.reshape(4, ROWS_OUT, 1), (4, ROWS_OUT, LANES)).astype(np.float32)
    taper_cols = (taper / SUB).reshape(1, FAC).astype(np.float32)
    pixel = np.arange(TILE)
    bell = (1.0 - 2.0 * (pixel % 2)) * np.exp(-(pixel * pixel) / 256.0)
    across = bell.reshape(TILE // 2, 2).T
    across = np.stack([across, across[::-1]])[:, :, None, :].repeat(2, 2).reshape(2, 1, LANES)
    bell = (bell[:, None] * across / SUB).astype(np.float32)
    return columns, rows, left, right, fold, np.ascontiguousarray(taper_rows), taper_cols, bell


SINE = [math.pi ** (2 * k + 1) * (-1) ** k / math.factorial(2 * k + 1) for k in range(7)]


def gridding_kernel(
    place_ref, tiles_hbm, coords_hbm, values_hbm, columns_hbm, rows_hbm, bell_hbm, left_hbm, taper_rows_hbm, taper_cols_hbm, right_hbm, fold_hbm,
    keep_ref, send_ref, left_ref, taper_rows_ref, taper_cols_ref, right_ref, fold_ref,
    tile_ref, coords, values, step8, slope, height, acc, grid16, halves, stacked, columns, rows, bell_ref,
    sems,
):
    place = place_ref[0]
    first = [(coords_hbm, coords), (values_hbm, values), (tiles_hbm, tile_ref)]
    later = [(columns_hbm, columns), (rows_hbm, rows), (bell_hbm, bell_ref)]
    last = [(left_hbm.at[place], left_ref), (taper_rows_hbm.at[place], taper_rows_ref)]
    last += [(taper_cols_hbm, taper_cols_ref), (right_hbm, right_ref), (fold_hbm, fold_ref)]
    copies = [pltpu.make_async_copy(*ends, sems.at[i]) for i, ends in enumerate(first + later + last)]
    for copy in copies:
        copy.start()
    acc[...] = jnp.zeros_like(acc)
    for copy in copies[: len(first)]:
        copy.wait()

    @pl.loop(0, BLOCKS * 8 // 64)
    def _(chunk):
        at = pl.ds(pl.multiple_of(chunk * 64, 64), 64)
        c = coords[at, :]
        r = jnp.round(c)
        c = jnp.where(c == r, c + (c * 2.0**-23 + 1e-20), c)
        f = c - r
        square = f * f
        sine = jnp.full_like(f, SINE[6])
        for k in range(5, -1, -1):
            sine = sine * square + SINE[k]
        half = r * 0.5
        odd = half - jnp.floor(half)
        sine = sine * f * ((1.0 - 4.0 * odd) * (1.0 / math.pi))
        coords[at, :] = c
        step8[at, :] = jnp.exp(c * (1.0 / 16.0))
        slope[at, :] = c * (1.0 / 128.0)
        height[at, :] = sine * jnp.exp(c * c * (-1.0 / 256.0))

    row_of = lax.broadcasted_iota(jnp.int32, (8, LANES), 0).astype(F32)

    def spread(ref, row, count=8):
        return jnp.broadcast_to(ref[pl.ds(row, 1), :], (count, LANES))

    rises = [row_of + 8.0 * a for a in range(8)]

    def taps(row, rises, ratio):
        c = spread(coords, row)
        w = spread(height, row) * jnp.exp(rises[0] * spread(slope, row))
        found = []
        for rise in rises:
            found.append(w * pl.reciprocal(rise - c, approx=True))
            w = w * ratio
        return jnp.concatenate(found, 0).astype(BF16)

    def patch_of(b):
        odd = (tile_ref[0, b] % 2).astype(F32)
        halves_v = [row_of * 2.0 + odd, row_of * 2.0 + (1.0 - odd)]
        rises_v = [[first + 16.0 * a for a in range(4)] for first in halves_v]
        u, v = [], [[] for _ in range(4)]
        for t in range(4):
            row = b * 8 + t * 2
            u.append(taps(row, rises, spread(step8, row)))
            ratio = spread(step8, row + 1)
            ratio = ratio * ratio
            found = [taps(row + 1, some, ratio) for some in rises_v]
            for part in range(2):
                value = spread(values, row + part, TILE // 2).astype(BF16)
                for half in range(2):
                    v[half * 2 + part].append(found[half] * value)
        u = jnp.concatenate(u, 1)
        v = jnp.concatenate([jnp.concatenate(piece, 1) for piece in v], 0)
        return lax.dot_general(u, v, (((1,), (1,)), ((), ())), preferred_element_type=F32)

    def deposit(b, patch):
        tile = tile_ref[0, b]
        at = (
            pl.ds(pl.multiple_of((tile // NBLK) * TILE, TILE), TILE),
            pl.ds(pl.multiple_of((tile % NBLK) * LANES, LANES), LANES),
        )
        acc[at] = acc[at] + patch

    @pl.loop(0, BLOCKS // GROUP)
    def _(group):
        held = None
        for i in range(GROUP):
            patch = patch_of(group * GROUP + i)
            if held is not None:
                deposit(group * GROUP + i - 1, held)
            held = patch
        deposit(group * GROUP + GROUP - 1, held)

    for copy in copies[len(first) :]:
        copy.wait()

    lane = lax.broadcasted_iota(jnp.int32, (1, LANES), 1)
    left_lane = lane < CONTRIB
    sign = jnp.where(left_lane, 1.0, -1.0)
    sign16 = jnp.broadcast_to(sign, (QUARTER, LANES)).astype(BF16)
    step = SUB // 4

    @pl.loop(0, NBLK)
    def _(a):
        at = pl.ds(pl.multiple_of(a * TILE, TILE), TILE)
        for e in range(NBLK // 2):
            even = acc[at, 2 * e * LANES : (2 * e + 1) * LANES] * bell_ref[0]
            odd = acc[at, (2 * e + 1) * LANES : (2 * e + 2) * LANES] * bell_ref[1]
            lanes = slice(e * LANES, (e + 1) * LANES)
            grid16[0, at, lanes] = jnp.where(left_lane, even, odd).astype(BF16)
            grid16[1, at, lanes] = jnp.where(left_lane, odd, even).astype(BF16)

    @pl.loop(0, SUB // 256)
    def _(n):
        at = pl.ds(pl.multiple_of(n * 256, 256), 256)
        for h in range(2):
            halves[h, :, at] = jnp.dot(grid16[h], columns[h, :, at], preferred_element_type=F32)

    @pl.loop(0, step // QUARTER)
    def _(m):
        first = pl.multiple_of(m * QUARTER, QUARTER)
        for i in range(NBLK // 2):
            lanes = slice(i * LANES, (i + 1) * LANES)
            low, high = [], []
            for q in range(4):
                some = halves[0, pl.ds(first + q * step, QUARTER), lanes]
                other = halves[1, pl.ds(first + q * step, QUARTER), lanes]
                low.append(some + other)
                high.append(some - other)
            for image, block in ((low, i), (high, i + NBLK // 2)):
                into = slice(block * LANES, (block + 1) * LANES)
                sum02, diff02 = image[0] + image[2], image[0] - image[2]
                sum13, diff13 = image[1] + image[3], image[1] - image[3]
                turned13 = pltpu.roll(diff13, CONTRIB, 1) * sign
                for v, x in enumerate((sum02 + sum13, diff02 + turned13, sum02 - sum13, diff02 - turned13)):
                    x = x.astype(BF16)
                    stacked[v, pl.ds(first, QUARTER), into] = x
                    stacked[v, pl.ds(first + step, QUARTER), into] = pltpu.roll(x, CONTRIB, 1) * sign16

    core = place % 2

    @pl.loop(0, WIDTH // 256)
    def _(n):
        at = pl.ds(pl.multiple_of(n * 256, 256), 256)
        for which, out in ((core, keep_ref), (1 - core, send_ref)):
            for x_lo in range(2):
                v = which + 2 * x_lo
                spectra = jnp.dot(rows[v], stacked[v, :, at], preferred_element_type=F32).astype(BF16)
                for i in range(2):
                    for ra in range(NBLK):
                        first = (ra * 2 + x_lo) * QUARTER
                        block = spectra[ra * QUARTER : (ra + 1) * QUARTER, i * LANES : (i + 1) * LANES]
                        out[n * 2 + i, first : first + QUARTER] = block


def gridding(place, arrays):
    hbm = pl.BlockSpec(memory_space=pltpu.HBM)
    vector = pl.BlockSpec(memory_space=pltpu.VMEM)
    half = jax.ShapeDtypeStruct((NBLK, HALF, LANES), BF16)
    plane = pltpu.VMEM((BLOCKS * 8, LANES), F32)
    return pl.pallas_call(
        gridding_kernel,
        out_shape=[half] * 2
        + [
            jax.ShapeDtypeStruct((2 * ROWS_OUT, SUB), BF16),
            jax.ShapeDtypeStruct((ROWS_OUT, LANES), F32),
            jax.ShapeDtypeStruct((1, FAC), F32),
            jax.ShapeDtypeStruct((2, CHUNKS, SUB, 2 * LANES), BF16),
            jax.ShapeDtypeStruct((SUB, 2 * LANES), BF16),
        ],
        in_specs=[pl.BlockSpec(memory_space=pltpu.SMEM)] + [hbm] * len(arrays),
        out_specs=[vector] * 7,
        scratch_shapes=[
            pltpu.SMEM((1, BLOCKS), jnp.int32),
            plane, plane, plane, plane, plane,
            pltpu.VMEM((SUB, WIDTH), F32),
            pltpu.VMEM((2, SUB, SUB), BF16),
            pltpu.VMEM((2, SUB, SUB), F32),
            pltpu.VMEM((4, SUB // 2, WIDTH), BF16),
            pltpu.VMEM((2, SUB, SUB), BF16),
            pltpu.VMEM((4, ROWS, SUB // 2), BF16),
            pltpu.VMEM((2, TILE, LANES), F32),
            pltpu.SemaphoreType.DMA((11,)),
        ],
        compiler_params=pltpu.CompilerParams(vmem_limit_bytes=24 * 1024 * 1024),
        name="gridding",
    )(place, *(stay(array) for array in arrays))


def stay(array):
    return pltpu.with_memory_space_constraint(array, pltpu.HBM)


def pair_sum_kernel(arrived, *halves):
    count = NBLK * NBLK // 2
    for i, half in enumerate(halves):

        @pl.loop(0, count // 8)
        def _(n):
            pairs = arrived[pl.ds(i * count + n * 8, 8)].astype(F32)
            half[pl.ds(n * 8, 8)] = (pairs[:, 0] + pairs[:, 1]).astype(BF16)


def pair_sum(arrived):
    vector = pl.BlockSpec(memory_space=pltpu.VMEM)
    half = jax.ShapeDtypeStruct((NBLK * NBLK // 2, QUARTER, LANES), BF16)
    return pl.pallas_call(
        pair_sum_kernel,
        out_shape=[half] * 2,
        in_specs=[vector],
        out_specs=[vector] * 2,
        compiler_params=pltpu.CompilerParams(vmem_limit_bytes=24 * 1024 * 1024),
        name="pair_sum",
    )(arrived)


def mix(parts, left, fold, products, mixture):
    for n in range(NBLK // 4):
        right_side = jnp.concatenate(
            [jnp.concatenate([part[2 * n], part[2 * n + 1]], 1) for part in parts], 0
        )
        both = jnp.dot(left[...], right_side, preferred_element_type=F32).astype(BF16)
        at = slice(n * ROWS_OUT, (n + 1) * ROWS_OUT)
        products[at, : 2 * LANES] = both[:ROWS_OUT]
        products[at, 2 * LANES :] = both[ROWS_OUT:]
    mixed = jnp.dot(products[...], fold[...], preferred_element_type=F32).astype(BF16)
    for n in range(NBLK // 4):
        at = slice(n * ROWS_OUT, (n + 1) * ROWS_OUT)
        for r in range(2):
            mixture[r, :, n * LANES : (n + 1) * LANES] = mixed[at, r * LANES : (r + 1) * LANES]


def mixture_kernel(own, by_core, by_x, by_both, left, fold, mixture, products):
    mix((own, by_core, by_x, by_both), left, fold, products, mixture)


def mixture_half(quarters, left, fold):
    vector = pl.BlockSpec(memory_space=pltpu.VMEM)
    return pl.pallas_call(
        mixture_kernel,
        out_shape=jax.ShapeDtypeStruct((2, ROWS_OUT, SUB // 2), BF16),
        in_specs=[vector] * 6,
        out_specs=vector,
        scratch_shapes=[pltpu.VMEM((NBLK // 4 * ROWS_OUT, 4 * LANES), BF16)],
        compiler_params=pltpu.CompilerParams(vmem_limit_bytes=24 * 1024 * 1024),
        cost_estimate=pl.CostEstimate(flops=2**28, bytes_accessed=2**20, transcendentals=0),
        name="mixture_half",
    )(*quarters, left, fold)


def facet_kernel(
    own, by_core, by_x, by_both, half_mixture, left, fold, taper_rows, taper_cols, right, out_hbm,
    mixture, products, image, sems,
):
    mix((own, by_core, by_x, by_both), left, fold, products, mixture)

    def departures(chunk):
        copies = []
        for part in range(2):
            for half in range(2):
                first = pl.multiple_of(half * (FAC // 2) + chunk * LANES, LANES)
                into = out_hbm.at[part, :, pl.ds(first, LANES)]
                sem = sems.at[chunk * 4 + part * 2 + half]
                copies.append(pltpu.make_async_copy(image.at[chunk, part, half], into, sem))
        return copies

    @pl.loop(0, CHUNKS)
    def _(chunk):
        evens, odds = (
            jnp.dot(
                jnp.concatenate([half_mixture[r], mixture[r]], 1), right[r, chunk], preferred_element_type=F32
            )
            for r in range(2)
        )
        weights = [
            taper_rows[...] * taper_cols[:, pl.ds(pl.multiple_of(half * (FAC // 2) + chunk * LANES, LANES), LANES)]
            for half in range(2)
        ]
        for part in range(2):
            lanes = slice(part * LANES, (part + 1) * LANES)
            image[chunk, part, 0] = (evens[:, lanes] + odds[:, lanes]) * weights[0]
            image[chunk, part, 1] = (evens[:, lanes] - odds[:, lanes]) * weights[1]
        for copy in departures(chunk):
            copy.start()

    for chunk in range(CHUNKS):
        for copy in departures(chunk):
            copy.wait()


def facet(quarters, half_mixture, left, fold, taper_rows, taper_cols, right):
    vector = pl.BlockSpec(memory_space=pltpu.VMEM)
    hbm = pl.BlockSpec(memory_space=pltpu.HBM)
    return pl.pallas_call(
        facet_kernel,
        out_shape=jax.ShapeDtypeStruct((2, ROWS_OUT, FAC), F32),
        in_specs=[vector] * 10,
        out_specs=hbm,
        scratch_shapes=[
            pltpu.VMEM((2, ROWS_OUT, SUB // 2), BF16),
            pltpu.VMEM((NBLK // 4 * ROWS_OUT, 4 * LANES), BF16),
            pltpu.VMEM((CHUNKS, 2, 2, ROWS_OUT, LANES), F32),
            pltpu.SemaphoreType.DMA((4 * CHUNKS,)),
        ],
        compiler_params=pltpu.CompilerParams(vmem_limit_bytes=24 * 1024 * 1024),
        name="facet",
    )(*quarters, half_mixture, left, fold, taper_rows, taper_cols, right)


def by_visibility_row(array):
    return array.reshape(BLOCKS, 2, BLK // LANES, LANES).transpose(0, 2, 1, 3).reshape(BLOCKS * 8, LANES)


def shards(vis_coords, vis_values, tile_index):
    columns, rows, left, right, fold, taper_rows, taper_cols, bell = (jnp.asarray(table) for table in tables())
    place = (lax.axis_index("x_lo") * 2 + lax.axis_index("core")).astype(jnp.int32).reshape(1)

    def swap(array, axis):
        return lax.ppermute(array, axis, [(0, 1), (1, 0)])

    keep, send, left, taper_rows, taper_cols, right, fold = gridding(
        place,
        [
            tile_index, by_visibility_row(vis_coords), by_visibility_row(vis_values),
            columns, rows, bell, left, taper_rows, taper_cols, right, fold,
        ],
    )
    total = (keep.astype(F32) + swap(send, "core").astype(F32)).astype(BF16)
    outgoing = total.reshape(NBLK * NBLK * 2, QUARTER, LANES)
    arrived = lax.all_to_all(outgoing, ("grid", "x_lo"), split_axis=0, concat_axis=0, tiled=True)
    halves = [half.reshape(NBLK // 2, ROWS, LANES) for half in pair_sum(arrived.reshape(NBLK * NBLK, 2, QUARTER, LANES))]
    by_core = [swap(half, "core") for half in halves]
    by_x = [swap(half, "x_lo") for half in halves]
    by_both = [swap(half, "core") for half in by_x]
    first, second = zip(halves, by_core, by_x, by_both)
    half_mixture = mixture_half(first, left, fold)
    return facet(second, half_mixture, left, fold, taper_rows, taper_cols, right)[None]


def solution(mesh):
    shape = (mesh.shape["grid"], 2, 2)
    split = jax.sharding.Mesh(mesh.devices.reshape(shape), ("grid", "x_lo", "core"))
    vis = ("x_lo", "core")
    placed = (P("grid", vis, None, None), P("grid", vis, None, None), P("grid", vis))
    return jax.shard_map(
        shards, mesh=split, in_specs=placed, out_specs=P("grid", None, vis, None), check_vma=False
    )
```

```python
import functools
import math

import jax
import jax.numpy as jnp
import ml_dtypes
import numpy as np
from jax import lax
from jax.experimental import pallas as pl
from jax.experimental.pallas import tpu as pltpu
from jax.sharding import PartitionSpec as P

SUB = 512
FAC = 1024
CONTRIB = 64
TILE = 64
BLK = 512
BLOCKS = 64
GROUP = 32
CHUNKS = FAC // 2 // 128
NBLK = 8
LANES = 128
QUARTER = 16
ROWS = NBLK * QUARTER
HALF = 2 * ROWS
ROWS_OUT = FAC // 4
WIDTH = 2 * SUB
BF16 = jnp.bfloat16
F32 = jnp.float32


def angles(first, second, length):
    return (first[:, None] * second[None, :] % length) * (2.0 * math.pi / length)


def as_bf16(table):
    return np.ascontiguousarray(table.astype(np.float32)).astype(ml_dtypes.bfloat16)


@functools.lru_cache(maxsize=None)
def tables():
    spectrum = np.arange(SUB)
    turn = angles(spectrum, np.arange(SUB // 2), SUB)
    turn = turn.reshape(NBLK // 2, 2, TILE // 2, 2, NBLK // 2, CONTRIB // 2, 2).transpose(3, 0, 1, 2, 4, 6, 5)
    turn = np.stack([turn[0], turn[1][:, ::-1]])
    cos, sin = np.cos(turn), np.sin(turn)
    columns = np.empty((2, NBLK // 2, 2, 2, TILE // 2, NBLK // 2, 2, 2, CONTRIB // 2))
    columns[:, :, :, 0, :, :, 0] = cos
    columns[:, :, :, 1, :, :, 0] = sin
    columns[:, :, :, 0, :, :, 1] = -sin
    columns[:, :, :, 1, :, :, 1] = cos
    columns = as_bf16(columns.reshape(2, SUB, SUB))
    turn = angles(spectrum, np.arange(SUB // 4), SUB).reshape(ROWS, 4, SUB // 4).transpose(1, 0, 2)
    rows = as_bf16(np.concatenate([np.cos(turn), np.sin(turn)], 2))
    turn = angles(np.arange(FAC), spectrum, FAC).reshape(4, ROWS_OUT, NBLK, QUARTER, 4)
    left = np.empty((4, 2, ROWS_OUT, 4, NBLK, QUARTER))
    for g in range(4):
        for j in range(4):
            left[g, 0, :, j] = np.cos(turn[g, ..., g ^ j])
            left[g, 1, :, j] = np.sin(turn[g, ..., g ^ j])
    left = as_bf16(left.reshape(4, 2 * ROWS_OUT, SUB))
    turn = angles(spectrum, np.arange(FAC // 2), FAC).reshape(NBLK // 2, 2, CONTRIB // 2, 2, CHUNKS, LANES)
    turn = turn.transpose(3, 4, 0, 1, 2, 5)
    cos, sin = np.cos(turn), np.sin(turn)
    right = np.empty((2, CHUNKS, NBLK // 2, 2, 2, CONTRIB // 2, 2, LANES))
    right[:, :, :, 0, :, :, 0] = cos
    right[:, :, :, 1, :, :, 0] = -sin
    right[:, :, :, 0, :, :, 1] = sin
    right[:, :, :, 1, :, :, 1] = cos
    right = as_bf16(right.reshape(2, CHUNKS, SUB, 2 * LANES))
    fold = np.zeros((2, 2, 2, 2, CONTRIB // 2, 2, 2, 2, CONTRIB // 2))
    j = np.arange(CONTRIB // 2)
    for sb in range(2):
        for r in range(2):
            for part in range(2):
                fold[0, sb, part, r, j, r, part, sb, j] = 1.0
                fold[1, sb, part, r, j, r, 1 - part, sb, j] = 1.0 - 2.0 * part
    fold = as_bf16(fold.reshape(SUB, 2 * LANES))
    spin = np.zeros((2, 2, CONTRIB, 2, 2, CONTRIB))
    j = np.arange(CONTRIB)
    for block in range(2):
        spin[block, 0, j, block, 1, j] = -1.0
        spin[block, 1, j, block, 0, j] = 1.0
    spin = as_bf16(spin.reshape(2 * LANES, 2 * LANES))
    sines = np.sin(math.pi * (np.arange(FAC) + 0.5) / FAC)
    taper = 0.25 + 0.75 * sines * sines
    taper_rows = np.broadcast_to(taper.reshape(4, ROWS_OUT, 1), (4, ROWS_OUT, LANES)).astype(np.float32)
    taper_cols = (taper / SUB).reshape(1, FAC).astype(np.float32)
    pixel = np.arange(TILE)
    bell = (1.0 - 2.0 * (pixel % 2)) * np.exp(-(pixel * pixel) / 256.0)
    across = bell.reshape(TILE // 2, 2).T
    across = np.stack([across, across[::-1]])[:, :, None, :].repeat(2, 2).reshape(2, 1, LANES)
    bell = (bell[:, None] * across / SUB).astype(np.float32)
    return columns, rows, left, right, fold, np.ascontiguousarray(taper_rows), taper_cols, bell, spin


SINE = [math.pi ** (2 * k + 1) * (-1) ** k / math.factorial(2 * k + 1) for k in range(7)]


def gridding_kernel(
    place_ref, tiles_hbm, coords_hbm, values_hbm, columns_hbm, rows_hbm, bell_hbm, left_hbm, taper_rows_hbm, taper_cols_hbm,
    right_hbm, fold_hbm, spin_hbm,
    keep_ref, send_ref, left_ref, taper_rows_ref, taper_cols_ref, right_ref, fold_ref,
    tile_ref, coords, values, step8, slope, height, acc, grid16, halves, stacked, columns, rows, bell_ref,
    spin, apart, sems,
):
    place = place_ref[0]
    first = [(coords_hbm, coords), (values_hbm, values), (tiles_hbm, tile_ref)]
    later = [(columns_hbm, columns), (rows_hbm, rows), (bell_hbm, bell_ref), (spin_hbm, spin)]
    last = [(left_hbm.at[place], left_ref), (taper_rows_hbm.at[place], taper_rows_ref)]
    last += [(taper_cols_hbm, taper_cols_ref), (right_hbm, right_ref), (fold_hbm, fold_ref)]
    copies = [pltpu.make_async_copy(*ends, sems.at[i]) for i, ends in enumerate(first + later + last)]
    for copy in copies:
        copy.start()
    acc[...] = jnp.zeros_like(acc)
    for copy in copies[: len(first)]:
        copy.wait()

    @pl.loop(0, BLOCKS * 8 // 64)
    def _(chunk):
        at = pl.ds(pl.multiple_of(chunk * 64, 64), 64)
        c = coords[at, :]
        r = jnp.round(c)
        c = jnp.where(c == r, c + (c * 2.0**-23 + 1e-20), c)
        f = c - r
        square = f * f
        sine = jnp.full_like(f, SINE[6])
        for k in range(5, -1, -1):
            sine = sine * square + SINE[k]
        half = r * 0.5
        odd = half - jnp.floor(half)
        sine = sine * f * ((1.0 - 4.0 * odd) * (1.0 / math.pi))
        coords[at, :] = c
        step8[at, :] = jnp.exp(c * (1.0 / 16.0))
        slope[at, :] = c * (1.0 / 128.0)
        height[at, :] = sine * jnp.exp(c * c * (-1.0 / 256.0))

    row_of = lax.broadcasted_iota(jnp.int32, (8, LANES), 0).astype(F32)

    def spread(ref, row, count=8):
        return jnp.broadcast_to(ref[pl.ds(row, 1), :], (count, LANES))

    rises = [row_of + 8.0 * a for a in range(8)]

    def taps(row, rises, ratio):
        c = spread(coords, row)
        w = spread(height, row) * jnp.exp(rises[0] * spread(slope, row))
        found = []
        for rise in rises:
            found.append(w * pl.reciprocal(rise - c, approx=True))
            w = w * ratio
        return jnp.concatenate(found, 0).astype(BF16)

    def patch_of(b):
        odd = (tile_ref[0, b] % 2).astype(F32)
        halves_v = [row_of * 2.0 + odd, row_of * 2.0 + (1.0 - odd)]
        rises_v = [[first + 16.0 * a for a in range(4)] for first in halves_v]
        u, v = [], [[] for _ in range(4)]
        for t in range(4):
            row = b * 8 + t * 2
            u.append(taps(row, rises, spread(step8, row)))
            ratio = spread(step8, row + 1)
            ratio = ratio * ratio
            found = [taps(row + 1, some, ratio) for some in rises_v]
            for part in range(2):
                value = spread(values, row + part, TILE // 2).astype(BF16)
                for half in range(2):
                    v[half * 2 + part].append(found[half] * value)
        u = jnp.concatenate(u, 1)
        v = jnp.concatenate([jnp.concatenate(piece, 1) for piece in v], 0)
        return lax.dot_general(u, v, (((1,), (1,)), ((), ())), preferred_element_type=F32)

    def deposit(b, patch):
        tile = tile_ref[0, b]
        at = (
            pl.ds(pl.multiple_of((tile // NBLK) * TILE, TILE), TILE),
            pl.ds(pl.multiple_of((tile % NBLK) * LANES, LANES), LANES),
        )
        acc[at] = acc[at] + patch

    @pl.loop(0, BLOCKS // GROUP)
    def _(group):
        held = None
        for i in range(GROUP):
            patch = patch_of(group * GROUP + i)
            if held is not None:
                deposit(group * GROUP + i - 1, held)
            held = patch
        deposit(group * GROUP + GROUP - 1, held)

    for copy in copies[len(first) :]:
        copy.wait()

    lane = lax.broadcasted_iota(jnp.int32, (1, LANES), 1)
    left_lane = lane < CONTRIB
    step = SUB // 4

    @pl.loop(0, NBLK)
    def _(a):
        at = pl.ds(pl.multiple_of(a * TILE, TILE), TILE)
        for e in range(NBLK // 2):
            even = acc[at, 2 * e * LANES : (2 * e + 1) * LANES] * bell_ref[0]
            odd = acc[at, (2 * e + 1) * LANES : (2 * e + 2) * LANES] * bell_ref[1]
            lanes = slice(e * LANES, (e + 1) * LANES)
            grid16[0, at, lanes] = jnp.where(left_lane, even, odd).astype(BF16)
            grid16[1, at, lanes] = jnp.where(left_lane, odd, even).astype(BF16)

    @pl.loop(0, SUB // 256)
    def _(n):
        at = pl.ds(pl.multiple_of(n * 256, 256), 256)
        for h in range(2):
            halves[h, :, at] = jnp.dot(grid16[h], columns[h, :, at], preferred_element_type=F32)

    @pl.loop(0, step // QUARTER)
    def _(m):
        first = pl.multiple_of(m * QUARTER, QUARTER)
        for i in range(NBLK // 2):
            lanes = slice(i * LANES, (i + 1) * LANES)
            low, high = [], []
            for q in range(4):
                some = halves[0, pl.ds(first + q * step, QUARTER), lanes]
                other = halves[1, pl.ds(first + q * step, QUARTER), lanes]
                low.append(some + other)
                high.append(some - other)
            for image, block in ((low, i), (high, i + NBLK // 2)):
                into = slice(block * LANES, (block + 1) * LANES)
                sum02, diff02 = image[0] + image[2], image[0] - image[2]
                sum13, diff13 = image[1] + image[3], image[1] - image[3]
                for i, x in enumerate((sum02 + sum13, sum02 - sum13, diff02, diff13)):
                    apart[i, pl.ds(first, QUARTER), into] = x.astype(BF16)

    @pl.loop(0, WIDTH // 256)
    def _(n):
        at = pl.ds(pl.multiple_of(n * 256, 256), 256)
        pieces = [apart[i, :, at] for i in range(4)]
        turned = jnp.dot(jnp.concatenate(pieces, 0), spin[...], preferred_element_type=F32)
        turned = [turned[i * step : (i + 1) * step] for i in range(4)]
        stacked[0, :step, at] = pieces[0]
        stacked[0, step:, at] = turned[0].astype(BF16)
        stacked[2, :step, at] = pieces[1]
        stacked[2, step:, at] = turned[1].astype(BF16)
        diff02, diff13 = pieces[2].astype(F32), pieces[3].astype(F32)
        stacked[1, :step, at] = (diff02 + turned[3]).astype(BF16)
        stacked[1, step:, at] = (turned[2] - diff13).astype(BF16)
        stacked[3, :step, at] = (diff02 - turned[3]).astype(BF16)
        stacked[3, step:, at] = (turned[2] + diff13).astype(BF16)

    core = place % 2

    @pl.loop(0, WIDTH // 256)
    def _(n):
        at = pl.ds(pl.multiple_of(n * 256, 256), 256)
        for which, out in ((core, keep_ref), (1 - core, send_ref)):
            for x_lo in range(2):
                v = which + 2 * x_lo
                spectra = jnp.dot(rows[v], stacked[v, :, at], preferred_element_type=F32).astype(BF16)
                for i in range(2):
                    for ra in range(NBLK):
                        first = (ra * 2 + x_lo) * QUARTER
                        block = spectra[ra * QUARTER : (ra + 1) * QUARTER, i * LANES : (i + 1) * LANES]
                        out[n * 2 + i, first : first + QUARTER] = block


def gridding(place, arrays):
    hbm = pl.BlockSpec(memory_space=pltpu.HBM)
    vector = pl.BlockSpec(memory_space=pltpu.VMEM)
    half = jax.ShapeDtypeStruct((NBLK, HALF, LANES), BF16)
    plane = pltpu.VMEM((BLOCKS * 8, LANES), F32)
    return pl.pallas_call(
        gridding_kernel,
        out_shape=[half] * 2
        + [
            jax.ShapeDtypeStruct((2 * ROWS_OUT, SUB), BF16),
            jax.ShapeDtypeStruct((ROWS_OUT, LANES), F32),
            jax.ShapeDtypeStruct((1, FAC), F32),
            jax.ShapeDtypeStruct((2, CHUNKS, SUB, 2 * LANES), BF16),
            jax.ShapeDtypeStruct((SUB, 2 * LANES), BF16),
        ],
        in_specs=[pl.BlockSpec(memory_space=pltpu.SMEM)] + [hbm] * len(arrays),
        out_specs=[vector] * 7,
        scratch_shapes=[
            pltpu.SMEM((1, BLOCKS), jnp.int32),
            plane, plane, plane, plane, plane,
            pltpu.VMEM((SUB, WIDTH), F32),
            pltpu.VMEM((2, SUB, SUB), BF16),
            pltpu.VMEM((2, SUB, SUB), F32),
            pltpu.VMEM((4, SUB // 2, WIDTH), BF16),
            pltpu.VMEM((2, SUB, SUB), BF16),
            pltpu.VMEM((4, ROWS, SUB // 2), BF16),
            pltpu.VMEM((2, TILE, LANES), F32),
            pltpu.VMEM((2 * LANES, 2 * LANES), BF16),
            pltpu.VMEM((4, SUB // 4, WIDTH), BF16),
            pltpu.SemaphoreType.DMA((12,)),
        ],
        compiler_params=pltpu.CompilerParams(vmem_limit_bytes=24 * 1024 * 1024),
        name="gridding",
    )(place, *(stay(array) for array in arrays))


def stay(array):
    return pltpu.with_memory_space_constraint(array, pltpu.HBM)


def pair_sum_kernel(arrived, *halves):
    count = NBLK * NBLK // 2
    for i, half in enumerate(halves):

        @pl.loop(0, count // 8)
        def _(n):
            pairs = arrived[pl.ds(i * count + n * 8, 8)].astype(F32)
            half[pl.ds(n * 8, 8)] = (pairs[:, 0] + pairs[:, 1]).astype(BF16)


def pair_sum(arrived):
    vector = pl.BlockSpec(memory_space=pltpu.VMEM)
    half = jax.ShapeDtypeStruct((NBLK * NBLK // 2, QUARTER, LANES), BF16)
    return pl.pallas_call(
        pair_sum_kernel,
        out_shape=[half] * 2,
        in_specs=[vector],
        out_specs=[vector] * 2,
        compiler_params=pltpu.CompilerParams(vmem_limit_bytes=24 * 1024 * 1024),
        name="pair_sum",
    )(arrived)


def mix(parts, left, fold, products, mixture):
    for n in range(NBLK // 4):
        right_side = jnp.concatenate(
            [jnp.concatenate([part[2 * n], part[2 * n + 1]], 1) for part in parts], 0
        )
        both = jnp.dot(left[...], right_side, preferred_element_type=F32).astype(BF16)
        at = slice(n * ROWS_OUT, (n + 1) * ROWS_OUT)
        products[at, : 2 * LANES] = both[:ROWS_OUT]
        products[at, 2 * LANES :] = both[ROWS_OUT:]
    mixed = jnp.dot(products[...], fold[...], preferred_element_type=F32).astype(BF16)
    for n in range(NBLK // 4):
        at = slice(n * ROWS_OUT, (n + 1) * ROWS_OUT)
        for r in range(2):
            mixture[r, :, n * LANES : (n + 1) * LANES] = mixed[at, r * LANES : (r + 1) * LANES]


def mixture_kernel(own, by_core, by_x, by_both, left, fold, mixture, products):
    mix((own, by_core, by_x, by_both), left, fold, products, mixture)


def mixture_half(quarters, left, fold):
    vector = pl.BlockSpec(memory_space=pltpu.VMEM)
    return pl.pallas_call(
        mixture_kernel,
        out_shape=jax.ShapeDtypeStruct((2, ROWS_OUT, SUB // 2), BF16),
        in_specs=[vector] * 6,
        out_specs=vector,
        scratch_shapes=[pltpu.VMEM((NBLK // 4 * ROWS_OUT, 4 * LANES), BF16)],
        compiler_params=pltpu.CompilerParams(vmem_limit_bytes=24 * 1024 * 1024),
        cost_estimate=pl.CostEstimate(flops=2**28, bytes_accessed=2**20, transcendentals=0),
        name="mixture_half",
    )(*quarters, left, fold)


def facet_kernel(
    own, by_core, by_x, by_both, half_mixture, left, fold, taper_rows, taper_cols, right, out_hbm,
    mixture, products, image, sems,
):
    mix((own, by_core, by_x, by_both), left, fold, products, mixture)

    def departures(chunk):
        copies = []
        for part in range(2):
            for half in range(2):
                first = pl.multiple_of(half * (FAC // 2) + chunk * LANES, LANES)
                into = out_hbm.at[part, :, pl.ds(first, LANES)]
                sem = sems.at[chunk * 4 + part * 2 + half]
                copies.append(pltpu.make_async_copy(image.at[chunk, part, half], into, sem))
        return copies

    @pl.loop(0, CHUNKS)
    def _(chunk):
        evens, odds = (
            jnp.dot(
                jnp.concatenate([half_mixture[r], mixture[r]], 1), right[r, chunk], preferred_element_type=F32
            )
            for r in range(2)
        )
        weights = [
            taper_rows[...] * taper_cols[:, pl.ds(pl.multiple_of(half * (FAC // 2) + chunk * LANES, LANES), LANES)]
            for half in range(2)
        ]
        for part in range(2):
            lanes = slice(part * LANES, (part + 1) * LANES)
            image[chunk, part, 0] = (evens[:, lanes] + odds[:, lanes]) * weights[0]
            image[chunk, part, 1] = (evens[:, lanes] - odds[:, lanes]) * weights[1]
        for copy in departures(chunk):
            copy.start()

    for chunk in range(CHUNKS):
        for copy in departures(chunk):
            copy.wait()


def facet(quarters, half_mixture, left, fold, taper_rows, taper_cols, right):
    vector = pl.BlockSpec(memory_space=pltpu.VMEM)
    hbm = pl.BlockSpec(memory_space=pltpu.HBM)
    return pl.pallas_call(
        facet_kernel,
        out_shape=jax.ShapeDtypeStruct((2, ROWS_OUT, FAC), F32),
        in_specs=[vector] * 10,
        out_specs=hbm,
        scratch_shapes=[
            pltpu.VMEM((2, ROWS_OUT, SUB // 2), BF16),
            pltpu.VMEM((NBLK // 4 * ROWS_OUT, 4 * LANES), BF16),
            pltpu.VMEM((CHUNKS, 2, 2, ROWS_OUT, LANES), F32),
            pltpu.SemaphoreType.DMA((4 * CHUNKS,)),
        ],
        compiler_params=pltpu.CompilerParams(vmem_limit_bytes=24 * 1024 * 1024),
        name="facet",
    )(*quarters, half_mixture, left, fold, taper_rows, taper_cols, right)


def by_visibility_row(array):
    return array.reshape(BLOCKS, 2, BLK // LANES, LANES).transpose(0, 2, 1, 3).reshape(BLOCKS * 8, LANES)


def shards(vis_coords, vis_values, tile_index):
    columns, rows, left, right, fold, taper_rows, taper_cols, bell, spin = (jnp.asarray(table) for table in tables())
    place = (lax.axis_index("x_lo") * 2 + lax.axis_index("core")).astype(jnp.int32).reshape(1)

    def swap(array, axis):
        return lax.ppermute(array, axis, [(0, 1), (1, 0)])

    keep, send, left, taper_rows, taper_cols, right, fold = gridding(
        place,
        [
            tile_index, by_visibility_row(vis_coords), by_visibility_row(vis_values),
            columns, rows, bell, left, taper_rows, taper_cols, right, fold, spin,
        ],
    )
    total = (keep.astype(F32) + swap(send, "core").astype(F32)).astype(BF16)
    outgoing = total.reshape(NBLK * NBLK * 2, QUARTER, LANES)
    arrived = lax.all_to_all(outgoing, ("grid", "x_lo"), split_axis=0, concat_axis=0, tiled=True)
    halves = [half.reshape(NBLK // 2, ROWS, LANES) for half in pair_sum(arrived.reshape(NBLK * NBLK, 2, QUARTER, LANES))]
    by_core = [swap(half, "core") for half in halves]
    by_x = [swap(half, "x_lo") for half in halves]
    by_both = [swap(half, "core") for half in by_x]
    first, second = zip(halves, by_core, by_x, by_both)
    half_mixture = mixture_half(first, left, fold)
    return facet(second, half_mixture, left, fold, taper_rows, taper_cols, right)[None]


def solution(mesh):
    shape = (mesh.shape["grid"], 2, 2)
    split = jax.sharding.Mesh(mesh.devices.reshape(shape), ("grid", "x_lo", "core"))
    vis = ("x_lo", "core")
    placed = (P("grid", vis, None, None), P("grid", vis, None, None), P("grid", vis))
    return jax.shard_map(
        shards, mesh=split, in_specs=placed, out_specs=P("grid", None, vis, None), check_vma=False
    )
```

```python
import functools
import math

import jax
import jax.numpy as jnp
import ml_dtypes
import numpy as np
from jax import lax
from jax.experimental import pallas as pl
from jax.experimental.pallas import tpu as pltpu
from jax.sharding import PartitionSpec as P

SUB = 512
FAC = 1024
CONTRIB = 64
TILE = 64
BLK = 512
BLOCKS = 64
GROUP = 32
CHUNKS = FAC // 2 // 128
NBLK = 8
LANES = 128
QUARTER = 16
ROWS = NBLK * QUARTER
HALF = 2 * ROWS
ROWS_OUT = FAC // 4
WIDTH = 2 * SUB
BF16 = jnp.bfloat16
F32 = jnp.float32


def angles(first, second, length):
    return (first[:, None] * second[None, :] % length) * (2.0 * math.pi / length)


def as_bf16(table):
    return np.ascontiguousarray(table.astype(np.float32)).astype(ml_dtypes.bfloat16)


@functools.lru_cache(maxsize=None)
def tables():
    spectrum = np.arange(SUB)
    turn = angles(spectrum, np.arange(SUB // 2), SUB)
    turn = turn.reshape(NBLK // 2, 2, TILE // 2, 2, NBLK // 2, CONTRIB // 2, 2).transpose(3, 0, 1, 2, 4, 6, 5)
    turn = np.stack([turn[0], turn[1][:, ::-1]])
    cos, sin = np.cos(turn), np.sin(turn)
    columns = np.empty((2, NBLK // 2, 2, 2, TILE // 2, NBLK // 2, 2, 2, CONTRIB // 2))
    columns[:, :, :, 0, :, :, 0] = cos
    columns[:, :, :, 1, :, :, 0] = sin
    columns[:, :, :, 0, :, :, 1] = -sin
    columns[:, :, :, 1, :, :, 1] = cos
    columns = as_bf16(columns.reshape(2, SUB, SUB))
    turn = angles(spectrum, np.arange(SUB // 4), SUB).reshape(ROWS, 4, SUB // 4).transpose(1, 0, 2)
    rows = as_bf16(np.concatenate([np.cos(turn), np.sin(turn)], 2))
    turn = angles(np.arange(FAC), spectrum, FAC).reshape(4, ROWS_OUT, NBLK, QUARTER, 4)
    left = np.empty((4, 2, ROWS_OUT, 4, NBLK, QUARTER))
    for g in range(4):
        for j in range(4):
            left[g, 0, :, j] = np.cos(turn[g, ..., g ^ j])
            left[g, 1, :, j] = np.sin(turn[g, ..., g ^ j])
    left = as_bf16(left.reshape(4, 2 * ROWS_OUT, SUB))
    turn = angles(spectrum, np.arange(FAC // 2), FAC).reshape(NBLK // 2, 2, CONTRIB // 2, 2, CHUNKS, LANES)
    turn = turn.transpose(3, 4, 0, 1, 2, 5)
    cos, sin = np.cos(turn), np.sin(turn)
    right = np.empty((2, CHUNKS, NBLK // 2, 2, 2, CONTRIB // 2, 2, LANES))
    right[:, :, :, 0, :, :, 0] = cos
    right[:, :, :, 1, :, :, 0] = -sin
    right[:, :, :, 0, :, :, 1] = sin
    right[:, :, :, 1, :, :, 1] = cos
    right = as_bf16(right.reshape(2, CHUNKS, SUB, 2 * LANES))
    fold = np.zeros((2, 2, 2, 2, CONTRIB // 2, 2, 2, 2, CONTRIB // 2))
    j = np.arange(CONTRIB // 2)
    for sb in range(2):
        for r in range(2):
            for part in range(2):
                fold[0, sb, part, r, j, r, part, sb, j] = 1.0
                fold[1, sb, part, r, j, r, 1 - part, sb, j] = 1.0 - 2.0 * part
    fold = as_bf16(fold.reshape(SUB, 2 * LANES))
    spin = np.zeros((2, 2, CONTRIB, 2, 2, CONTRIB))
    j = np.arange(CONTRIB)
    for block in range(2):
        spin[block, 0, j, block, 1, j] = -1.0
        spin[block, 1, j, block, 0, j] = 1.0
    spin = as_bf16(spin.reshape(2 * LANES, 2 * LANES))
    sines = np.sin(math.pi * (np.arange(FAC) + 0.5) / FAC)
    taper = 0.25 + 0.75 * sines * sines
    taper_rows = np.broadcast_to(taper.reshape(4, ROWS_OUT, 1), (4, ROWS_OUT, LANES)).astype(np.float32)
    taper_cols = (taper / SUB).reshape(1, FAC).astype(np.float32)
    pixel = np.arange(TILE)
    bell = (1.0 - 2.0 * (pixel % 2)) * np.exp(-(pixel * pixel) / 256.0)
    across = bell.reshape(TILE // 2, 2).T
    across = np.stack([across, across[::-1]])[:, :, None, :].repeat(2, 2).reshape(2, 1, LANES)
    bell = (bell[:, None] * across / SUB).astype(np.float32)
    return columns, rows, left, right, fold, np.ascontiguousarray(taper_rows), taper_cols, bell, spin


SINE = [math.pi ** (2 * k + 1) * (-1) ** k / math.factorial(2 * k + 1) for k in range(7)]


def gridding_kernel(
    place_ref, tiles_hbm, coords_hbm, values_hbm, columns_hbm, rows_hbm, bell_hbm, left_hbm, taper_rows_hbm, taper_cols_hbm,
    right_hbm, fold_hbm, spin_hbm,
    send_ref, rows, stacked, left_ref, taper_rows_ref, taper_cols_ref, right_ref, fold_ref,
    tile_ref, coords, values, step8, slope, height, acc, grid16, halves, columns, bell_ref,
    spin, apart, sems,
):
    place = place_ref[0]
    first = [(coords_hbm, coords), (values_hbm, values), (tiles_hbm, tile_ref)]
    later = [(columns_hbm, columns), (rows_hbm, rows), (bell_hbm, bell_ref), (spin_hbm, spin)]
    last = [(left_hbm.at[place], left_ref), (taper_rows_hbm.at[place], taper_rows_ref)]
    last += [(taper_cols_hbm, taper_cols_ref), (right_hbm, right_ref), (fold_hbm, fold_ref)]
    copies = [pltpu.make_async_copy(*ends, sems.at[i]) for i, ends in enumerate(first + later + last)]
    for copy in copies:
        copy.start()
    acc[...] = jnp.zeros_like(acc)
    for copy in copies[: len(first)]:
        copy.wait()

    @pl.loop(0, BLOCKS * 8 // 64)
    def _(chunk):
        at = pl.ds(pl.multiple_of(chunk * 64, 64), 64)
        c = coords[at, :]
        r = jnp.round(c)
        c = jnp.where(c == r, c + (c * 2.0**-23 + 1e-20), c)
        f = c - r
        square = f * f
        sine = jnp.full_like(f, SINE[6])
        for k in range(5, -1, -1):
            sine = sine * square + SINE[k]
        half = r * 0.5
        odd = half - jnp.floor(half)
        sine = sine * f * ((1.0 - 4.0 * odd) * (1.0 / math.pi))
        coords[at, :] = c
        step8[at, :] = jnp.exp(c * (1.0 / 16.0))
        slope[at, :] = c * (1.0 / 128.0)
        height[at, :] = sine * jnp.exp(c * c * (-1.0 / 256.0))

    row_of = lax.broadcasted_iota(jnp.int32, (8, LANES), 0).astype(F32)

    def spread(ref, row, count=8):
        return jnp.broadcast_to(ref[pl.ds(row, 1), :], (count, LANES))

    rises = [row_of + 8.0 * a for a in range(8)]

    def taps(row, rises, ratio):
        c = spread(coords, row)
        w = spread(height, row) * jnp.exp(rises[0] * spread(slope, row))
        found = []
        for rise in rises:
            found.append(w * pl.reciprocal(rise - c, approx=True))
            w = w * ratio
        return jnp.concatenate(found, 0).astype(BF16)

    def patch_of(b):
        odd = (tile_ref[0, b] % 2).astype(F32)
        halves_v = [row_of * 2.0 + odd, row_of * 2.0 + (1.0 - odd)]
        rises_v = [[first + 16.0 * a for a in range(4)] for first in halves_v]
        u, v = [], [[] for _ in range(4)]
        for t in range(4):
            row = b * 8 + t * 2
            u.append(taps(row, rises, spread(step8, row)))
            ratio = spread(step8, row + 1)
            ratio = ratio * ratio
            found = [taps(row + 1, some, ratio) for some in rises_v]
            for part in range(2):
                value = spread(values, row + part, TILE // 2).astype(BF16)
                for half in range(2):
                    v[half * 2 + part].append(found[half] * value)
        u = jnp.concatenate(u, 1)
        v = jnp.concatenate([jnp.concatenate(piece, 1) for piece in v], 0)
        return lax.dot_general(u, v, (((1,), (1,)), ((), ())), preferred_element_type=F32)

    def deposit(b, patch):
        tile = tile_ref[0, b]
        at = (
            pl.ds(pl.multiple_of((tile // NBLK) * TILE, TILE), TILE),
            pl.ds(pl.multiple_of((tile % NBLK) * LANES, LANES), LANES),
        )
        acc[at] = acc[at] + patch

    @pl.loop(0, BLOCKS // GROUP)
    def _(group):
        held = None
        for i in range(GROUP):
            patch = patch_of(group * GROUP + i)
            if held is not None:
                deposit(group * GROUP + i - 1, held)
            held = patch
        deposit(group * GROUP + GROUP - 1, held)

    for copy in copies[len(first) :]:
        copy.wait()

    lane = lax.broadcasted_iota(jnp.int32, (1, LANES), 1)
    left_lane = lane < CONTRIB
    step = SUB // 4

    @pl.loop(0, NBLK)
    def _(a):
        at = pl.ds(pl.multiple_of(a * TILE, TILE), TILE)
        for e in range(NBLK // 2):
            even = acc[at, 2 * e * LANES : (2 * e + 1) * LANES] * bell_ref[0]
            odd = acc[at, (2 * e + 1) * LANES : (2 * e + 2) * LANES] * bell_ref[1]
            lanes = slice(e * LANES, (e + 1) * LANES)
            grid16[0, at, lanes] = jnp.where(left_lane, even, odd).astype(BF16)
            grid16[1, at, lanes] = jnp.where(left_lane, odd, even).astype(BF16)

    @pl.loop(0, SUB // 256)
    def _(n):
        at = pl.ds(pl.multiple_of(n * 256, 256), 256)
        for h in range(2):
            halves[h, :, at] = jnp.dot(grid16[h], columns[h, :, at], preferred_element_type=F32)

    @pl.loop(0, step // QUARTER)
    def _(m):
        first = pl.multiple_of(m * QUARTER, QUARTER)
        for i in range(NBLK // 2):
            lanes = slice(i * LANES, (i + 1) * LANES)
            low, high = [], []
            for q in range(4):
                some = halves[0, pl.ds(first + q * step, QUARTER), lanes]
                other = halves[1, pl.ds(first + q * step, QUARTER), lanes]
                low.append(some + other)
                high.append(some - other)
            for image, block in ((low, i), (high, i + NBLK // 2)):
                into = slice(block * LANES, (block + 1) * LANES)
                sum02, diff02 = image[0] + image[2], image[0] - image[2]
                sum13, diff13 = image[1] + image[3], image[1] - image[3]
                for i, x in enumerate((sum02 + sum13, sum02 - sum13, diff02, diff13)):
                    apart[i, pl.ds(first, QUARTER), into] = x.astype(BF16)

    @pl.loop(0, WIDTH // 256)
    def _(n):
        at = pl.ds(pl.multiple_of(n * 256, 256), 256)
        pieces = [apart[i, :, at] for i in range(4)]
        turned = jnp.dot(jnp.concatenate(pieces, 0), spin[...], preferred_element_type=F32)
        turned = [turned[i * step : (i + 1) * step] for i in range(4)]
        stacked[0, :step, at] = pieces[0]
        stacked[0, step:, at] = turned[0].astype(BF16)
        stacked[2, :step, at] = pieces[1]
        stacked[2, step:, at] = turned[1].astype(BF16)
        diff02, diff13 = pieces[2].astype(F32), pieces[3].astype(F32)
        stacked[1, :step, at] = (diff02 + turned[3]).astype(BF16)
        stacked[1, step:, at] = (turned[2] - diff13).astype(BF16)
        stacked[3, :step, at] = (diff02 - turned[3]).astype(BF16)
        stacked[3, step:, at] = (turned[2] + diff13).astype(BF16)

    facet_rows(1 - place % 2, rows, stacked, send_ref)


def facet_rows(core, rows, stacked, out):
    @pl.loop(0, WIDTH // 256)
    def _(n):
        at = pl.ds(pl.multiple_of(n * 256, 256), 256)
        for x_lo in range(2):
            v = core + 2 * x_lo
            spectra = jnp.dot(rows[v], stacked[v, :, at], preferred_element_type=F32).astype(BF16)
            for i in range(2):
                for ra in range(NBLK):
                    first = (ra * 2 + x_lo) * QUARTER
                    block = spectra[ra * QUARTER : (ra + 1) * QUARTER, i * LANES : (i + 1) * LANES]
                    out[n * 2 + i, first : first + QUARTER] = block


def keep_kernel(place_ref, rows, stacked, out):
    facet_rows(place_ref[0] % 2, rows, stacked, out)


def keep_half(place, rows, stacked):
    vector = pl.BlockSpec(memory_space=pltpu.VMEM)
    return pl.pallas_call(
        keep_kernel,
        out_shape=jax.ShapeDtypeStruct((NBLK, HALF, LANES), BF16),
        in_specs=[pl.BlockSpec(memory_space=pltpu.SMEM), vector, vector],
        out_specs=vector,
        compiler_params=pltpu.CompilerParams(vmem_limit_bytes=24 * 1024 * 1024),
        cost_estimate=pl.CostEstimate(flops=2**27, bytes_accessed=2**20, transcendentals=0),
        name="keep_half",
    )(place, rows, stacked)


def gridding(place, arrays):
    hbm = pl.BlockSpec(memory_space=pltpu.HBM)
    vector = pl.BlockSpec(memory_space=pltpu.VMEM)
    half = jax.ShapeDtypeStruct((NBLK, HALF, LANES), BF16)
    plane = pltpu.VMEM((BLOCKS * 8, LANES), F32)
    return pl.pallas_call(
        gridding_kernel,
        out_shape=[half]
        + [
            jax.ShapeDtypeStruct((4, ROWS, SUB // 2), BF16),
            jax.ShapeDtypeStruct((4, SUB // 2, WIDTH), BF16),
            jax.ShapeDtypeStruct((2 * ROWS_OUT, SUB), BF16),
            jax.ShapeDtypeStruct((ROWS_OUT, LANES), F32),
            jax.ShapeDtypeStruct((1, FAC), F32),
            jax.ShapeDtypeStruct((2, CHUNKS, SUB, 2 * LANES), BF16),
            jax.ShapeDtypeStruct((SUB, 2 * LANES), BF16),
        ],
        in_specs=[pl.BlockSpec(memory_space=pltpu.SMEM)] + [hbm] * len(arrays),
        out_specs=[vector] * 8,
        scratch_shapes=[
            pltpu.SMEM((1, BLOCKS), jnp.int32),
            plane, plane, plane, plane, plane,
            pltpu.VMEM((SUB, WIDTH), F32),
            pltpu.VMEM((2, SUB, SUB), BF16),
            pltpu.VMEM((2, SUB, SUB), F32),
            pltpu.VMEM((2, SUB, SUB), BF16),
            pltpu.VMEM((2, TILE, LANES), F32),
            pltpu.VMEM((2 * LANES, 2 * LANES), BF16),
            pltpu.VMEM((4, SUB // 4, WIDTH), BF16),
            pltpu.SemaphoreType.DMA((12,)),
        ],
        compiler_params=pltpu.CompilerParams(vmem_limit_bytes=24 * 1024 * 1024),
        name="gridding",
    )(place, *(stay(array) for array in arrays))


def stay(array):
    return pltpu.with_memory_space_constraint(array, pltpu.HBM)


def pair_sum_kernel(arrived, *halves):
    count = NBLK * NBLK // 2
    for i, half in enumerate(halves):

        @pl.loop(0, count // 8)
        def _(n):
            pairs = arrived[pl.ds(i * count + n * 8, 8)].astype(F32)
            half[pl.ds(n * 8, 8)] = (pairs[:, 0] + pairs[:, 1]).astype(BF16)


def pair_sum(arrived):
    vector = pl.BlockSpec(memory_space=pltpu.VMEM)
    half = jax.ShapeDtypeStruct((NBLK * NBLK // 2, QUARTER, LANES), BF16)
    return pl.pallas_call(
        pair_sum_kernel,
        out_shape=[half] * 2,
        in_specs=[vector],
        out_specs=[vector] * 2,
        compiler_params=pltpu.CompilerParams(vmem_limit_bytes=24 * 1024 * 1024),
        name="pair_sum",
    )(arrived)


def mix(parts, left, fold, products, mixture):
    for n in range(NBLK // 4):
        right_side = jnp.concatenate(
            [jnp.concatenate([part[2 * n], part[2 * n + 1]], 1) for part in parts], 0
        )
        both = jnp.dot(left[...], right_side, preferred_element_type=F32).astype(BF16)
        at = slice(n * ROWS_OUT, (n + 1) * ROWS_OUT)
        products[at, : 2 * LANES] = both[:ROWS_OUT]
        products[at, 2 * LANES :] = both[ROWS_OUT:]
    mixed = jnp.dot(products[...], fold[...], preferred_element_type=F32).astype(BF16)
    for n in range(NBLK // 4):
        at = slice(n * ROWS_OUT, (n + 1) * ROWS_OUT)
        for r in range(2):
            mixture[r, :, n * LANES : (n + 1) * LANES] = mixed[at, r * LANES : (r + 1) * LANES]


def mixture_kernel(own, by_core, by_x, by_both, left, fold, mixture, products):
    mix((own, by_core, by_x, by_both), left, fold, products, mixture)


def mixture_half(quarters, left, fold):
    vector = pl.BlockSpec(memory_space=pltpu.VMEM)
    return pl.pallas_call(
        mixture_kernel,
        out_shape=jax.ShapeDtypeStruct((2, ROWS_OUT, SUB // 2), BF16),
        in_specs=[vector] * 6,
        out_specs=vector,
        scratch_shapes=[pltpu.VMEM((NBLK // 4 * ROWS_OUT, 4 * LANES), BF16)],
        compiler_params=pltpu.CompilerParams(vmem_limit_bytes=24 * 1024 * 1024),
        cost_estimate=pl.CostEstimate(flops=2**28, bytes_accessed=2**20, transcendentals=0),
        name="mixture_half",
    )(*quarters, left, fold)


def facet_kernel(
    own, by_core, by_x, by_both, half_mixture, left, fold, taper_rows, taper_cols, right, out_hbm,
    mixture, products, image, sems,
):
    mix((own, by_core, by_x, by_both), left, fold, products, mixture)

    def departures(chunk):
        copies = []
        for part in range(2):
            for half in range(2):
                first = pl.multiple_of(half * (FAC // 2) + chunk * LANES, LANES)
                into = out_hbm.at[part, :, pl.ds(first, LANES)]
                sem = sems.at[chunk * 4 + part * 2 + half]
                copies.append(pltpu.make_async_copy(image.at[chunk, part, half], into, sem))
        return copies

    @pl.loop(0, CHUNKS)
    def _(chunk):
        evens, odds = (
            jnp.dot(
                jnp.concatenate([half_mixture[r], mixture[r]], 1), right[r, chunk], preferred_element_type=F32
            )
            for r in range(2)
        )
        weights = [
            taper_rows[...] * taper_cols[:, pl.ds(pl.multiple_of(half * (FAC // 2) + chunk * LANES, LANES), LANES)]
            for half in range(2)
        ]
        for part in range(2):
            lanes = slice(part * LANES, (part + 1) * LANES)
            image[chunk, part, 0] = (evens[:, lanes] + odds[:, lanes]) * weights[0]
            image[chunk, part, 1] = (evens[:, lanes] - odds[:, lanes]) * weights[1]
        for copy in departures(chunk):
            copy.start()

    for chunk in range(CHUNKS):
        for copy in departures(chunk):
            copy.wait()


def facet(quarters, half_mixture, left, fold, taper_rows, taper_cols, right):
    vector = pl.BlockSpec(memory_space=pltpu.VMEM)
    hbm = pl.BlockSpec(memory_space=pltpu.HBM)
    return pl.pallas_call(
        facet_kernel,
        out_shape=jax.ShapeDtypeStruct((2, ROWS_OUT, FAC), F32),
        in_specs=[vector] * 10,
        out_specs=hbm,
        scratch_shapes=[
            pltpu.VMEM((2, ROWS_OUT, SUB // 2), BF16),
            pltpu.VMEM((NBLK // 4 * ROWS_OUT, 4 * LANES), BF16),
            pltpu.VMEM((CHUNKS, 2, 2, ROWS_OUT, LANES), F32),
            pltpu.SemaphoreType.DMA((4 * CHUNKS,)),
        ],
        compiler_params=pltpu.CompilerParams(vmem_limit_bytes=24 * 1024 * 1024),
        name="facet",
    )(*quarters, half_mixture, left, fold, taper_rows, taper_cols, right)


def by_visibility_row(array):
    return array.reshape(BLOCKS, 2, BLK // LANES, LANES).transpose(0, 2, 1, 3).reshape(BLOCKS * 8, LANES)


def shards(vis_coords, vis_values, tile_index):
    columns, rows, left, right, fold, taper_rows, taper_cols, bell, spin = (jnp.asarray(table) for table in tables())
    place = (lax.axis_index("x_lo") * 2 + lax.axis_index("core")).astype(jnp.int32).reshape(1)

    def swap(array, axis):
        return lax.ppermute(array, axis, [(0, 1), (1, 0)])

    send, rows, stacked, left, taper_rows, taper_cols, right, fold = gridding(
        place,
        [
            tile_index, by_visibility_row(vis_coords), by_visibility_row(vis_values),
            columns, rows, bell, left, taper_rows, taper_cols, right, fold, spin,
        ],
    )
    got = swap(send, "core")
    keep = keep_half(place, rows, stacked)
    total = (keep.astype(F32) + got.astype(F32)).astype(BF16)
    outgoing = total.reshape(NBLK * NBLK * 2, QUARTER, LANES)
    arrived = lax.all_to_all(outgoing, ("grid", "x_lo"), split_axis=0, concat_axis=0, tiled=True)
    halves = [half.reshape(NBLK // 2, ROWS, LANES) for half in pair_sum(arrived.reshape(NBLK * NBLK, 2, QUARTER, LANES))]
    by_core = [swap(half, "core") for half in halves]
    by_x = [swap(half, "x_lo") for half in halves]
    by_both = [swap(half, "core") for half in by_x]
    first, second = zip(halves, by_core, by_x, by_both)
    half_mixture = mixture_half(first, left, fold)
    return facet(second, half_mixture, left, fold, taper_rows, taper_cols, right)[None]


def solution(mesh):
    shape = (mesh.shape["grid"], 2, 2)
    split = jax.sharding.Mesh(mesh.devices.reshape(shape), ("grid", "x_lo", "core"))
    vis = ("x_lo", "core")
    placed = (P("grid", vis, None, None), P("grid", vis, None, None), P("grid", vis))
    return jax.shard_map(
        shards, mesh=split, in_specs=placed, out_specs=P("grid", None, vis, None), check_vma=False
    )
```

```python
import functools
import math

import jax
import jax.numpy as jnp
import ml_dtypes
import numpy as np
from jax import lax
from jax.experimental import pallas as pl
from jax.experimental.pallas import tpu as pltpu
from jax.sharding import PartitionSpec as P

SUB = 512
FAC = 1024
CONTRIB = 64
TILE = 64
BLK = 512
BLOCKS = 64
GROUP = 32
CHUNKS = FAC // 2 // 128
NBLK = 8
LANES = 128
QUARTER = 16
ROWS = NBLK * QUARTER
HALF = 2 * ROWS
ROWS_OUT = FAC // 4
WIDTH = 2 * SUB
BF16 = jnp.bfloat16
F32 = jnp.float32


def angles(first, second, length):
    return (first[:, None] * second[None, :] % length) * (2.0 * math.pi / length)


def as_bf16(table):
    return np.ascontiguousarray(table.astype(np.float32)).astype(ml_dtypes.bfloat16)


@functools.lru_cache(maxsize=None)
def tables():
    spectrum = np.arange(SUB)
    turn = angles(spectrum, np.arange(SUB // 2), SUB)
    turn = turn.reshape(NBLK // 2, 2, TILE // 2, 2, NBLK // 2, CONTRIB // 2, 2).transpose(3, 0, 1, 2, 4, 6, 5)
    turn = np.stack([turn[0], turn[1][:, ::-1]])
    cos, sin = np.cos(turn), np.sin(turn)
    columns = np.empty((2, NBLK // 2, 2, 2, TILE // 2, NBLK // 2, 2, 2, CONTRIB // 2))
    columns[:, :, :, 0, :, :, 0] = cos
    columns[:, :, :, 1, :, :, 0] = sin
    columns[:, :, :, 0, :, :, 1] = -sin
    columns[:, :, :, 1, :, :, 1] = cos
    columns = as_bf16(columns.reshape(2, SUB, SUB))
    turn = angles(spectrum, np.arange(SUB // 4), SUB).reshape(ROWS, 4, SUB // 4).transpose(1, 0, 2)
    rows = as_bf16(np.concatenate([np.cos(turn), np.sin(turn)], 2))
    turn = angles(np.arange(FAC), spectrum, FAC).reshape(4, ROWS_OUT, NBLK, QUARTER, 4)
    left = np.empty((4, 2, ROWS_OUT, 4, NBLK, QUARTER))
    for g in range(4):
        for j in range(4):
            left[g, 0, :, j] = np.cos(turn[g, ..., g ^ j])
            left[g, 1, :, j] = np.sin(turn[g, ..., g ^ j])
    left = as_bf16(left.reshape(4, 2 * ROWS_OUT, SUB))
    turn = angles(spectrum, np.arange(FAC // 2), FAC).reshape(NBLK // 2, 2, CONTRIB // 2, 2, CHUNKS, LANES)
    turn = turn.transpose(3, 4, 0, 1, 2, 5)
    cos, sin = np.cos(turn), np.sin(turn)
    right = np.empty((2, CHUNKS, NBLK // 2, 2, 2, CONTRIB // 2, 2, LANES))
    right[:, :, :, 0, :, :, 0] = cos
    right[:, :, :, 1, :, :, 0] = -sin
    right[:, :, :, 0, :, :, 1] = sin
    right[:, :, :, 1, :, :, 1] = cos
    right = as_bf16(right.reshape(2, CHUNKS, SUB, 2 * LANES))
    fold = np.zeros((2, 2, 2, 2, CONTRIB // 2, 2, 2, 2, CONTRIB // 2))
    j = np.arange(CONTRIB // 2)
    for sb in range(2):
        for r in range(2):
            for part in range(2):
                fold[0, sb, part, r, j, r, part, sb, j] = 1.0
                fold[1, sb, part, r, j, r, 1 - part, sb, j] = 1.0 - 2.0 * part
    fold = as_bf16(fold.reshape(SUB, 2 * LANES))
    spin = np.zeros((2, 2, CONTRIB, 2, 2, CONTRIB))
    j = np.arange(CONTRIB)
    for block in range(2):
        spin[block, 0, j, block, 1, j] = -1.0
        spin[block, 1, j, block, 0, j] = 1.0
    spin = as_bf16(spin.reshape(2 * LANES, 2 * LANES))
    sines = np.sin(math.pi * (np.arange(FAC) + 0.5) / FAC)
    taper = 0.25 + 0.75 * sines * sines
    taper_rows = np.broadcast_to(taper.reshape(4, ROWS_OUT, 1), (4, ROWS_OUT, LANES)).astype(np.float32)
    taper_cols = (taper / SUB).reshape(1, FAC).astype(np.float32)
    pixel = np.arange(TILE)
    bell = (1.0 - 2.0 * (pixel % 2)) * np.exp(-(pixel * pixel) / 256.0)
    across = bell.reshape(TILE // 2, 2).T
    across = np.stack([across, across[::-1]])[:, :, None, :].repeat(2, 2).reshape(2, 1, LANES)
    bell = (bell[:, None] * across / SUB).astype(np.float32)
    return columns, rows, left, right, fold, np.ascontiguousarray(taper_rows), taper_cols, bell, spin


SINE = [math.pi ** (2 * k + 1) * (-1) ** k / math.factorial(2 * k + 1) for k in range(7)]


def gridding_kernel(
    place_ref, tiles_hbm, coords_hbm, values_hbm, columns_hbm, rows_hbm, bell_hbm, left_hbm, taper_rows_hbm, taper_cols_hbm,
    right_hbm, fold_hbm, spin_hbm,
    send_ref, rows, stacked, left_ref, taper_rows_ref, taper_cols_ref, right_ref, fold_ref,
    tile_ref, coords, values, step8, slope, height, acc, grid16, halves, columns, bell_ref,
    spin, apart, sems,
):
    place = place_ref[0]
    first = [(coords_hbm, coords), (values_hbm, values), (tiles_hbm, tile_ref)]
    later = [(columns_hbm, columns), (rows_hbm, rows), (bell_hbm, bell_ref), (spin_hbm, spin)]
    last = [(left_hbm.at[place], left_ref), (taper_rows_hbm.at[place], taper_rows_ref)]
    last += [(taper_cols_hbm, taper_cols_ref), (right_hbm, right_ref), (fold_hbm, fold_ref)]
    copies = [pltpu.make_async_copy(*ends, sems.at[i]) for i, ends in enumerate(first + later + last)]
    for copy in copies[: len(first)]:
        copy.start()
    acc[...] = jnp.zeros_like(acc)
    for copy in copies[: len(first)]:
        copy.wait()
    for copy in copies[len(first) :]:
        copy.start()

    @pl.loop(0, BLOCKS * 8 // 128)
    def _(chunk):
        at = pl.ds(pl.multiple_of(chunk * 128, 128), 128)
        c = coords[at, :]
        r = jnp.round(c)
        c = jnp.where(c == r, c + (c * 2.0**-23 + 1e-20), c)
        f = c - r
        square = f * f
        sine = jnp.full_like(f, SINE[6])
        for k in range(5, -1, -1):
            sine = sine * square + SINE[k]
        half = r * 0.5
        odd = half - jnp.floor(half)
        sine = sine * f * ((1.0 - 4.0 * odd) * (1.0 / math.pi))
        coords[at, :] = c
        step8[at, :] = jnp.exp(c * (1.0 / 16.0))
        slope[at, :] = c * (1.0 / 128.0)
        height[at, :] = sine * jnp.exp(c * c * (-1.0 / 256.0))

    row_of = lax.broadcasted_iota(jnp.int32, (8, LANES), 0).astype(F32)

    def spread(ref, row, count=8):
        return jnp.broadcast_to(ref[pl.ds(row, 1), :], (count, LANES))

    rises = [row_of + 8.0 * a for a in range(8)]

    def taps(row, rises, ratio):
        c = spread(coords, row)
        w = spread(height, row) * jnp.exp(rises[0] * spread(slope, row))
        found = []
        for rise in rises:
            found.append(w * pl.reciprocal(rise - c, approx=True))
            w = w * ratio
        return jnp.concatenate(found, 0).astype(BF16)

    def patch_of(b):
        odd = (tile_ref[0, b] % 2).astype(F32)
        halves_v = [row_of * 2.0 + odd, row_of * 2.0 + (1.0 - odd)]
        rises_v = [[first + 16.0 * a for a in range(4)] for first in halves_v]
        u, v = [], [[] for _ in range(4)]
        for t in range(4):
            row = b * 8 + t * 2
            u.append(taps(row, rises, spread(step8, row)))
            ratio = spread(step8, row + 1)
            ratio = ratio * ratio
            found = [taps(row + 1, some, ratio) for some in rises_v]
            for part in range(2):
                value = spread(values, row + part, TILE // 2).astype(BF16)
                for half in range(2):
                    v[half * 2 + part].append(found[half] * value)
        u = jnp.concatenate(u, 1)
        v = jnp.concatenate([jnp.concatenate(piece, 1) for piece in v], 0)
        return lax.dot_general(u, v, (((1,), (1,)), ((), ())), preferred_element_type=F32)

    def deposit(b, patch):
        tile = tile_ref[0, b]
        at = (
            pl.ds(pl.multiple_of((tile // NBLK) * TILE, TILE), TILE),
            pl.ds(pl.multiple_of((tile % NBLK) * LANES, LANES), LANES),
        )
        acc[at] = acc[at] + patch

    @pl.loop(0, BLOCKS // GROUP)
    def _(group):
        held = None
        for i in range(GROUP):
            patch = patch_of(group * GROUP + i)
            if held is not None:
                deposit(group * GROUP + i - 1, held)
            held = patch
        deposit(group * GROUP + GROUP - 1, held)

    for copy in copies[len(first) :]:
        copy.wait()

    lane = lax.broadcasted_iota(jnp.int32, (1, LANES), 1)
    left_lane = lane < CONTRIB
    step = SUB // 4

    @pl.loop(0, NBLK)
    def _(a):
        at = pl.ds(pl.multiple_of(a * TILE, TILE), TILE)
        for e in range(NBLK // 2):
            even = acc[at, 2 * e * LANES : (2 * e + 1) * LANES] * bell_ref[0]
            odd = acc[at, (2 * e + 1) * LANES : (2 * e + 2) * LANES] * bell_ref[1]
            lanes = slice(e * LANES, (e + 1) * LANES)
            grid16[0, at, lanes] = jnp.where(left_lane, even, odd).astype(BF16)
            grid16[1, at, lanes] = jnp.where(left_lane, odd, even).astype(BF16)

    @pl.loop(0, SUB // 256)
    def _(n):
        at = pl.ds(pl.multiple_of(n * 256, 256), 256)
        for h in range(2):
            halves[h, :, at] = jnp.dot(grid16[h], columns[h, :, at], preferred_element_type=F32)

    @pl.loop(0, step // QUARTER)
    def _(m):
        first = pl.multiple_of(m * QUARTER, QUARTER)
        for i in range(NBLK // 2):
            lanes = slice(i * LANES, (i + 1) * LANES)
            low, high = [], []
            for q in range(4):
                some = halves[0, pl.ds(first + q * step, QUARTER), lanes]
                other = halves[1, pl.ds(first + q * step, QUARTER), lanes]
                low.append(some + other)
                high.append(some - other)
            for image, block in ((low, i), (high, i + NBLK // 2)):
                into = slice(block * LANES, (block + 1) * LANES)
                sum02, diff02 = image[0] + image[2], image[0] - image[2]
                sum13, diff13 = image[1] + image[3], image[1] - image[3]
                for i, x in enumerate((sum02 + sum13, sum02 - sum13, diff02, diff13)):
                    apart[i, pl.ds(first, QUARTER), into] = x.astype(BF16)

    @pl.loop(0, WIDTH // 256)
    def _(n):
        at = pl.ds(pl.multiple_of(n * 256, 256), 256)
        pieces = [apart[i, :, at] for i in range(4)]
        turned = jnp.dot(jnp.concatenate(pieces, 0), spin[...], preferred_element_type=F32)
        turned = [turned[i * step : (i + 1) * step] for i in range(4)]
        stacked[0, :step, at] = pieces[0]
        stacked[0, step:, at] = turned[0].astype(BF16)
        stacked[2, :step, at] = pieces[1]
        stacked[2, step:, at] = turned[1].astype(BF16)
        diff02, diff13 = pieces[2].astype(F32), pieces[3].astype(F32)
        stacked[1, :step, at] = (diff02 + turned[3]).astype(BF16)
        stacked[1, step:, at] = (turned[2] - diff13).astype(BF16)
        stacked[3, :step, at] = (diff02 - turned[3]).astype(BF16)
        stacked[3, step:, at] = (turned[2] + diff13).astype(BF16)

    facet_rows(1 - place % 2, rows, stacked, send_ref)


def facet_rows(core, rows, stacked, out):
    @pl.loop(0, WIDTH // 256)
    def _(n):
        at = pl.ds(pl.multiple_of(n * 256, 256), 256)
        for x_lo in range(2):
            v = core + 2 * x_lo
            spectra = jnp.dot(rows[v], stacked[v, :, at], preferred_element_type=F32).astype(BF16)
            for i in range(2):
                for ra in range(NBLK):
                    first = (ra * 2 + x_lo) * QUARTER
                    block = spectra[ra * QUARTER : (ra + 1) * QUARTER, i * LANES : (i + 1) * LANES]
                    out[n * 2 + i, first : first + QUARTER] = block


def keep_kernel(place_ref, rows, stacked, out):
    facet_rows(place_ref[0] % 2, rows, stacked, out)


def keep_half(place, rows, stacked):
    vector = pl.BlockSpec(memory_space=pltpu.VMEM)
    return pl.pallas_call(
        keep_kernel,
        out_shape=jax.ShapeDtypeStruct((NBLK, HALF, LANES), BF16),
        in_specs=[pl.BlockSpec(memory_space=pltpu.SMEM), vector, vector],
        out_specs=vector,
        compiler_params=pltpu.CompilerParams(vmem_limit_bytes=24 * 1024 * 1024),
        cost_estimate=pl.CostEstimate(flops=2**27, bytes_accessed=2**20, transcendentals=0),
        name="keep_half",
    )(place, rows, stacked)


def gridding(place, arrays):
    hbm = pl.BlockSpec(memory_space=pltpu.HBM)
    vector = pl.BlockSpec(memory_space=pltpu.VMEM)
    half = jax.ShapeDtypeStruct((NBLK, HALF, LANES), BF16)
    plane = pltpu.VMEM((BLOCKS * 8, LANES), F32)
    return pl.pallas_call(
        gridding_kernel,
        out_shape=[half]
        + [
            jax.ShapeDtypeStruct((4, ROWS, SUB // 2), BF16),
            jax.ShapeDtypeStruct((4, SUB // 2, WIDTH), BF16),
            jax.ShapeDtypeStruct((2 * ROWS_OUT, SUB), BF16),
            jax.ShapeDtypeStruct((ROWS_OUT, LANES), F32),
            jax.ShapeDtypeStruct((1, FAC), F32),
            jax.ShapeDtypeStruct((2, CHUNKS, SUB, 2 * LANES), BF16),
            jax.ShapeDtypeStruct((SUB, 2 * LANES), BF16),
        ],
        in_specs=[pl.BlockSpec(memory_space=pltpu.SMEM)] + [hbm] * len(arrays),
        out_specs=[vector] * 8,
        scratch_shapes=[
            pltpu.SMEM((1, BLOCKS), jnp.int32),
            plane, plane, plane, plane, plane,
            pltpu.VMEM((SUB, WIDTH), F32),
            pltpu.VMEM((2, SUB, SUB), BF16),
            pltpu.VMEM((2, SUB, SUB), F32),
            pltpu.VMEM((2, SUB, SUB), BF16),
            pltpu.VMEM((2, TILE, LANES), F32),
            pltpu.VMEM((2 * LANES, 2 * LANES), BF16),
            pltpu.VMEM((4, SUB // 4, WIDTH), BF16),
            pltpu.SemaphoreType.DMA((12,)),
        ],
        compiler_params=pltpu.CompilerParams(vmem_limit_bytes=24 * 1024 * 1024),
        name="gridding",
    )(place, *(stay(array) for array in arrays))


def stay(array):
    return pltpu.with_memory_space_constraint(array, pltpu.HBM)


def pair_sum_kernel(arrived, *halves):
    count = NBLK * NBLK // 2
    for i, half in enumerate(halves):

        @pl.loop(0, count // 8)
        def _(n):
            pairs = arrived[pl.ds(i * count + n * 8, 8)].astype(F32)
            half[pl.ds(n * 8, 8)] = (pairs[:, 0] + pairs[:, 1]).astype(BF16)


def pair_sum(arrived):
    vector = pl.BlockSpec(memory_space=pltpu.VMEM)
    half = jax.ShapeDtypeStruct((NBLK * NBLK // 2, QUARTER, LANES), BF16)
    return pl.pallas_call(
        pair_sum_kernel,
        out_shape=[half] * 2,
        in_specs=[vector],
        out_specs=[vector] * 2,
        compiler_params=pltpu.CompilerParams(vmem_limit_bytes=24 * 1024 * 1024),
        name="pair_sum",
    )(arrived)


def mix(parts, left, fold, products, mixture):
    for n in range(NBLK // 4):
        right_side = jnp.concatenate(
            [jnp.concatenate([part[2 * n], part[2 * n + 1]], 1) for part in parts], 0
        )
        both = jnp.dot(left[...], right_side, preferred_element_type=F32).astype(BF16)
        at = slice(n * ROWS_OUT, (n + 1) * ROWS_OUT)
        products[at, : 2 * LANES] = both[:ROWS_OUT]
        products[at, 2 * LANES :] = both[ROWS_OUT:]
    mixed = jnp.dot(products[...], fold[...], preferred_element_type=F32).astype(BF16)
    for n in range(NBLK // 4):
        at = slice(n * ROWS_OUT, (n + 1) * ROWS_OUT)
        for r in range(2):
            mixture[r, :, n * LANES : (n + 1) * LANES] = mixed[at, r * LANES : (r + 1) * LANES]


def mixture_kernel(own, by_core, by_x, by_both, left, fold, mixture, products):
    mix((own, by_core, by_x, by_both), left, fold, products, mixture)


def mixture_half(quarters, left, fold):
    vector = pl.BlockSpec(memory_space=pltpu.VMEM)
    return pl.pallas_call(
        mixture_kernel,
        out_shape=jax.ShapeDtypeStruct((2, ROWS_OUT, SUB // 2), BF16),
        in_specs=[vector] * 6,
        out_specs=vector,
        scratch_shapes=[pltpu.VMEM((NBLK // 4 * ROWS_OUT, 4 * LANES), BF16)],
        compiler_params=pltpu.CompilerParams(vmem_limit_bytes=24 * 1024 * 1024),
        cost_estimate=pl.CostEstimate(flops=2**28, bytes_accessed=2**20, transcendentals=0),
        name="mixture_half",
    )(*quarters, left, fold)


def facet_kernel(
    own, by_core, by_x, by_both, half_mixture, left, fold, taper_rows, taper_cols, right, out_hbm,
    mixture, products, image, sems,
):
    mix((own, by_core, by_x, by_both), left, fold, products, mixture)

    def departures(chunk):
        copies = []
        for part in range(2):
            for half in range(2):
                first = pl.multiple_of(half * (FAC // 2) + chunk * LANES, LANES)
                into = out_hbm.at[part, :, pl.ds(first, LANES)]
                sem = sems.at[chunk * 4 + part * 2 + half]
                copies.append(pltpu.make_async_copy(image.at[chunk, part, half], into, sem))
        return copies

    @pl.loop(0, CHUNKS)
    def _(chunk):
        evens, odds = (
            jnp.dot(
                jnp.concatenate([half_mixture[r], mixture[r]], 1), right[r, chunk], preferred_element_type=F32
            )
            for r in range(2)
        )
        weights = [
            taper_rows[...] * taper_cols[:, pl.ds(pl.multiple_of(half * (FAC // 2) + chunk * LANES, LANES), LANES)]
            for half in range(2)
        ]
        for part in range(2):
            lanes = slice(part * LANES, (part + 1) * LANES)
            image[chunk, part, 0] = (evens[:, lanes] + odds[:, lanes]) * weights[0]
            image[chunk, part, 1] = (evens[:, lanes] - odds[:, lanes]) * weights[1]
        for copy in departures(chunk):
            copy.start()

    for chunk in range(CHUNKS):
        for copy in departures(chunk):
            copy.wait()


def facet(quarters, half_mixture, left, fold, taper_rows, taper_cols, right):
    vector = pl.BlockSpec(memory_space=pltpu.VMEM)
    hbm = pl.BlockSpec(memory_space=pltpu.HBM)
    return pl.pallas_call(
        facet_kernel,
        out_shape=jax.ShapeDtypeStruct((2, ROWS_OUT, FAC), F32),
        in_specs=[vector] * 10,
        out_specs=hbm,
        scratch_shapes=[
            pltpu.VMEM((2, ROWS_OUT, SUB // 2), BF16),
            pltpu.VMEM((NBLK // 4 * ROWS_OUT, 4 * LANES), BF16),
            pltpu.VMEM((CHUNKS, 2, 2, ROWS_OUT, LANES), F32),
            pltpu.SemaphoreType.DMA((4 * CHUNKS,)),
        ],
        compiler_params=pltpu.CompilerParams(vmem_limit_bytes=24 * 1024 * 1024),
        name="facet",
    )(*quarters, half_mixture, left, fold, taper_rows, taper_cols, right)


def by_visibility_row(array):
    return array.reshape(BLOCKS, 2, BLK // LANES, LANES).transpose(0, 2, 1, 3).reshape(BLOCKS * 8, LANES)


def shards(vis_coords, vis_values, tile_index):
    columns, rows, left, right, fold, taper_rows, taper_cols, bell, spin = (jnp.asarray(table) for table in tables())
    place = (lax.axis_index("x_lo") * 2 + lax.axis_index("core")).astype(jnp.int32).reshape(1)

    def swap(array, axis):
        return lax.ppermute(array, axis, [(0, 1), (1, 0)])

    send, rows, stacked, left, taper_rows, taper_cols, right, fold = gridding(
        place,
        [
            tile_index, by_visibility_row(vis_coords), by_visibility_row(vis_values),
            columns, rows, bell, left, taper_rows, taper_cols, right, fold, spin,
        ],
    )
    got = swap(send, "core")
    keep = keep_half(place, rows, stacked)
    total = (keep.astype(F32) + got.astype(F32)).astype(BF16)
    outgoing = total.reshape(NBLK * NBLK * 2, QUARTER, LANES)
    arrived = lax.all_to_all(outgoing, ("grid", "x_lo"), split_axis=0, concat_axis=0, tiled=True)
    halves = [half.reshape(NBLK // 2, ROWS, LANES) for half in pair_sum(arrived.reshape(NBLK * NBLK, 2, QUARTER, LANES))]
    by_core = [swap(half, "core") for half in halves]
    by_x = [swap(half, "x_lo") for half in halves]
    by_both = [swap(half, "core") for half in by_x]
    first, second = zip(halves, by_core, by_x, by_both)
    half_mixture = mixture_half(first, left, fold)
    return facet(second, half_mixture, left, fold, taper_rows, taper_cols, right)[None]


def solution(mesh):
    shape = (mesh.shape["grid"], 2, 2)
    split = jax.sharding.Mesh(mesh.devices.reshape(shape), ("grid", "x_lo", "core"))
    vis = ("x_lo", "core")
    placed = (P("grid", vis, None, None), P("grid", vis, None, None), P("grid", vis))
    return jax.shard_map(
        shards, mesh=split, in_specs=placed, out_specs=P("grid", None, vis, None), check_vma=False
    )
```

```python
import functools
import math

import jax
import jax.numpy as jnp
import ml_dtypes
import numpy as np
from jax import lax
from jax.experimental import pallas as pl
from jax.experimental.pallas import tpu as pltpu
from jax.sharding import PartitionSpec as P

SUB = 512
FAC = 1024
CONTRIB = 64
TILE = 64
BLK = 512
BLOCKS = 64
GROUP = 32
CHUNKS = FAC // 2 // 128
NBLK = 8
LANES = 128
QUARTER = 16
ROWS = NBLK * QUARTER
HALF = 2 * ROWS
ROWS_OUT = FAC // 4
WIDTH = 2 * SUB
BF16 = jnp.bfloat16
F32 = jnp.float32


def angles(first, second, length):
    return (first[:, None] * second[None, :] % length) * (2.0 * math.pi / length)


def as_bf16(table):
    return np.ascontiguousarray(table.astype(np.float32)).astype(ml_dtypes.bfloat16)


@functools.lru_cache(maxsize=None)
def tables():
    spectrum = np.arange(SUB)
    turn = angles(spectrum, np.arange(SUB // 2), SUB)
    turn = turn.reshape(NBLK // 2, 2, TILE // 2, 2, NBLK // 2, CONTRIB // 2, 2).transpose(3, 0, 1, 2, 4, 6, 5)
    turn = np.stack([turn[0], turn[1][:, ::-1]])
    cos, sin = np.cos(turn), np.sin(turn)
    columns = np.empty((2, NBLK // 2, 2, 2, TILE // 2, NBLK // 2, 2, 2, CONTRIB // 2))
    columns[:, :, :, 0, :, :, 0] = cos
    columns[:, :, :, 1, :, :, 0] = sin
    columns[:, :, :, 0, :, :, 1] = -sin
    columns[:, :, :, 1, :, :, 1] = cos
    columns = as_bf16(columns.reshape(2, SUB, SUB))
    turn = angles(spectrum, np.arange(SUB // 4), SUB).reshape(ROWS, 4, SUB // 4).transpose(1, 0, 2)
    rows = as_bf16(np.concatenate([np.cos(turn), np.sin(turn)], 2))
    turn = angles(np.arange(FAC), spectrum, FAC).reshape(4, ROWS_OUT, NBLK, QUARTER, 4)
    left = np.empty((4, 2, ROWS_OUT, 4, NBLK, QUARTER))
    for g in range(4):
        for j in range(4):
            left[g, 0, :, j] = np.cos(turn[g, ..., g ^ j])
            left[g, 1, :, j] = np.sin(turn[g, ..., g ^ j])
    left = as_bf16(left.reshape(4, 2 * ROWS_OUT, SUB))
    turn = angles(spectrum, np.arange(FAC // 2), FAC).reshape(NBLK // 2, 2, CONTRIB // 2, 2, CHUNKS, LANES)
    turn = turn.transpose(3, 4, 0, 1, 2, 5)
    cos, sin = np.cos(turn), np.sin(turn)
    right = np.empty((2, CHUNKS, NBLK // 2, 2, 2, CONTRIB // 2, 2, LANES))
    right[:, :, :, 0, :, :, 0] = cos
    right[:, :, :, 1, :, :, 0] = -sin
    right[:, :, :, 0, :, :, 1] = sin
    right[:, :, :, 1, :, :, 1] = cos
    right = as_bf16(right.reshape(2, CHUNKS, SUB, 2 * LANES))
    fold = np.zeros((2, 2, 2, 2, CONTRIB // 2, 2, 2, 2, CONTRIB // 2))
    j = np.arange(CONTRIB // 2)
    for sb in range(2):
        for r in range(2):
            for part in range(2):
                fold[0, sb, part, r, j, r, part, sb, j] = 1.0
                fold[1, sb, part, r, j, r, 1 - part, sb, j] = 1.0 - 2.0 * part
    fold = as_bf16(fold.reshape(SUB, 2 * LANES))
    spin = np.zeros((2, 2, CONTRIB, 2, 2, CONTRIB))
    j = np.arange(CONTRIB)
    for block in range(2):
        spin[block, 0, j, block, 1, j] = -1.0
        spin[block, 1, j, block, 0, j] = 1.0
    spin = as_bf16(spin.reshape(2 * LANES, 2 * LANES))
    sines = np.sin(math.pi * (np.arange(FAC) + 0.5) / FAC)
    taper = 0.25 + 0.75 * sines * sines
    taper_rows = np.broadcast_to(taper.reshape(4, ROWS_OUT, 1), (4, ROWS_OUT, LANES)).astype(np.float32)
    taper_cols = (taper / SUB).reshape(1, FAC).astype(np.float32)
    pixel = np.arange(TILE)
    bell = (1.0 - 2.0 * (pixel % 2)) * np.exp(-(pixel * pixel) / 256.0)
    across = bell.reshape(TILE // 2, 2).T
    across = np.stack([across, across[::-1]])[:, :, None, :].repeat(2, 2).reshape(2, 1, LANES)
    bell = (bell[:, None] * across / SUB).astype(np.float32)
    return columns, rows, left, right, fold, np.ascontiguousarray(taper_rows), taper_cols, bell, spin


SINE = [math.pi ** (2 * k + 1) * (-1) ** k / math.factorial(2 * k + 1) for k in range(7)]


def gridding_kernel(
    place_ref, tiles_hbm, coords_hbm, values_hbm, columns_hbm, rows_hbm, bell_hbm, left_hbm, taper_rows_hbm, taper_cols_hbm,
    right_hbm, fold_hbm, spin_hbm,
    send_ref, rows, stacked, left_ref, taper_rows_ref, taper_cols_ref, right_ref, fold_ref,
    tile_ref, coords, values, step8, slope, height, acc, grid16, halves, columns, bell_ref,
    spin, apart, sems,
):
    place = place_ref[0]
    first = [(coords_hbm, coords), (values_hbm, values), (tiles_hbm, tile_ref)]
    later = [(columns_hbm, columns), (rows_hbm, rows), (bell_hbm, bell_ref), (spin_hbm, spin)]
    last = [(left_hbm.at[place], left_ref), (taper_rows_hbm.at[place], taper_rows_ref)]
    last += [(taper_cols_hbm, taper_cols_ref), (right_hbm, right_ref), (fold_hbm, fold_ref)]
    copies = [pltpu.make_async_copy(*ends, sems.at[i]) for i, ends in enumerate(first + later + last)]
    for copy in copies[: len(first)]:
        copy.start()
    acc[...] = jnp.zeros_like(acc)
    for copy in copies[: len(first)]:
        copy.wait()
    for copy in copies[len(first) :]:
        copy.start()

    @pl.loop(0, BLOCKS * 8 // 128)
    def _(chunk):
        at = pl.ds(pl.multiple_of(chunk * 128, 128), 128)
        c = coords[at, :]
        r = jnp.round(c)
        c = jnp.where(c == r, c + (c * 2.0**-23 + 1e-20), c)
        f = c - r
        square = f * f
        sine = jnp.full_like(f, SINE[6])
        for k in range(5, -1, -1):
            sine = sine * square + SINE[k]
        half = r * 0.5
        odd = half - jnp.floor(half)
        sine = sine * f * ((1.0 - 4.0 * odd) * (1.0 / math.pi))
        coords[at, :] = c
        step8[at, :] = jnp.exp(c * (1.0 / 16.0))
        slope[at, :] = c * (1.0 / 128.0)
        height[at, :] = sine * jnp.exp(c * c * (-1.0 / 256.0))

    row_of = lax.broadcasted_iota(jnp.int32, (8, LANES), 0).astype(F32)

    def spread(ref, row, count=8):
        return jnp.broadcast_to(ref[pl.ds(row, 1), :], (count, LANES))

    rises = [row_of + 8.0 * a for a in range(8)]

    def taps(row, rises, ratio):
        c = spread(coords, row)
        w = spread(height, row) * jnp.exp(rises[0] * spread(slope, row))
        found = []
        for rise in rises:
            found.append(w * pl.reciprocal(rise - c, approx=True))
            w = w * ratio
        return jnp.concatenate(found, 0).astype(BF16)

    def patch_of(b):
        odd = (tile_ref[0, b] % 2).astype(F32)
        halves_v = [row_of * 2.0 + odd, row_of * 2.0 + (1.0 - odd)]
        rises_v = [[first + 16.0 * a for a in range(4)] for first in halves_v]
        u, v = [], [[] for _ in range(4)]
        for t in range(4):
            row = b * 8 + t * 2
            u.append(taps(row, rises, spread(step8, row)))
            ratio = spread(step8, row + 1)
            ratio = ratio * ratio
            found = [taps(row + 1, some, ratio) for some in rises_v]
            for part in range(2):
                value = spread(values, row + part, TILE // 2).astype(BF16)
                for half in range(2):
                    v[half * 2 + part].append(found[half] * value)
        u = jnp.concatenate(u, 1)
        v = jnp.concatenate([jnp.concatenate(piece, 1) for piece in v], 0)
        return lax.dot_general(u, v, (((1,), (1,)), ((), ())), preferred_element_type=F32)

    def deposit(b, patch):
        tile = tile_ref[0, b]
        at = (
            pl.ds(pl.multiple_of((tile // NBLK) * TILE, TILE), TILE),
            pl.ds(pl.multiple_of((tile % NBLK) * LANES, LANES), LANES),
        )
        acc[at] = acc[at] + patch

    @pl.loop(0, BLOCKS // GROUP)
    def _(group):
        held = None
        for i in range(GROUP):
            patch = patch_of(group * GROUP + i)
            if held is not None:
                deposit(group * GROUP + i - 1, held)
            held = patch
        deposit(group * GROUP + GROUP - 1, held)

    for copy in copies[len(first) :]:
        copy.wait()

    lane = lax.broadcasted_iota(jnp.int32, (1, LANES), 1)
    left_lane = lane < CONTRIB
    step = SUB // 4

    @pl.loop(0, NBLK)
    def _(a):
        at = pl.ds(pl.multiple_of(a * TILE, TILE), TILE)
        for e in range(NBLK // 2):
            even = acc[at, 2 * e * LANES : (2 * e + 1) * LANES] * bell_ref[0]
            odd = acc[at, (2 * e + 1) * LANES : (2 * e + 2) * LANES] * bell_ref[1]
            lanes = slice(e * LANES, (e + 1) * LANES)
            grid16[0, at, lanes] = jnp.where(left_lane, even, odd).astype(BF16)
            grid16[1, at, lanes] = jnp.where(left_lane, odd, even).astype(BF16)

    @pl.loop(0, SUB // 256)
    def _(n):
        at = pl.ds(pl.multiple_of(n * 256, 256), 256)
        for h in range(2):
            halves[h, :, at] = jnp.dot(grid16[h], columns[h, :, at], preferred_element_type=F32)

    @pl.loop(0, step // QUARTER)
    def _(m):
        first = pl.multiple_of(m * QUARTER, QUARTER)
        for i in range(NBLK // 2):
            lanes = slice(i * LANES, (i + 1) * LANES)
            low, high = [], []
            for q in range(4):
                some = halves[0, pl.ds(first + q * step, QUARTER), lanes]
                other = halves[1, pl.ds(first + q * step, QUARTER), lanes]
                low.append(some + other)
                high.append(some - other)
            for image, block in ((low, i), (high, i + NBLK // 2)):
                into = slice(block * LANES, (block + 1) * LANES)
                sum02, diff02 = image[0] + image[2], image[0] - image[2]
                sum13, diff13 = image[1] + image[3], image[1] - image[3]
                for i, x in enumerate((sum02 + sum13, sum02 - sum13, diff02, diff13)):
                    apart[i, pl.ds(first, QUARTER), into] = x.astype(BF16)

    @pl.loop(0, WIDTH // 256)
    def _(n):
        at = pl.ds(pl.multiple_of(n * 256, 256), 256)
        pieces = [apart[i, :, at] for i in range(4)]
        turned = jnp.dot(jnp.concatenate(pieces, 0), spin[...], preferred_element_type=F32)
        turned = [turned[i * step : (i + 1) * step] for i in range(4)]
        stacked[0, :step, at] = pieces[0]
        stacked[0, step:, at] = turned[0].astype(BF16)
        stacked[2, :step, at] = pieces[1]
        stacked[2, step:, at] = turned[1].astype(BF16)
        diff02, diff13 = pieces[2].astype(F32), pieces[3].astype(F32)
        stacked[1, :step, at] = (diff02 + turned[3]).astype(BF16)
        stacked[1, step:, at] = (turned[2] - diff13).astype(BF16)
        stacked[3, :step, at] = (diff02 - turned[3]).astype(BF16)
        stacked[3, step:, at] = (turned[2] + diff13).astype(BF16)

    facet_rows(1 - place % 2, rows, stacked, send_ref)


def facet_rows(core, rows, stacked, out):
    @pl.loop(0, WIDTH // 256)
    def _(n):
        at = pl.ds(pl.multiple_of(n * 256, 256), 256)
        for x_lo in range(2):
            v = core + 2 * x_lo
            spectra = jnp.dot(rows[v], stacked[v, :, at], preferred_element_type=F32).astype(BF16)
            for i in range(2):
                for ra in range(NBLK):
                    first = (ra * 2 + x_lo) * QUARTER
                    block = spectra[ra * QUARTER : (ra + 1) * QUARTER, i * LANES : (i + 1) * LANES]
                    out[n * 2 + i, first : first + QUARTER] = block


def keep_kernel(place_ref, rows, stacked, out):
    facet_rows(place_ref[0] % 2, rows, stacked, out)


def keep_half(place, rows, stacked):
    vector = pl.BlockSpec(memory_space=pltpu.VMEM)
    return pl.pallas_call(
        keep_kernel,
        out_shape=jax.ShapeDtypeStruct((NBLK, HALF, LANES), BF16),
        in_specs=[pl.BlockSpec(memory_space=pltpu.SMEM), vector, vector],
        out_specs=vector,
        compiler_params=pltpu.CompilerParams(vmem_limit_bytes=24 * 1024 * 1024),
        cost_estimate=pl.CostEstimate(flops=2**27, bytes_accessed=2**20, transcendentals=0),
        name="keep_half",
    )(place, rows, stacked)


def gridding(place, arrays):
    hbm = pl.BlockSpec(memory_space=pltpu.HBM)
    vector = pl.BlockSpec(memory_space=pltpu.VMEM)
    half = jax.ShapeDtypeStruct((NBLK, HALF, LANES), BF16)
    plane = pltpu.VMEM((BLOCKS * 8, LANES), F32)
    return pl.pallas_call(
        gridding_kernel,
        out_shape=[half]
        + [
            jax.ShapeDtypeStruct((4, ROWS, SUB // 2), BF16),
            jax.ShapeDtypeStruct((4, SUB // 2, WIDTH), BF16),
            jax.ShapeDtypeStruct((2 * ROWS_OUT, SUB), BF16),
            jax.ShapeDtypeStruct((ROWS_OUT, LANES), F32),
            jax.ShapeDtypeStruct((1, FAC), F32),
            jax.ShapeDtypeStruct((2, CHUNKS, SUB, 2 * LANES), BF16),
            jax.ShapeDtypeStruct((SUB, 2 * LANES), BF16),
        ],
        in_specs=[pl.BlockSpec(memory_space=pltpu.SMEM)] + [hbm] * len(arrays),
        out_specs=[vector] * 8,
        scratch_shapes=[
            pltpu.SMEM((1, BLOCKS), jnp.int32),
            plane, plane, plane, plane, plane,
            pltpu.VMEM((SUB, WIDTH), F32),
            pltpu.VMEM((2, SUB, SUB), BF16),
            pltpu.VMEM((2, SUB, SUB), F32),
            pltpu.VMEM((2, SUB, SUB), BF16),
            pltpu.VMEM((2, TILE, LANES), F32),
            pltpu.VMEM((2 * LANES, 2 * LANES), BF16),
            pltpu.VMEM((4, SUB // 4, WIDTH), BF16),
            pltpu.SemaphoreType.DMA((12,)),
        ],
        compiler_params=pltpu.CompilerParams(vmem_limit_bytes=24 * 1024 * 1024),
        name="gridding",
    )(place, *(stay(array) for array in arrays))


def stay(array):
    return pltpu.with_memory_space_constraint(array, pltpu.HBM)


def pair_sum_kernel(arrived, whole, *halves):
    count = NBLK * NBLK // 2
    for i, half in enumerate(halves):

        @pl.loop(0, count // 8)
        def _(n):
            pairs = arrived[pl.ds(i * count + n * 8, 8)].astype(F32)
            total = (pairs[:, 0] + pairs[:, 1]).astype(BF16)
            whole[pl.ds(i * count + n * 8, 8)] = total
            half[pl.ds(n * 8, 8)] = total


def pair_sum(arrived):
    vector = pl.BlockSpec(memory_space=pltpu.VMEM)
    half = jax.ShapeDtypeStruct((NBLK * NBLK // 2, QUARTER, LANES), BF16)
    whole = jax.ShapeDtypeStruct((NBLK * NBLK, QUARTER, LANES), BF16)
    return pl.pallas_call(
        pair_sum_kernel,
        out_shape=[whole, half, half],
        in_specs=[vector],
        out_specs=[vector] * 3,
        compiler_params=pltpu.CompilerParams(vmem_limit_bytes=24 * 1024 * 1024),
        name="pair_sum",
    )(arrived)


def mix(parts, left, fold, products, mixture):
    for n in range(NBLK // 4):
        right_side = jnp.concatenate(
            [jnp.concatenate([part[2 * n], part[2 * n + 1]], 1) for part in parts], 0
        )
        both = jnp.dot(left[...], right_side, preferred_element_type=F32).astype(BF16)
        at = slice(n * ROWS_OUT, (n + 1) * ROWS_OUT)
        products[at, : 2 * LANES] = both[:ROWS_OUT]
        products[at, 2 * LANES :] = both[ROWS_OUT:]
    mixed = jnp.dot(products[...], fold[...], preferred_element_type=F32).astype(BF16)
    for n in range(NBLK // 4):
        at = slice(n * ROWS_OUT, (n + 1) * ROWS_OUT)
        for r in range(2):
            mixture[r, :, n * LANES : (n + 1) * LANES] = mixed[at, r * LANES : (r + 1) * LANES]


def mixture_kernel(own, by_core, by_x, by_both, left, fold, mixture, products):
    first = pl.ds(0, NBLK // 2)
    mix((own.at[first], by_core.at[first], by_x, by_both), left, fold, products, mixture)


def mixture_half(quarters, left, fold):
    vector = pl.BlockSpec(memory_space=pltpu.VMEM)
    return pl.pallas_call(
        mixture_kernel,
        out_shape=jax.ShapeDtypeStruct((2, ROWS_OUT, SUB // 2), BF16),
        in_specs=[vector] * 6,
        out_specs=vector,
        scratch_shapes=[pltpu.VMEM((NBLK // 4 * ROWS_OUT, 4 * LANES), BF16)],
        compiler_params=pltpu.CompilerParams(vmem_limit_bytes=24 * 1024 * 1024),
        cost_estimate=pl.CostEstimate(flops=2**28, bytes_accessed=2**20, transcendentals=0),
        name="mixture_half",
    )(*quarters, left, fold)


def facet_kernel(
    own, by_core, by_x, by_both, half_mixture, left, fold, taper_rows, taper_cols, right, out_hbm,
    mixture, products, image, sems,
):
    second = pl.ds(NBLK // 2, NBLK // 2)
    mix((own.at[second], by_core.at[second], by_x, by_both), left, fold, products, mixture)

    def departures(chunk):
        copies = []
        for part in range(2):
            for half in range(2):
                first = pl.multiple_of(half * (FAC // 2) + chunk * LANES, LANES)
                into = out_hbm.at[part, :, pl.ds(first, LANES)]
                sem = sems.at[chunk * 4 + part * 2 + half]
                copies.append(pltpu.make_async_copy(image.at[chunk, part, half], into, sem))
        return copies

    @pl.loop(0, CHUNKS)
    def _(chunk):
        evens, odds = (
            jnp.dot(
                jnp.concatenate([half_mixture[r], mixture[r]], 1), right[r, chunk], preferred_element_type=F32
            )
            for r in range(2)
        )
        weights = [
            taper_rows[...] * taper_cols[:, pl.ds(pl.multiple_of(half * (FAC // 2) + chunk * LANES, LANES), LANES)]
            for half in range(2)
        ]
        for part in range(2):
            lanes = slice(part * LANES, (part + 1) * LANES)
            image[chunk, part, 0] = (evens[:, lanes] + odds[:, lanes]) * weights[0]
            image[chunk, part, 1] = (evens[:, lanes] - odds[:, lanes]) * weights[1]
        for copy in departures(chunk):
            copy.start()

    for chunk in range(CHUNKS):
        for copy in departures(chunk):
            copy.wait()


def facet(quarters, half_mixture, left, fold, taper_rows, taper_cols, right):
    vector = pl.BlockSpec(memory_space=pltpu.VMEM)
    hbm = pl.BlockSpec(memory_space=pltpu.HBM)
    return pl.pallas_call(
        facet_kernel,
        out_shape=jax.ShapeDtypeStruct((2, ROWS_OUT, FAC), F32),
        in_specs=[vector] * 10,
        out_specs=hbm,
        scratch_shapes=[
            pltpu.VMEM((2, ROWS_OUT, SUB // 2), BF16),
            pltpu.VMEM((NBLK // 4 * ROWS_OUT, 4 * LANES), BF16),
            pltpu.VMEM((CHUNKS, 2, 2, ROWS_OUT, LANES), F32),
            pltpu.SemaphoreType.DMA((4 * CHUNKS,)),
        ],
        compiler_params=pltpu.CompilerParams(vmem_limit_bytes=24 * 1024 * 1024),
        name="facet",
    )(*quarters, half_mixture, left, fold, taper_rows, taper_cols, right)


def by_visibility_row(array):
    return array.reshape(BLOCKS, 2, BLK // LANES, LANES).transpose(0, 2, 1, 3).reshape(BLOCKS * 8, LANES)


def shards(vis_coords, vis_values, tile_index):
    columns, rows, left, right, fold, taper_rows, taper_cols, bell, spin = (jnp.asarray(table) for table in tables())
    place = (lax.axis_index("x_lo") * 2 + lax.axis_index("core")).astype(jnp.int32).reshape(1)

    def swap(array, axis):
        return lax.ppermute(array, axis, [(0, 1), (1, 0)])

    send, rows, stacked, left, taper_rows, taper_cols, right, fold = gridding(
        place,
        [
            tile_index, by_visibility_row(vis_coords), by_visibility_row(vis_values),
            columns, rows, bell, left, taper_rows, taper_cols, right, fold, spin,
        ],
    )
    got = swap(send, "core")
    keep = keep_half(place, rows, stacked)
    total = (keep.astype(F32) + got.astype(F32)).astype(BF16)
    outgoing = total.reshape(NBLK * NBLK * 2, QUARTER, LANES)
    arrived = lax.all_to_all(outgoing, ("grid", "x_lo"), split_axis=0, concat_axis=0, tiled=True)
    own, *halves = pair_sum(arrived.reshape(NBLK * NBLK, 2, QUARTER, LANES))
    own = own.reshape(NBLK, ROWS, LANES)
    by_x = [swap(half.reshape(NBLK // 2, ROWS, LANES), "x_lo") for half in halves]
    by_core = swap(own, "core")
    by_both = [swap(half, "core") for half in by_x]
    first, second = ((own, by_core, *pair) for pair in zip(by_x, by_both))
    half_mixture = mixture_half(first, left, fold)
    return facet(second, half_mixture, left, fold, taper_rows, taper_cols, right)[None]


def solution(mesh):
    shape = (mesh.shape["grid"], 2, 2)
    split = jax.sharding.Mesh(mesh.devices.reshape(shape), ("grid", "x_lo", "core"))
    vis = ("x_lo", "core")
    placed = (P("grid", vis, None, None), P("grid", vis, None, None), P("grid", vis))
    return jax.shard_map(
        shards, mesh=split, in_specs=placed, out_specs=P("grid", None, vis, None), check_vma=False
    )
```
